32 devices in a mesh: img: 8 (over z, x), proto: 4 (over y, core).
Axes of the slice: x: 2, y: 2, z: 4, core: 2. Of those that a mesh axis runs over, the one named last changes fastest.
Arguments:
- student_feats: bfloat16 [8, 128, 384], P('img'), may hold values from -1 to 1
- teacher_feats: bfloat16 [8, 128, 384], P('img'), may hold values from -1 to 1
- student_weight: bfloat16 [384, 131072], P(None, ('img', 'proto')), may hold values from -1 to 1
- teacher_weight: bfloat16 [384, 131072], P(None, ('img', 'proto')), may hold values from -1 to 1
- patch_masks: int32 [8, 128], P('img'), may hold values from 0 to 1, as said below
Outputs:
- patch_loss: float32 [], replicated
- grad_weight: float32 [384, 131072], P(None, ('img', 'proto'))
- grad_rows: float32 [512, 384], P(('img', 'proto'))
The draws below stay inside these ranges and needn't reach their ends.
Inputs may be any that keep to these rules, and one draw needn't show every extreme that they name: `patch_masks`: exactly 4 images have masked patches, chosen at random; a quarter of these each have 128 / 8, 32, 48 and 64 masked patches at random positions, so 160 patches are masked in all.
All inputs are finite; a program needn't handle non-finite values.
Results may differ from the reference program's by a relative error of at most 0.0085.
Values may be sent and summed in bfloat16 or wider, within the bound.
No kernel may reach another device: no remote copies, remote signals or barrier semaphores. Data moves between devices by JAX's collectives and lax.ppermute only.
A program may use at most 64 MiB of HBM per device.

```python
import math
import jax
import jax.numpy as jnp
from jax import lax

E = 384
P_SIZE = 131072
PATCH = 128
ITERS = 3
IMAGES = 8
ROWS = 160
DEVICES = 32


def shared_directions(key):
    return jax.random.normal(jax.random.fold_in(key, 101), (8, E), jnp.float32)


def image_directions(key):
    return jax.random.normal(jax.random.fold_in(key, 102), (IMAGES, E), jnp.float32)


def head_columns(key, salt_value, tilted, mode):
    folded = jax.random.fold_in(key, salt_value)
    first_key, second_key, third_key = jax.random.split(folded, 3)
    mixing = jax.random.normal(first_key, (8, P_SIZE), jnp.float32) / math.sqrt(8.0)
    position = jnp.arange(P_SIZE, dtype=jnp.float32) / P_SIZE
    growth = 0.3 + 1.5 * position
    jitter = 0.6 * jax.random.normal(second_key, (E, P_SIZE), jnp.float32)
    tilt = 2.5 - 5.0 * position
    directions = shared_directions(key)
    base = jnp.dot(directions.T, mixing) * growth[None, :] + jitter
    if tilted:
        base = base + directions[0][:, None] * tilt[None, :]
    column_ids = jnp.arange(P_SIZE, dtype=jnp.int32)
    if mode == 1:
        owner = (column_ids * IMAGES // P_SIZE + IMAGES // 2) % IMAGES
        base = base + 2.5 * image_directions(key)[owner].T
    if mode == 2:
        block_width = max(P_SIZE // DEVICES, 1)
        owner = column_ids // block_width % IMAGES
        base = base + 2.5 * image_directions(key)[owner].T
    spread = jnp.exp(jax.random.uniform(third_key, (1, P_SIZE), jnp.float32, math.log(0.1), 0.0))
    columns = base * spread / math.sqrt(E)
    return jnp.clip(columns, -1.0, 1.0).astype(jnp.bfloat16)


def patch_features(key, salt_value, aligned):
    folded = jax.random.fold_in(key, salt_value)
    first_key, second_key, third_key = jax.random.split(folded, 3)
    mixing = jax.random.normal(first_key, (IMAGES, PATCH, 8), jnp.float32) / math.sqrt(8.0)
    directions = shared_directions(key)
    anchor = jnp.einsum('ipa,ae->ipe', mixing, directions) + 1.5 * directions[0][None, None, :]
    if aligned:
        anchor = anchor + 2.5 * image_directions(key)[:, None, :]
    jitter = 0.5 * jax.random.normal(second_key, (IMAGES, PATCH, E), jnp.float32)
    spread = jnp.exp(jax.random.uniform(third_key, (IMAGES, PATCH, 1), jnp.float32, math.log(0.03), math.log(0.3)))
    values = (anchor + jitter) * spread / math.sqrt(E)
    return jnp.clip(values, -1.0, 1.0).astype(jnp.bfloat16)


def draw_student_feats(key, part):
    return patch_features(key, 201, True)


def draw_teacher_feats(key, part):
    return patch_features(key, 202, True)


def draw_student_weight(key, part):
    return head_columns(key, 211, True, 1)


def draw_teacher_weight(key, part):
    return head_columns(key, 212, False, 2)


def draw_patch_masks(key, part):
    folded = jax.random.fold_in(key, 301)
    shuffled = jax.random.permutation(jax.random.fold_in(folded, 1), IMAGES)
    rank_of = jnp.argsort(shuffled).astype(jnp.int32)
    counts = jnp.where(rank_of < IMAGES // 2, PATCH // 8 * (1 + rank_of % 4), 0)
    image_keys = jax.random.split(jax.random.fold_in(folded, 2), IMAGES)

    def patch_order(image_key):
        return jnp.argsort(jax.random.permutation(image_key, PATCH)).astype(jnp.int32)
    places = jax.vmap(patch_order)(image_keys)
    return (places < counts[:, None]).astype(jnp.int32)


def setup_inputs(seed: int = 0) -> dict:
    seeds = jax.random.split(jax.random.key(seed), 6)
    return {
        "student_feats": draw_student_feats(jax.random.fold_in(seeds[5], 71), 0),
        "teacher_feats": draw_teacher_feats(jax.random.fold_in(seeds[5], 71), 0),
        "student_weight": draw_student_weight(jax.random.fold_in(seeds[5], 71), 0),
        "teacher_weight": draw_teacher_weight(jax.random.fold_in(seeds[5], 71), 0),
        "patch_masks": draw_patch_masks(jax.random.fold_in(seeds[5], 71), 0),
    }


TEACHER_TEMP = 0.07
STUDENT_TEMP = 0.1
NORM_EPS = 1e-06

def slot_rows(features, mask_rows, slot_count):
    rank_of = jnp.cumsum(mask_rows, axis=1) - 1
    slot_ids = jnp.arange(slot_count, dtype=jnp.int32)
    select = ((mask_rows[:, None, :] == 1) & (rank_of[:, None, :] == slot_ids[None, :, None])).astype(jnp.float32)
    return jnp.einsum('isp,ipe->ise', select, features.astype(jnp.float32))

def unit_rows(slot_data):
    norm_rows = jnp.sqrt(lax.optimization_barrier(jnp.sum(slot_data * slot_data, axis=-1)) + NORM_EPS)
    return ((slot_data / norm_rows[..., None]).astype(jnp.bfloat16), norm_rows)

def unit_columns(weight):
    w_float = weight.astype(jnp.float32)
    norm_cols = jnp.sqrt(lax.optimization_barrier(jnp.sum(w_float * w_float, axis=0)) + NORM_EPS)
    return ((w_float / norm_cols[None, :]).astype(jnp.bfloat16), norm_cols)

def reference(student_feats, teacher_feats, student_weight, teacher_weight, patch_masks):
    slot_count = PATCH // 2
    counts = lax.optimization_barrier(jnp.sum(patch_masks, axis=1))
    valid_slot = (jnp.arange(slot_count, dtype=jnp.int32)[None, :] < counts[:, None]).reshape(-1)
    packed_ids = jnp.nonzero(valid_slot, size=ROWS)[0].astype(jnp.int32)
    stu_unit, stu_norm = unit_rows(slot_rows(student_feats, patch_masks, slot_count).reshape(-1, E)[packed_ids])
    tea_unit, _ = unit_rows(slot_rows(teacher_feats, patch_masks, slot_count).reshape(-1, E)[packed_ids])
    count_f = counts.astype(jnp.float32)
    masked_images = jnp.sum((counts > 0).astype(jnp.float32))
    row_weight = 1.0 / (jnp.repeat(jnp.maximum(count_f, 1.0), slot_count)[packed_ids] * masked_images)
    w_unit, w_norm = unit_columns(student_weight)
    tea_w_unit, _ = unit_columns(teacher_weight)
    block_width = min(P_SIZE, 8192)
    blocks = P_SIZE // block_width
    stu_blocks = w_unit.reshape(E, blocks, block_width).transpose(1, 0, 2)
    tea_blocks = tea_w_unit.reshape(E, blocks, block_width).transpose(1, 0, 2)

    def kernel_block(w_block):
        return jnp.exp(jnp.dot(tea_unit, w_block, preferred_element_type=jnp.float32) / TEACHER_TEMP)

    def total_block(w_block):
        logits = jnp.dot(stu_unit, w_block, preferred_element_type=jnp.float32) / STUDENT_TEMP
        return lax.optimization_barrier(jnp.sum(jnp.exp(logits), axis=1))
    kernel = lax.map(kernel_block, tea_blocks)
    partition = lax.optimization_barrier(jnp.sum(lax.map(total_block, stu_blocks), axis=0))
    row_scale = jnp.ones((ROWS,), jnp.float32)
    col_scale = jnp.ones((blocks, block_width), jnp.float32)
    for sweep_idx in range(ITERS):
        col_scale = 1.0 / jnp.einsum('r,nrb->nb', row_scale, kernel, precision=lax.Precision.HIGHEST)
        row_scale = 1.0 / jnp.einsum('nrb,nb->r', kernel, col_scale, precision=lax.Precision.HIGHEST)
    log_part = jnp.log(partition)
    scaled_weight = row_weight * ROWS

    def final_block(running, pieces):
        w_block, k_block, c_block = pieces
        logits = jnp.dot(stu_unit, w_block, preferred_element_type=jnp.float32) / STUDENT_TEMP
        targets = row_scale[:, None] * k_block * c_block[None, :]
        loss_piece = jnp.sum(row_weight * lax.optimization_barrier(jnp.sum(targets * (log_part[:, None] - logits), axis=1)))
        probability = jnp.exp(logits) / partition[:, None]
        grad_logits = (scaled_weight[:, None] * (probability - targets) / STUDENT_TEMP).astype(jnp.bfloat16)
        grad_unit_w = lax.dot_general(stu_unit, grad_logits, (((0,), (0,)), ((), ())), preferred_element_type=jnp.float32)
        grad_unit_x = lax.dot_general(grad_logits, w_block, (((1,), (1,)), ((), ())), preferred_element_type=jnp.float32)
        return ((running[0] + loss_piece, running[1] + grad_unit_x), grad_unit_w)
    start_carry = (jnp.zeros((), jnp.float32), jnp.zeros((ROWS, E), jnp.float32))
    (patch_loss, grad_unit_x), grad_w_blocks = lax.scan(final_block, start_carry, (stu_blocks, kernel, col_scale))
    grad_unit_w = grad_w_blocks.transpose(1, 0, 2).reshape(E, P_SIZE)
    w_float = w_unit.astype(jnp.float32)
    grad_weight = P_SIZE / 128.0 * (grad_unit_w - w_float * lax.optimization_barrier(jnp.sum(w_float * grad_unit_w, axis=0))[None, :]) / w_norm[None, :]
    unit_float = stu_unit.astype(jnp.float32)
    grad_x = (grad_unit_x - unit_float * lax.optimization_barrier(jnp.sum(unit_float * grad_unit_x, axis=1))[:, None]) / stu_norm[:, None]
    grad_rows = jnp.zeros((IMAGES * slot_count, E), jnp.float32).at[packed_ids].set(grad_x)
    return (patch_loss, grad_weight, grad_rows)
```

```python
import functools

import jax
import jax.numpy as jnp
from jax import lax
from jax.experimental import pallas as pl
from jax.experimental.pallas import tpu as pltpu
from jax.sharding import PartitionSpec as P

ITERS = 3
TEACHER_TEMP = 0.07
STUDENT_TEMP = 0.1
NORM_EPS = 1e-06
GRAD_SCALE = 1.0 / 128.0
EMPTY = 2.0
LANES = 128
F32 = jnp.float32
BF16 = jnp.bfloat16
AXES = ("img", "proto")

VMEM = pl.BlockSpec(memory_space=pltpu.VMEM)
SMEM = pl.BlockSpec(memory_space=pltpu.SMEM)


def call(body, outs, *args, flops=0, moved=0, exps=0):
    return pl.pallas_call(
        body,
        out_shape=outs,
        in_specs=[VMEM] * len(args),
        out_specs=jax.tree.map(lambda _: VMEM, outs),
        compiler_params=pltpu.CompilerParams(vmem_limit_bytes=56 * 1024 * 1024),
        cost_estimate=pl.CostEstimate(flops=flops, bytes_accessed=moved, transcendentals=exps),
    )(*args)


def dot(a, b, dims):
    return lax.dot_general(a, b, (dims, ((), ())), preferred_element_type=F32)


def iota(shape, dim):
    return lax.broadcasted_iota(jnp.int32, shape, dim)


def sds(shape, dtype):
    return jax.ShapeDtypeStruct(shape, dtype)


def to_column(row, rows):
    wide = jnp.broadcast_to(row, (LANES, row.shape[1]))
    return wide.T[:rows]


def to_row(part, width):
    rows = part.shape[0]
    if width > rows:
        part = jnp.concatenate([part, jnp.zeros((width - rows, LANES), F32)], axis=0)
    return jnp.sum(part.T, axis=0, keepdims=True)


def fold(x):
    parts = [x[:, i : i + LANES] for i in range(0, x.shape[1], LANES)]
    return functools.reduce(jnp.add, parts)


def spread(col, width):
    return jnp.concatenate([col] * (width // LANES), axis=1)


def chunks(columns):
    step = min(512, columns)
    return step, columns // step


def select_kernel(mask_ref, stu_ref, tea_ref, tea_out, stu_out, unit_out, norm_out):
    own = unit_out.shape[0]
    patches = mask_ref.shape[1]
    slot = iota((own, patches), 0) + lax.axis_index("proto") * own
    mask = jnp.broadcast_to(mask_ref[...].astype(F32), (own, patches))
    upto = (iota((patches, patches), 0) <= iota((patches, patches), 1)).astype(BF16)
    rank = dot(mask.astype(BF16), upto, ((1,), (0,)))
    pick = jnp.where((rank == slot.astype(F32) + 1.0) & (mask > 0.5), 1.0, 0.0).astype(BF16)
    valid = slot[:, :1].astype(F32) < rank[:, patches - 1 :]
    for source, target in ((tea_ref, tea_out), (stu_ref, stu_out)):
        rows = dot(pick, source[0], ((1,), (0,)))
        norm = jnp.sqrt(jnp.sum(rows * rows, axis=1, keepdims=True) + NORM_EPS)
        unit = (rows / norm).astype(BF16)
        sent = jnp.where(valid, unit.astype(F32), EMPTY).astype(BF16)
        target[...] = jnp.broadcast_to(sent[None], target.shape)
        if source is stu_ref:
            unit_out[...] = unit.astype(F32)
            norm_out[...] = jnp.broadcast_to(norm, norm_out.shape)


def norms_kernel(stu_w, tea_w, stu_out, tea_out):
    step, count = chunks(stu_w.shape[1])
    for ref, out in ((tea_w, tea_out), (stu_w, stu_out)):

        def body(i, _, ref=ref, out=out):
            at = pl.ds(pl.multiple_of(i * step, step), step)
            w = ref[:, at].astype(F32)
            out[:, at] = 1.0 / jnp.sqrt(jnp.sum(w * w, axis=0, keepdims=True) + NORM_EPS)
            return 0

        lax.fori_loop(0, count, body, 0)


def packing(slots_ref, rows, emit):
    total, width = slots_ref.shape
    step = min(512, total)
    before = jnp.zeros((1, 1), F32)
    upto = (iota((step, step), 0) <= iota((step, step), 1)).astype(BF16)
    for c in range(total // step):
        data = slots_ref[c * step : (c + 1) * step, :]
        flags = jnp.where(data[:, :LANES].astype(F32) < 1.5, 1.0, 0.0).astype(BF16)
        upto_here = dot(flags, upto, ((0,), (0,)))[:1]
        own = dot(flags, (iota((step, step), 0) == iota((step, step), 1)).astype(BF16), ((0,), (0,)))[:1]
        place = before + upto_here
        row = iota((rows, step), 0).astype(F32) + 1.0
        hot = jnp.where((row == place) & (own > 0.5), 1.0, 0.0).astype(BF16)
        emit(c, hot, data, flags)
        before = place[:, step - 1 :]


def pack_rows(slots_ref, rows):
    parts = []
    packing(slots_ref, rows, lambda c, hot, data, flags: parts.append(dot(hot, data, ((1,), (0,)))))
    return functools.reduce(jnp.add, parts).astype(BF16)


def first_kernel(tea_all, tea_w, inv, kernel_out, sent_out, *, rows):
    x = pack_rows(tea_all, rows)
    step, count = chunks(tea_w.shape[1])

    def body(i, acc):
        at = pl.ds(pl.multiple_of(i * step, step), step)
        z = dot(x, tea_w[:, at], ((1,), (0,)))
        k = jnp.exp(z * (inv[:, at] * (1.0 / TEACHER_TEMP)))
        kernel_out[:, at] = k
        c = 1.0 / jnp.sum(k, axis=0, keepdims=True)
        return acc + fold(k * c)

    acc = lax.fori_loop(0, count, body, jnp.zeros((rows, LANES), F32))
    row = to_row(acc, sent_out.shape[2])
    sent_out[...] = jnp.broadcast_to(row[None], sent_out.shape)


def student_kernel(stu_all, stu_w, inv, logits_out, part_out, x_out, hot_out, weight_out, *, per_image):
    rows = x_out.shape[0]
    state = {"x": [], "count": [], "images": []}

    def emit(c, hot, data, flags):
        step = data.shape[0]
        state["x"].append(dot(hot, data, ((1,), (0,))))
        hot_out[:, c * step : (c + 1) * step] = hot
        same = (iota((step, step), 0) // per_image == iota((step, step), 1) // per_image).astype(BF16)
        held = dot(same, flags, ((1,), (0,)))
        state["count"].append(dot(hot, held.astype(BF16), ((1,), (0,))))
        first = (iota(held.shape, 0) % per_image == 0) & (held > 0.5)
        state["images"].append(jnp.sum(first.astype(F32), axis=0, keepdims=True))

    packing(stu_all, rows, emit)
    add = functools.partial(functools.reduce, jnp.add)
    x = add(state["x"]).astype(BF16)
    x_out[...] = x
    weight_out[...] = 1.0 / (jnp.maximum(add(state["count"]), 1.0) * add(state["images"]))
    step, count = chunks(stu_w.shape[1])

    def body(i, acc):
        at = pl.ds(pl.multiple_of(i * step, step), step)
        l = dot(x, stu_w[:, at], ((1,), (0,))) * (inv[:, at] * (1.0 / STUDENT_TEMP))
        logits_out[:, at] = l
        return acc + fold(jnp.exp(l))

    acc = lax.fori_loop(0, count, body, jnp.zeros((rows, LANES), F32))
    part_out[...] = to_row(acc, part_out.shape[1])


def sweep_kernel(got, kernel, sent_out):
    rows, columns = kernel.shape
    scale = to_column(1.0 / jnp.sum(got[...], axis=0), rows)
    step, count = chunks(columns)
    wide = spread(scale, step)

    def body(i, acc):
        at = pl.ds(pl.multiple_of(i * step, step), step)
        k = kernel[:, at]
        c = 1.0 / jnp.sum(k * wide, axis=0, keepdims=True)
        return acc + fold(k * c)

    acc = lax.fori_loop(0, count, body, jnp.zeros((rows, LANES), F32))
    row = to_row(acc, sent_out.shape[2])
    sent_out[...] = jnp.broadcast_to(row[None], sent_out.shape)


def last_sweep_kernel(got, kernel, logits, part, scaled_out, sent_out):
    rows, columns = kernel.shape
    width = part.shape[1]
    scale = to_column(1.0 / jnp.sum(got[...], axis=0), rows)
    step, count = chunks(columns)
    wide = spread(scale, step)

    def body(i, accs):
        at = pl.ds(pl.multiple_of(i * step, step), step)
        k = kernel[:, at]
        kc = k / jnp.sum(k * wide, axis=0, keepdims=True)
        scaled_out[:, at] = kc
        return accs[0] + fold(kc), accs[1] + fold(kc * logits[:, at])

    zero = jnp.zeros((rows, LANES), F32)
    total, cross = lax.fori_loop(0, count, body, (zero, zero))
    row = jnp.concatenate([to_row(total, width), to_row(cross, width), part[...]], axis=1)
    sent_out[...] = jnp.broadcast_to(row[None], sent_out.shape)


def grads_kernel(got, scaled, logits, stu_w, inv, hot, weight, sent_out, grad_out, along_out, loss_out):
    rows, columns = scaled.shape
    width = got.shape[2] // 3
    sums = jnp.sum(got[...], axis=0)
    total = to_column(sums[:, :width], rows)
    cross = to_column(sums[:, width : 2 * width], rows)
    partition = to_column(sums[:, 2 * width :], rows)
    share = weight[...]
    loss = jnp.sum(share * (jnp.log(partition) - cross / total), axis=0, keepdims=True)
    loss_out[...] = loss[:, :1]
    factor = share * (rows / STUDENT_TEMP)
    step, count = chunks(columns)
    grow = spread(factor / partition, step)
    shrink = spread(factor / total, step)

    def body(i, acc):
        at = pl.ds(pl.multiple_of(i * step, step), step)
        l = logits[:, at]
        g = grow * jnp.exp(l) - shrink * scaled[:, at]
        n = inv[:, at]
        along_out[:, at] = jnp.sum(g * l, axis=0, keepdims=True) * STUDENT_TEMP
        gn = (g * n).astype(BF16)
        grad_out[:, at] = gn
        return acc + dot(gn, stu_w[:, at], ((1,), (1,)))

    acc = lax.fori_loop(0, count, body, jnp.zeros((rows, stu_w.shape[0]), F32))
    spots = dot(hot[...], acc.astype(BF16), ((0,), (0,)))
    sent_out[...] = spots.astype(BF16).reshape(sent_out.shape)


def weight_grad_kernel(x, grad, along, inv, stu_w, out, *, scale):
    n = inv[...]
    direct = dot(x[...], grad[...], ((0,), (0,)))
    out[...] = scale * (direct - stu_w[...].astype(F32) * (along[...] * n * n))


def rows_kernel(got, unit, norm, out):
    full = jnp.sum(got[...].astype(F32), axis=0)
    u = unit[...]
    out[...] = (full - u * jnp.sum(u * full, axis=1, keepdims=True)) / norm[:, :1]


def shards(student_feats, teacher_feats, student_weight, teacher_weight, patch_masks):
    devices = lax.axis_size(AXES)
    protos = lax.axis_size("proto")
    images, patches, feat = student_feats.shape
    assert images == 1
    columns = student_weight.shape[1]
    per_image = patches // 2
    own = per_image // protos
    slots = own * devices
    rows = slots * 5 // 16
    width = -(-rows // LANES) * LANES
    big = rows * columns
    exchange = functools.partial(lax.all_to_all, axis_name=AXES, split_axis=0, concat_axis=0)

    tea_sent, stu_sent, unit, norm = call(
        select_kernel,
        (
            sds((devices, own, feat), BF16),
            sds((devices, own, feat), BF16),
            sds((own, feat), F32),
            sds((own, LANES), F32),
        ),
        patch_masks,
        student_feats,
        teacher_feats,
    )
    tea_all = exchange(tea_sent).reshape(slots, feat)
    stu_all = exchange(stu_sent).reshape(slots, feat)
    stu_inv, tea_inv = call(
        norms_kernel,
        (sds((1, columns), F32), sds((1, columns), F32)),
        student_weight,
        teacher_weight,
        flops=4 * feat * columns,
        moved=4 * feat * columns,
    )
    vector = sds((devices, 1, width), F32)
    kernel, sent = call(
        functools.partial(first_kernel, rows=rows),
        (sds((rows, columns), F32), vector),
        tea_all,
        teacher_weight,
        tea_inv,
        flops=2 * big * feat,
        moved=4 * big,
        exps=big,
    )
    got = exchange(sent)
    logits, part, x, hot, weight = call(
        functools.partial(student_kernel, per_image=per_image),
        (
            sds((rows, columns), F32),
            sds((1, width), F32),
            sds((rows, feat), BF16),
            sds((rows, slots), BF16),
            sds((rows, LANES), F32),
        ),
        stu_all,
        student_weight,
        stu_inv,
        flops=2 * big * feat,
        moved=4 * big,
        exps=big,
    )
    for _ in range(ITERS - 2):
        sent = call(sweep_kernel, vector, got, kernel, flops=4 * big, moved=4 * big)
        got = exchange(sent)
    scaled, sent = call(
        last_sweep_kernel,
        (sds((rows, columns), F32), sds((devices, 1, 3 * width), F32)),
        got,
        kernel,
        logits,
        part,
        flops=6 * big,
        moved=12 * big,
    )
    got = exchange(sent)
    sent, grad, along, loss = call(
        grads_kernel,
        (
            sds((devices, own, feat), BF16),
            sds((rows, columns), BF16),
            sds((1, columns), F32),
            sds((1, 1), F32),
        ),
        got,
        scaled,
        logits,
        student_weight,
        stu_inv,
        hot,
        weight,
        flops=2 * big * feat,
        moved=8 * big,
        exps=big,
    )
    got = exchange(sent)
    step = min(512, columns)
    grad_weight = pl.pallas_call(
        functools.partial(weight_grad_kernel, scale=columns * devices * GRAD_SCALE),
        out_shape=sds((feat, columns), F32),
        grid=(columns // step,),
        in_specs=[
            pl.BlockSpec((rows, feat), lambda i: (0, 0)),
            pl.BlockSpec((rows, step), lambda i: (0, i)),
            pl.BlockSpec((1, step), lambda i: (0, i)),
            pl.BlockSpec((1, step), lambda i: (0, i)),
            pl.BlockSpec((feat, step), lambda i: (0, i)),
        ],
        out_specs=pl.BlockSpec((feat, step), lambda i: (0, i)),
        cost_estimate=pl.CostEstimate(flops=2 * big * feat, bytes_accessed=6 * feat * columns, transcendentals=0),
    )(x, grad, along, stu_inv, student_weight)
    grad_rows = call(rows_kernel, sds((own, feat), F32), got, unit, norm)
    return loss.reshape(()), grad_weight, grad_rows


def solution(mesh):
    placed = (
        P("img", None, None),
        P("img", None, None),
        P(None, AXES),
        P(None, AXES),
        P("img", None),
    )
    return jax.shard_map(
        shards,
        mesh=mesh,
        in_specs=placed,
        out_specs=(P(), P(None, AXES), P(AXES, None)),
        check_vma=False,
    )
```

```python
import functools

import jax
import jax.numpy as jnp
from jax import lax
from jax.experimental import pallas as pl
from jax.experimental.pallas import tpu as pltpu
from jax.sharding import PartitionSpec as P

ITERS = 3
TEACHER_TEMP = 0.07
STUDENT_TEMP = 0.1
NORM_EPS = 1e-06
GRAD_SCALE = 1.0 / 128.0
EMPTY = 2.0
LANES = 128
F32 = jnp.float32
BF16 = jnp.bfloat16
AXES = ("img", "proto")

VMEM = pl.BlockSpec(memory_space=pltpu.VMEM)


def call(body, outs, *args, flops=0, moved=0, exps=0, limit=24):
    return pl.pallas_call(
        body,
        out_shape=outs,
        in_specs=[VMEM] * len(args),
        out_specs=tuple(VMEM for _ in outs),
        compiler_params=pltpu.CompilerParams(vmem_limit_bytes=limit * 1024 * 1024),
        cost_estimate=pl.CostEstimate(flops=flops, bytes_accessed=moved, transcendentals=exps),
    )(*args)


def near(x):
    return pltpu.with_memory_space_constraint(x, pltpu.VMEM)


def dot(a, b, dims, precision=None):
    return lax.dot_general(a, b, (dims, ((), ())), precision=precision, preferred_element_type=F32)


def iota(shape, dim):
    return lax.broadcasted_iota(jnp.int32, shape, dim)


def add_all(parts):
    return functools.reduce(jnp.add, parts)


def to_column(vector, rows):
    parts = [jnp.broadcast_to(vector[i : i + 1], (LANES, LANES)).T for i in range(vector.shape[0])]
    return jnp.concatenate(parts, axis=0)[:rows]


def to_tiles(part, width):
    rows = part.shape[0]
    if width > rows:
        part = jnp.concatenate([part, jnp.zeros((width - rows, LANES), F32)], axis=0)
    row = jnp.sum(part.T, axis=0, keepdims=True)
    return jnp.concatenate([row[:, i : i + LANES] for i in range(0, width, LANES)], axis=0)


def split(tiles):
    high = tiles.astype(BF16).astype(F32)
    return [high, tiles - high]


def fold(x):
    return add_all([x[:, i : i + LANES] for i in range(0, x.shape[1], LANES)])


def spread(col, width):
    return jnp.concatenate([col] * (width // LANES), axis=1)


def chunks(columns):
    step = min(512, columns)
    return step, columns // step


def odd_half():
    return lax.rem(lax.axis_index("proto"), 2)


def select_kernel(mask_ref, stu_ref, tea_ref, sent_out, unit_out, norm_out):
    own, feat = unit_out.shape
    patches = mask_ref.shape[1]
    slot = iota((own, patches), 0) + lax.axis_index("proto") * own
    mask = jnp.broadcast_to(mask_ref[...].astype(F32), (own, patches))
    upto = (iota((patches, patches), 0) <= iota((patches, patches), 1)).astype(BF16)
    rank = dot(mask.astype(BF16), upto, ((1,), (0,)))
    pick = jnp.where((rank == slot.astype(F32) + 1.0) & (mask > 0.5), 1.0, 0.0).astype(BF16)
    valid = slot[:, :1].astype(F32) < rank[:, patches - 1 :]
    for source, at in ((tea_ref, 0), (stu_ref, feat)):
        rows = dot(pick, source[0], ((1,), (0,)))
        norm = jnp.sqrt(jnp.sum(rows * rows, axis=1, keepdims=True) + NORM_EPS)
        unit = (rows / norm).astype(BF16)
        sent = jnp.where(valid, unit.astype(F32), EMPTY).astype(BF16)
        sent_out[:, :, at : at + feat] = jnp.broadcast_to(sent[None], (sent_out.shape[0], own, feat))
        if source is stu_ref:
            unit_out[...] = unit.astype(F32)
            norm_out[...] = jnp.broadcast_to(norm, norm_out.shape)


def norms_kernel(stu_w, tea_w, stu_out, tea_out):
    step, count = chunks(stu_w.shape[1])
    for ref, out in ((tea_w, tea_out), (stu_w, stu_out)):

        def body(i, _, ref=ref, out=out):
            at = pl.ds(pl.multiple_of(i * step, step), step)
            w = ref[:, at].astype(F32)
            out[:, at] = 1.0 / jnp.sqrt(jnp.sum(w * w, axis=0, keepdims=True) + NORM_EPS)
            return 0

        lax.fori_loop(0, count, body, 0)


def packing(mine, other, at, feat, rows, emit):
    half = mine.shape[0]
    step = min(256, half)
    before = jnp.zeros((1, 1), F32)
    upto = (iota((step, step), 0) <= iota((step, step), 1)).astype(BF16)
    same = (iota((step, step), 0) == iota((step, step), 1)).astype(BF16)
    row = iota((rows, step), 0).astype(F32) + 1.0
    for h in range(2):
        for c in range(0, half, step):
            block = slice(c, c + step), slice(at, at + feat)
            data = jnp.where(odd_half() == h, mine[block], other[block])
            flags = jnp.where(data[:, :LANES].astype(F32) < 1.5, 1.0, 0.0).astype(BF16)
            place = before + dot(flags, upto, ((0,), (0,)))[:1]
            held = dot(flags, same, ((0,), (0,)))[:1]
            hot = jnp.where((row == place) & (held > 0.5), 1.0, 0.0).astype(BF16)
            emit(h * half + c, hot, data, flags)
            before = place[:, step - 1 :]


def first_kernel(mine, other, tea_w, inv, kernel_out, sent_out):
    rows = kernel_out.shape[0]
    feat = tea_w.shape[0]
    parts = []
    packing(mine, other, 0, feat, rows, lambda at, hot, data, flags: parts.append(dot(hot, data, ((1,), (0,)))))
    x = add_all(parts).astype(BF16)
    step, count = chunks(tea_w.shape[1])

    def body(i, acc):
        at = pl.ds(pl.multiple_of(i * step, step), step)
        z = dot(x, tea_w[:, at], ((1,), (0,)))
        k = jnp.exp(z * (inv[:, at] * (1.0 / TEACHER_TEMP)))
        kernel_out[:, at] = k
        c = 1.0 / jnp.sum(k, axis=0, keepdims=True)
        return acc + fold(k * c)

    acc = lax.fori_loop(0, count, body, jnp.zeros((rows, LANES), F32))
    tiles = to_tiles(acc, sent_out.shape[1] * LANES)
    sent_out[...] = jnp.broadcast_to(tiles[None], sent_out.shape)


def spots(hot, x, at, half):
    return dot(hot[:, at : at + half], x, ((0,), (0,)))


def halves(hot, x, keep_out, give_out):
    half = keep_out.shape[0]
    low, high = spots(hot, x, 0, half), spots(hot, x, half, half)
    odd = odd_half() == 1
    keep_out[...] = jnp.where(odd, high, low)
    give_out[...] = jnp.where(odd, low, high)


def student_kernel(
    mine, other, stu_w, inv, logits_out, part_out, x_out, hot_out, own_out, weight_out, keep_out, give_out, *, protos
):
    rows, feat = x_out.shape
    devices = lax.axis_size(AXES)
    each = mine.shape[0] // devices
    per_image = each * protos
    packed, count, images = [], [], []

    def emit(at, hot, data, flags):
        step = data.shape[0]
        packed.append(dot(hot, data, ((1,), (0,))))
        hot_out[:, at : at + step] = hot

    packing(mine, other, feat, feat, rows, emit)
    x = add_all(packed).astype(BF16)
    x_out[...] = x

    half = mine.shape[0]
    step = min(256, half)
    block = lax.broadcasted_iota(jnp.int32, (step, step), 0) // per_image
    same = (block == iota((step, step), 1) // per_image).astype(BF16)
    for c in range(0, half, step):
        flags = [
            jnp.where(ref[c : c + step, feat : feat + LANES].astype(F32) < 1.5, 1.0, 0.0) for ref in (mine, other)
        ]
        held = dot(same, (flags[0] + flags[1]).astype(BF16), ((1,), (0,)))
        for h in range(2):
            hot = hot_out[:, h * half + c : h * half + c + step]
            count.append(dot(hot, held.astype(BF16), ((1,), (0,))))
        first = (iota(held.shape, 0) % per_image == 0) & (held > 0.5)
        images.append(jnp.sum(first.astype(F32), axis=0, keepdims=True))
    weight_out[...] = 1.0 / (jnp.maximum(add_all(count), 1.0) * add_all(images))

    own = own_out.shape[0]
    me = lax.axis_index("img") * protos + lax.axis_index("proto")
    q = iota((own, 2 * half), 0)
    spot = q // each * half + me * each + q % each
    mark = (iota((own, 2 * half), 1) == spot).astype(BF16)
    own_out[...] = dot(mark, hot_out[...], ((1,), (1,)))

    step, count = chunks(stu_w.shape[1])

    def body(i, accs):
        at = pl.ds(pl.multiple_of(i * step, step), step)
        w = stu_w[:, at]
        n = inv[:, at]
        l = dot(x, w, ((1,), (0,))) * (n * (1.0 / STUDENT_TEMP))
        logits_out[:, at] = l
        p = jnp.exp(l)
        return accs[0] + fold(p), accs[1] + dot((p * n).astype(BF16), w, ((1,), (1,)))

    zeros = jnp.zeros((rows, LANES), F32), jnp.zeros((rows, feat), F32)
    acc, pull = lax.fori_loop(0, count, body, zeros)
    part_out[...] = to_tiles(acc, part_out.shape[0] * LANES)
    halves(hot_out, pull.astype(BF16), keep_out, give_out)


def fill(sent_out, keep, got, vectors):
    devices, each, wide = sent_out.shape
    feat = keep.shape[1]
    sent_out[:, :, :feat] = (keep[...] + got[...]).reshape(devices, each, feat).astype(BF16)
    tiles = add_all_rows([part for vector in vectors for part in split(vector)], each, (wide - feat) // LANES)
    sent_out[:, :, feat:] = jnp.broadcast_to(tiles[None], (devices, each, wide - feat)).astype(BF16)


def add_all_rows(parts, each, groups):
    tiles = jnp.concatenate(parts, axis=0)
    spare = each * groups - tiles.shape[0]
    if spare:
        tiles = jnp.concatenate([tiles, jnp.zeros((spare, LANES), F32)], axis=0)
    return jnp.concatenate([tiles[g * each : (g + 1) * each] for g in range(groups)], axis=1)


def vectors_of(got, feat, width, count):
    _, each, wide = got.shape
    sums = jnp.sum(got[:, :, feat:].astype(F32), axis=0)
    tiles = jnp.concatenate([sums[:, g : g + LANES] for g in range(0, wide - feat, LANES)], axis=0)
    m = width // LANES
    return [tiles[2 * v * m : (2 * v + 1) * m] + tiles[(2 * v + 1) * m : (2 * v + 2) * m] for v in range(count)]


def slots_of(got, feat):
    devices, each, _ = got.shape
    parts = got[:, :, :feat].astype(F32).reshape(devices // 2, 2, each, feat)
    return jnp.sum(parts, axis=0).reshape(2 * each, feat)


def sweep_kernel(got, kernel, part, keep, give, sent_out):
    rows, columns = kernel.shape
    width = part.shape[0] * LANES
    scale = to_column(1.0 / jnp.sum(got[...], axis=0), rows)
    step, count = chunks(columns)
    wide = spread(scale, step)

    def body(i, acc):
        at = pl.ds(pl.multiple_of(i * step, step), step)
        k = kernel[:, at]
        c = 1.0 / jnp.sum(k * wide, axis=0, keepdims=True)
        return acc + fold(k * c)

    acc = lax.fori_loop(0, count, body, jnp.zeros((rows, LANES), F32))
    fill(sent_out, keep, give, [to_tiles(acc, width), part[...]])


def last_sweep_kernel(
    got, kernel, logits, stu_w, inv, hot, scaled_out, total_out, cross_out, keep_out, give_out
):
    rows, columns = kernel.shape
    feat = stu_w.shape[0]
    width = total_out.shape[0] * LANES
    (total,) = vectors_of(got, feat, width, 1)
    scale = to_column(1.0 / total, rows)
    step, count = chunks(columns)
    wide = spread(scale, step)

    def body(i, accs):
        at = pl.ds(pl.multiple_of(i * step, step), step)
        k = kernel[:, at]
        kc = k * (1.0 / jnp.sum(k * wide, axis=0, keepdims=True))
        scaled_out[:, at] = kc
        kn = (kc * inv[:, at]).astype(BF16)
        return (
            accs[0] + fold(kc),
            accs[1] + fold(kc * logits[:, at]),
            accs[2] + dot(kn, stu_w[:, at], ((1,), (1,))),
        )

    zero = jnp.zeros((rows, LANES), F32)
    total, cross, push = lax.fori_loop(0, count, body, (zero, zero, jnp.zeros((rows, feat), F32)))
    total_out[...] = to_tiles(total, width)
    cross_out[...] = to_tiles(cross, width)
    halves(hot, push.astype(BF16), keep_out, give_out)


def fill_kernel(keep, got, total, cross, sent_out):
    fill(sent_out, keep, got, [total[...], cross[...]])


def prepare_kernel(got, scaled, logits, inv, weight, own, pull_out, push_out, rise_out, loss_out, *, scale):
    rows, columns = scaled.shape
    feat = rise_out.shape[1]
    width = -(-rows // LANES) * LANES
    _, partition = vectors_of(got, feat, width, 2)
    partition = to_column(partition, rows)
    share = weight[...]
    loss_out[...] = jnp.log(partition)
    factor = share * (rows / STUDENT_TEMP)
    step, count = chunks(columns)
    grow, shrink = spread(factor / partition, step), spread(factor, step)

    def body(i, _):
        at = pl.ds(pl.multiple_of(i * step, step), step)
        n = inv[:, at] * scale
        pull_out[:, at] = grow * jnp.exp(logits[:, at]) * n
        push_out[:, at] = shrink * scaled[:, at] * n
        return 0

    lax.fori_loop(0, count, body, 0)
    held = dot(own[...], factor / partition, ((1,), (0,)), lax.Precision.HIGHEST)
    rise_out[...] = slots_of(got, feat) * held[:, :1]


def final_kernel(
    got, pull, push, logits, inv, stu_w, x, weight, own, rise, log_part, unit, norm, out, rows_out, loss_out, scale_ref
):
    rows = pull.shape[0]
    feat = x.shape[1]
    width = -(-rows // LANES) * LANES

    @pl.when(pl.program_id(0) == 0)
    def _():
        total, cross = (to_column(v, rows) for v in vectors_of(got, feat, width, 2))
        scale = 1.0 / total
        scale_ref[...] = scale
        share = weight[...]
        loss = jnp.sum(share * (log_part[...] - cross * scale), axis=0, keepdims=True)
        loss_out[...] = loss[:, :1]
        held = dot(own[...], share * (rows / STUDENT_TEMP) * scale, ((1,), (0,)), lax.Precision.HIGHEST)
        full = rise[...] - slots_of(got, feat) * held[:, :1]
        u = unit[...]
        rows_out[...] = (full - u * jnp.sum(u * full, axis=1, keepdims=True)) / norm[:, :1]

    g = pull[...] - spread(scale_ref[...], pull.shape[1]) * push[...]
    along = jnp.sum(g * logits[...], axis=0, keepdims=True) * (inv[...] * STUDENT_TEMP)
    out[...] = dot(x[...], g.astype(BF16), ((0,), (0,))) - stu_w[...].astype(F32) * along


def shards(student_feats, teacher_feats, student_weight, teacher_weight, patch_masks):
    devices = lax.axis_size(AXES)
    protos = lax.axis_size("proto")
    images, patches, feat = student_feats.shape
    assert images == 1 and protos % 2 == 0
    columns = student_weight.shape[1]
    own = patches // 2 // protos
    each = own // 2
    half = each * devices
    rows = 2 * half * 5 // 16
    tiles = -(-rows // LANES)
    wide = feat + LANES * -(-4 * tiles // each)
    big = rows * columns
    exchange = functools.partial(lax.all_to_all, axis_name=AXES, split_axis=0, concat_axis=0)
    swap = functools.partial(lax.ppermute, axis_name="proto", perm=[(p, p ^ 1) for p in range(protos)])
    vector = pltpu.VMEM((tiles, LANES), F32)
    matrix = pltpu.VMEM((rows, columns), F32)
    column = pltpu.VMEM((rows, LANES), F32)
    line = pltpu.VMEM((1, columns), F32)
    block = pltpu.VMEM((half, feat), F32)
    payload = pltpu.VMEM((devices, each, wide), BF16)

    stu_w, tea_w = near(student_weight), near(teacher_weight)
    sent, unit, norm = call(
        select_kernel,
        (
            pltpu.VMEM((devices // 2, own, 2 * feat), BF16),
            pltpu.VMEM((own, feat), F32),
            pltpu.VMEM((own, LANES), F32),
        ),
        patch_masks,
        student_feats,
        teacher_feats,
    )
    mine = exchange(sent.reshape(devices, each, 2 * feat)).reshape(half, 2 * feat)
    other = near(swap(mine))
    mine = near(mine)
    stu_inv, tea_inv = call(
        norms_kernel,
        (line, line),
        stu_w,
        tea_w,
        flops=4 * feat * columns,
        moved=4 * feat * columns,
    )
    kernel, sent = call(
        first_kernel,
        (matrix, pltpu.VMEM((devices, tiles, LANES), F32)),
        mine,
        other,
        tea_w,
        tea_inv,
        flops=2 * big * feat,
        moved=4 * big,
        exps=big,
    )
    got = near(exchange(sent))
    logits, part, x, hot, own_hot, weight, keep, give = call(
        functools.partial(student_kernel, protos=protos),
        (
            matrix,
            vector,
            pltpu.VMEM((rows, feat), BF16),
            pltpu.VMEM((rows, 2 * half), BF16),
            pltpu.VMEM((own, rows), F32),
            column,
            block,
            block,
        ),
        mine,
        other,
        stu_w,
        stu_inv,
        flops=4 * big * feat,
        moved=4 * big,
        exps=big,
    )
    give = near(swap(give))
    (sent,) = call(sweep_kernel, (payload,), got, kernel, part, keep, give, flops=4 * big, moved=4 * big)
    swept = near(exchange(sent))
    scaled, total, cross, keep, give = call(
        last_sweep_kernel,
        (matrix, vector, vector, block, block),
        swept,
        kernel,
        logits,
        stu_w,
        stu_inv,
        hot,
        flops=2 * big * feat,
        moved=12 * big,
    )
    (sent,) = call(fill_kernel, (payload,), keep, near(swap(give)), total, cross)
    got = near(exchange(sent))
    pull, push, rise, log_part = call(
        functools.partial(prepare_kernel, scale=columns * devices * GRAD_SCALE),
        (matrix, matrix, pltpu.VMEM((own, feat), F32), column),
        swept,
        scaled,
        logits,
        stu_inv,
        weight,
        own_hot,
        flops=4 * big,
        moved=16 * big,
        exps=big,
    )
    step = min(512, columns)
    whole = lambda shape: pl.BlockSpec(shape, lambda i: (0,) * len(shape))
    part = lambda height: pl.BlockSpec((height, step), lambda i: (0, i))
    grad_weight, grad_rows, loss = pl.pallas_call(
        final_kernel,
        out_shape=(
            jax.ShapeDtypeStruct((feat, columns), F32),
            jax.ShapeDtypeStruct((own, feat), F32),
            jax.ShapeDtypeStruct((1, 1), F32),
        ),
        grid=(columns // step,),
        in_specs=[
            whole((devices, each, wide)),
            part(rows),
            part(rows),
            part(rows),
            part(1),
            part(feat),
            whole((rows, feat)),
            whole((rows, LANES)),
            whole((own, rows)),
            whole((own, feat)),
            whole((rows, LANES)),
            whole((own, feat)),
            whole((own, LANES)),
        ],
        out_specs=(part(feat), whole((own, feat)), whole((1, 1))),
        scratch_shapes=[pltpu.VMEM((rows, LANES), F32)],
        compiler_params=pltpu.CompilerParams(vmem_limit_bytes=24 * 1024 * 1024),
        cost_estimate=pl.CostEstimate(flops=2 * big * feat, bytes_accessed=6 * feat * columns, transcendentals=0),
    )(got, pull, push, logits, stu_inv, stu_w, x, weight, own_hot, rise, log_part, unit, norm)
    return loss.reshape(()), grad_weight, grad_rows


def solution(mesh):
    placed = (
        P("img", None, None),
        P("img", None, None),
        P(None, AXES),
        P(None, AXES),
        P("img", None),
    )
    return jax.shard_map(
        shards,
        mesh=mesh,
        in_specs=placed,
        out_specs=(P(), P(None, AXES), P(AXES, None)),
        check_vma=False,
    )
```

```python
import functools

import jax
import jax.numpy as jnp
from jax import lax
from jax.experimental import pallas as pl
from jax.experimental.pallas import tpu as pltpu
from jax.sharding import PartitionSpec as P

ITERS = 3
TEACHER_TEMP = 0.07
STUDENT_TEMP = 0.1
NORM_EPS = 1e-06
GRAD_SCALE = 1.0 / 128.0
EMPTY = 2.0
LANES = 128
F32 = jnp.float32
BF16 = jnp.bfloat16
AXES = ("img", "proto")

VMEM = pl.BlockSpec(memory_space=pltpu.VMEM)
HBM = pl.BlockSpec(memory_space=pltpu.HBM)


def call(body, outs, *args, flops=0, moved=0, exps=0, limit=24, specs=None, out_specs=None, scratch=()):
    return pl.pallas_call(
        body,
        out_shape=outs,
        in_specs=specs or [VMEM] * len(args),
        out_specs=out_specs or tuple(VMEM for _ in outs),
        scratch_shapes=scratch,
        compiler_params=pltpu.CompilerParams(vmem_limit_bytes=limit * 1024 * 1024),
        cost_estimate=pl.CostEstimate(flops=flops, bytes_accessed=moved, transcendentals=exps),
    )(*args)


def near(x):
    return pltpu.with_memory_space_constraint(x, pltpu.VMEM)


def far(x):
    return pltpu.with_memory_space_constraint(x, pltpu.HBM)


def dot(a, b, dims, precision=None):
    return lax.dot_general(a, b, (dims, ((), ())), precision=precision, preferred_element_type=F32)


def iota(shape, dim):
    return lax.broadcasted_iota(jnp.int32, shape, dim)


def add_all(parts):
    return functools.reduce(jnp.add, parts)


def to_column(vector, rows):
    parts = [jnp.broadcast_to(vector[i : i + 1], (LANES, LANES)).T for i in range(vector.shape[0])]
    return jnp.concatenate(parts, axis=0)[:rows]


def to_tiles(part, width):
    rows = part.shape[0]
    if width > rows:
        part = jnp.concatenate([part, jnp.zeros((width - rows, LANES), F32)], axis=0)
    row = jnp.sum(part.T, axis=0, keepdims=True)
    return jnp.concatenate([row[:, i : i + LANES] for i in range(0, width, LANES)], axis=0)


def split(tiles):
    high = tiles.astype(BF16).astype(F32)
    return [high, tiles - high]


def fold(x):
    return add_all([x[:, i : i + LANES] for i in range(0, x.shape[1], LANES)])


def spread(col, width):
    return jnp.concatenate([col] * (width // LANES), axis=1)


def chunks(columns):
    step = min(512, columns)
    return step, columns // step


def odd_half():
    return lax.rem(lax.axis_index("proto"), 2)


def select_kernel(mask_hbm, stu_hbm, tea_hbm, sent_out, unit_out, norm_out, mask_ref, stu_ref, tea_ref, sems):
    pairs = ((mask_hbm, mask_ref), (tea_hbm, tea_ref), (stu_hbm, stu_ref))
    copies = [pltpu.make_async_copy(*pair, sems.at[i]) for i, pair in enumerate(pairs)]
    for copy in copies:
        copy.start()
    for copy in copies:
        copy.wait()
    own, feat = unit_out.shape
    patches = mask_ref.shape[1]
    slot = iota((own, patches), 0) + lax.axis_index("proto") * own
    mask = jnp.broadcast_to(mask_ref[...].astype(F32), (own, patches))
    upto = (iota((patches, patches), 0) <= iota((patches, patches), 1)).astype(BF16)
    rank = dot(mask.astype(BF16), upto, ((1,), (0,)))
    pick = jnp.where((rank == slot.astype(F32) + 1.0) & (mask > 0.5), 1.0, 0.0).astype(BF16)
    valid = slot[:, :1].astype(F32) < rank[:, patches - 1 :]
    for source, at in ((tea_ref, 0), (stu_ref, feat)):
        rows = dot(pick, source[0], ((1,), (0,)))
        norm = jnp.sqrt(jnp.sum(rows * rows, axis=1, keepdims=True) + NORM_EPS)
        unit = (rows / norm).astype(BF16)
        sent = jnp.where(valid, unit.astype(F32), EMPTY).astype(BF16)
        sent_out[:, :, at : at + feat] = jnp.broadcast_to(sent[None], (sent_out.shape[0], own, feat))
        if source is stu_ref:
            unit_out[...] = unit.astype(F32)
            norm_out[...] = jnp.broadcast_to(norm, norm_out.shape)


def norms_kernel(stu_hbm, tea_hbm, stu_w, tea_w, stu_out, tea_out, sems):
    step, count = chunks(stu_w.shape[1])
    parts = [slice(i * step, (i + 1) * step) for i in range(count)]
    sets = ((tea_hbm, tea_w, tea_out), (stu_hbm, stu_w, stu_out))
    copies = [
        [pltpu.make_async_copy(source.at[:, at], ref.at[:, at], sems.at[k, i]) for i, at in enumerate(parts)]
        for k, (source, ref, _) in enumerate(sets)
    ]
    for row in copies:
        for copy in row:
            copy.start()
    for row, (_, ref, out) in zip(copies, sets):
        for copy, at in zip(row, parts):
            copy.wait()
            w = ref[:, at].astype(F32)
            out[:, at] = 1.0 / jnp.sqrt(jnp.sum(w * w, axis=0, keepdims=True) + NORM_EPS)


def packing(mine, other, at, feat, rows, emit):
    half = mine.shape[0]
    step = min(256, half)
    before = jnp.zeros((1, 1), F32)
    upto = (iota((step, step), 0) <= iota((step, step), 1)).astype(BF16)
    same = (iota((step, step), 0) == iota((step, step), 1)).astype(BF16)
    row = iota((rows, step), 0).astype(F32) + 1.0
    for h in range(2):
        for c in range(0, half, step):
            block = slice(c, c + step), slice(at, at + feat)
            data = jnp.where(odd_half() == h, mine[block], other[block])
            flags = jnp.where(data[:, :LANES].astype(F32) < 1.5, 1.0, 0.0).astype(BF16)
            place = before + dot(flags, upto, ((0,), (0,)))[:1]
            held = dot(flags, same, ((0,), (0,)))[:1]
            hot = jnp.where((row == place) & (held > 0.5), 1.0, 0.0).astype(BF16)
            emit(h * half + c, hot, data, flags)
            before = place[:, step - 1 :]


def first_kernel(mine, other, tea_w, inv, kernel_out, sent_out):
    rows = kernel_out.shape[0]
    feat = tea_w.shape[0]
    parts = []
    packing(mine, other, 0, feat, rows, lambda at, hot, data, flags: parts.append(dot(hot, data, ((1,), (0,)))))
    x = add_all(parts).astype(BF16)
    step, count = chunks(tea_w.shape[1])

    def body(i, acc):
        at = pl.ds(pl.multiple_of(i * step, step), step)
        z = dot(x, tea_w[:, at], ((1,), (0,)))
        k = jnp.exp(z * (inv[:, at] * (1.0 / TEACHER_TEMP)))
        kernel_out[:, at] = k
        c = 1.0 / jnp.sum(k, axis=0, keepdims=True)
        return acc + fold(k * c)

    acc = lax.fori_loop(0, count, body, jnp.zeros((rows, LANES), F32))
    tiles = to_tiles(acc, sent_out.shape[1] * LANES)
    sent_out[...] = jnp.broadcast_to(tiles[None], sent_out.shape)


def spots(hot, x, at, half):
    return dot(hot[:, at : at + half], x, ((0,), (0,)))


def halves(hot, x, keep_out, give_out):
    half = keep_out.shape[0]
    low, high = spots(hot, x, 0, half), spots(hot, x, half, half)
    odd = odd_half() == 1
    keep_out[...] = jnp.where(odd, high, low)
    give_out[...] = jnp.where(odd, low, high)


def student_kernel(
    mine, other, stu_w, inv, logits_out, part_out, x_out, hot_out, own_out, weight_out, keep_out, give_out, *, protos
):
    rows, feat = x_out.shape
    devices = lax.axis_size(AXES)
    each = mine.shape[0] // devices
    per_image = each * protos
    packed, count, images = [], [], []

    def emit(at, hot, data, flags):
        step = data.shape[0]
        packed.append(dot(hot, data, ((1,), (0,))))
        hot_out[:, at : at + step] = hot

    packing(mine, other, feat, feat, rows, emit)
    x = add_all(packed).astype(BF16)
    x_out[...] = x

    half = mine.shape[0]
    step = min(256, half)
    block = lax.broadcasted_iota(jnp.int32, (step, step), 0) // per_image
    same = (block == iota((step, step), 1) // per_image).astype(BF16)
    for c in range(0, half, step):
        flags = [
            jnp.where(ref[c : c + step, feat : feat + LANES].astype(F32) < 1.5, 1.0, 0.0) for ref in (mine, other)
        ]
        held = dot(same, (flags[0] + flags[1]).astype(BF16), ((1,), (0,)))
        for h in range(2):
            hot = hot_out[:, h * half + c : h * half + c + step]
            count.append(dot(hot, held.astype(BF16), ((1,), (0,))))
        first = (iota(held.shape, 0) % per_image == 0) & (held > 0.5)
        images.append(jnp.sum(first.astype(F32), axis=0, keepdims=True))
    weight_out[...] = 1.0 / (jnp.maximum(add_all(count), 1.0) * add_all(images))

    own = own_out.shape[0]
    me = lax.axis_index("img") * protos + lax.axis_index("proto")
    q = iota((own, 2 * half), 0)
    spot = q // each * half + me * each + q % each
    mark = (iota((own, 2 * half), 1) == spot).astype(BF16)
    own_out[...] = dot(mark, hot_out[...], ((1,), (1,)))

    step, count = chunks(stu_w.shape[1])

    def body(i, accs):
        at = pl.ds(pl.multiple_of(i * step, step), step)
        w = stu_w[:, at]
        n = inv[:, at]
        l = dot(x, w, ((1,), (0,))) * (n * (1.0 / STUDENT_TEMP))
        logits_out[:, at] = l
        p = jnp.exp(l)
        return accs[0] + fold(p), accs[1] + dot((p * n).astype(BF16), w, ((1,), (1,)))

    zeros = jnp.zeros((rows, LANES), F32), jnp.zeros((rows, feat), F32)
    acc, pull = lax.fori_loop(0, count, body, zeros)
    part_out[...] = to_tiles(acc, part_out.shape[0] * LANES)
    halves(hot_out, pull.astype(BF16), keep_out, give_out)


def fill(sent_out, keep, got, vectors):
    devices, each, wide = sent_out.shape
    feat = keep.shape[1]
    sent_out[:, :, :feat] = (keep[...] + got[...]).reshape(devices, each, feat).astype(BF16)
    tiles = add_all_rows([part for vector in vectors for part in split(vector)], each, (wide - feat) // LANES)
    sent_out[:, :, feat:] = jnp.broadcast_to(tiles[None], (devices, each, wide - feat)).astype(BF16)


def add_all_rows(parts, each, groups):
    tiles = jnp.concatenate(parts, axis=0)
    spare = each * groups - tiles.shape[0]
    if spare:
        tiles = jnp.concatenate([tiles, jnp.zeros((spare, LANES), F32)], axis=0)
    return jnp.concatenate([tiles[g * each : (g + 1) * each] for g in range(groups)], axis=1)


def vectors_of(got, feat, width, count):
    _, each, wide = got.shape
    sums = jnp.sum(got[:, :, feat:].astype(F32), axis=0)
    tiles = jnp.concatenate([sums[:, g : g + LANES] for g in range(0, wide - feat, LANES)], axis=0)
    m = width // LANES
    return [tiles[2 * v * m : (2 * v + 1) * m] + tiles[(2 * v + 1) * m : (2 * v + 2) * m] for v in range(count)]


def slots_of(got, feat):
    devices, each, _ = got.shape
    parts = got[:, :, :feat].astype(F32).reshape(devices // 2, 2, each, feat)
    return jnp.sum(parts, axis=0).reshape(2 * each, feat)


def sweep_kernel(got, kernel, total_out):
    rows, columns = kernel.shape
    scale = to_column(1.0 / jnp.sum(got[...], axis=0), rows)
    step, count = chunks(columns)
    wide = spread(scale, step)

    def body(i, acc):
        at = pl.ds(pl.multiple_of(i * step, step), step)
        k = kernel[:, at]
        c = 1.0 / jnp.sum(k * wide, axis=0, keepdims=True)
        return acc + fold(k * c)

    acc = lax.fori_loop(0, count, body, jnp.zeros((rows, LANES), F32))
    total_out[...] = to_tiles(acc, total_out.shape[0] * LANES)


def last_sweep_kernel(
    got, kernel, x, stu_w, inv, hot, scaled_out, total_out, cross_out, keep_out, give_out
):
    rows, columns = kernel.shape
    feat = stu_w.shape[0]
    width = total_out.shape[0] * LANES
    (total,) = vectors_of(got, feat, width, 1)
    scale = to_column(1.0 / total, rows)
    step, count = chunks(columns)
    wide = spread(scale, step)

    def body(i, accs):
        at = pl.ds(pl.multiple_of(i * step, step), step)
        k = kernel[:, at]
        kc = k * (1.0 / jnp.sum(k * wide, axis=0, keepdims=True))
        scaled_out[:, at] = kc
        kn = (kc * inv[:, at]).astype(BF16)
        return accs[0] + fold(kc), accs[1] + dot(kn, stu_w[:, at], ((1,), (1,)))

    zeros = jnp.zeros((rows, LANES), F32), jnp.zeros((rows, feat), F32)
    total, push = lax.fori_loop(0, count, body, zeros)
    total_out[...] = to_tiles(total, width)
    cross_out[...] = to_tiles(fold(push * x[...].astype(F32)) * (1.0 / STUDENT_TEMP), width)
    halves(hot, push.astype(BF16), keep_out, give_out)


def fill_kernel(keep, got, total, cross, sent_out):
    fill(sent_out, keep, got, [total[...], cross[...]])


def prepare_kernel(got, scaled, logits, inv, weight, own, pull_out, push_out, rise_out, loss_out, *, scale):
    rows, columns = scaled.shape
    feat = rise_out.shape[1]
    width = -(-rows // LANES) * LANES
    _, partition = vectors_of(got, feat, width, 2)
    partition = to_column(partition, rows)
    share = weight[...]
    loss_out[...] = jnp.log(partition)
    factor = share * (rows / STUDENT_TEMP)
    step, count = chunks(columns)
    grow, shrink = spread(factor / partition, step), spread(factor, step)

    def body(i, _):
        at = pl.ds(pl.multiple_of(i * step, step), step)
        n = inv[:, at] * scale
        pull_out[:, at] = grow * jnp.exp(logits[:, at]) * n
        push_out[:, at] = shrink * scaled[:, at] * n
        return 0

    lax.fori_loop(0, count, body, 0)
    held = dot(own[...], factor / partition, ((1,), (0,)), lax.Precision.HIGHEST)
    rise_out[...] = slots_of(got, feat) * held[:, :1]


def final_kernel(
    got, pull, push, logits, inv, stu_w, x, weight, own, rise, log_part, unit, norm, out_hbm, rows_out, loss_out, out, sems
):
    rows, columns = pull.shape
    feat = x.shape[1]
    width = -(-rows // LANES) * LANES
    total, cross = (to_column(v, rows) for v in vectors_of(got, feat, width, 2))
    scale = 1.0 / total
    step, count = chunks(columns)
    wide = spread(scale, step)
    copies = []
    for i in range(count):
        at = slice(i * step, (i + 1) * step)
        g = pull[:, at] - wide * push[:, at]
        along = jnp.sum(g * logits[:, at], axis=0, keepdims=True) * (inv[:, at] * STUDENT_TEMP)
        out[:, at] = dot(x[...], g.astype(BF16), ((0,), (0,))) - stu_w[:, at].astype(F32) * along
        copies.append(pltpu.make_async_copy(out.at[:, at], out_hbm.at[:, at], sems.at[i]))
        copies[-1].start()
    share = weight[...]
    loss = jnp.sum(share * (log_part[...] - cross * scale), axis=0, keepdims=True)
    loss_out[...] = loss[:, :1]
    held = dot(own[...], share * (rows / STUDENT_TEMP) * scale, ((1,), (0,)), lax.Precision.HIGHEST)
    full = rise[...] - slots_of(got, feat) * held[:, :1]
    u = unit[...]
    rows_out[...] = (full - u * jnp.sum(u * full, axis=1, keepdims=True)) / norm[:, :1]
    for copy in copies:
        copy.wait()


def shards(student_feats, teacher_feats, student_weight, teacher_weight, patch_masks):
    devices = lax.axis_size(AXES)
    protos = lax.axis_size("proto")
    images, patches, feat = student_feats.shape
    assert images == 1 and protos % 2 == 0
    columns = student_weight.shape[1]
    own = patches // 2 // protos
    each = own // 2
    half = each * devices
    rows = 2 * half * 5 // 16
    tiles = -(-rows // LANES)
    wide = feat + LANES * -(-4 * tiles // each)
    big = rows * columns
    exchange = functools.partial(lax.all_to_all, axis_name=AXES, split_axis=0, concat_axis=0)
    swap = functools.partial(lax.ppermute, axis_name="proto", perm=[(p, p ^ 1) for p in range(protos)])
    vector = pltpu.VMEM((tiles, LANES), F32)
    matrix = pltpu.VMEM((rows, columns), F32)
    column = pltpu.VMEM((rows, LANES), F32)
    line = pltpu.VMEM((1, columns), F32)
    block = pltpu.VMEM((half, feat), F32)
    payload = pltpu.VMEM((devices, each, wide), BF16)

    sent, unit, norm = call(
        select_kernel,
        (
            pltpu.VMEM((devices // 2, own, 2 * feat), BF16),
            pltpu.VMEM((own, feat), F32),
            pltpu.VMEM((own, LANES), F32),
        ),
        far(patch_masks),
        far(student_feats),
        far(teacher_feats),
        specs=[HBM] * 3,
        scratch=[
            pltpu.VMEM(patch_masks.shape, patch_masks.dtype),
            pltpu.VMEM(student_feats.shape, BF16),
            pltpu.VMEM(teacher_feats.shape, BF16),
            pltpu.SemaphoreType.DMA((3,)),
        ],
    )
    mine = exchange(sent.reshape(devices, each, 2 * feat)).reshape(half, 2 * feat)
    mine, student_weight, teacher_weight = lax.optimization_barrier((mine, student_weight, teacher_weight))
    other = near(swap(mine))
    mine = near(mine)
    held = pltpu.VMEM(student_weight.shape, BF16)
    stu_w, tea_w, stu_inv, tea_inv = call(
        norms_kernel,
        (held, held, line, line),
        far(student_weight),
        far(teacher_weight),
        flops=4 * feat * columns,
        moved=8 * feat * columns,
        specs=[HBM] * 2,
        scratch=[pltpu.SemaphoreType.DMA((2, chunks(columns)[1]))],
    )
    kernel, sent = call(
        first_kernel,
        (matrix, pltpu.VMEM((devices, tiles, LANES), F32)),
        mine,
        other,
        tea_w,
        tea_inv,
        flops=2 * big * feat,
        moved=4 * big,
        exps=big,
    )
    got = near(exchange(sent))
    mine, other, got = lax.optimization_barrier((mine, other, got))
    logits, part, x, hot, own_hot, weight, keep, give = call(
        functools.partial(student_kernel, protos=protos),
        (
            matrix,
            vector,
            pltpu.VMEM((rows, feat), BF16),
            pltpu.VMEM((rows, 2 * half), BF16),
            pltpu.VMEM((own, rows), F32),
            column,
            block,
            block,
        ),
        mine,
        other,
        stu_w,
        stu_inv,
        flops=4 * big * feat,
        moved=4 * big,
        exps=big,
    )
    give = near(swap(give))
    (total,) = call(sweep_kernel, (vector,), got, kernel, flops=4 * big, moved=4 * big)
    (sent,) = call(fill_kernel, (payload,), keep, give, total, part)
    swept = near(exchange(sent))
    scaled, total, cross, keep, give = call(
        last_sweep_kernel,
        (matrix, vector, vector, block, block),
        swept,
        kernel,
        x,
        stu_w,
        stu_inv,
        hot,
        flops=2 * big * feat,
        moved=12 * big,
    )
    give = near(swap(give))
    pull, push, rise, log_part = call(
        functools.partial(prepare_kernel, scale=columns * devices * GRAD_SCALE),
        (matrix, matrix, pltpu.VMEM((own, feat), F32), column),
        swept,
        scaled,
        logits,
        stu_inv,
        weight,
        own_hot,
        flops=4 * big,
        moved=16 * big,
        exps=big,
    )
    keep, pull, push, rise, log_part = lax.optimization_barrier((keep, pull, push, rise, log_part))
    (sent,) = call(fill_kernel, (payload,), keep, give, total, cross)
    got = near(exchange(sent))
    grad_weight, grad_rows, loss = call(
        final_kernel,
        (
            jax.ShapeDtypeStruct((feat, columns), F32),
            jax.ShapeDtypeStruct((own, feat), F32),
            jax.ShapeDtypeStruct((1, 1), F32),
        ),
        got,
        pull,
        push,
        logits,
        stu_inv,
        stu_w,
        x,
        weight,
        own_hot,
        rise,
        log_part,
        unit,
        norm,
        flops=2 * big * feat,
        moved=8 * feat * columns,
        out_specs=(HBM, VMEM, VMEM),
        scratch=[pltpu.VMEM((feat, columns), F32), pltpu.SemaphoreType.DMA((chunks(columns)[1],))],
    )
    return loss.reshape(()), grad_weight, grad_rows


def solution(mesh):
    placed = (
        P("img", None, None),
        P("img", None, None),
        P(None, AXES),
        P(None, AXES),
        P("img", None),
    )
    return jax.shard_map(
        shards,
        mesh=mesh,
        in_specs=placed,
        out_specs=(P(), P(None, AXES), P(AXES, None)),
        check_vma=False,
    )
```

```python
import functools

import jax
import jax.numpy as jnp
from jax import lax
from jax.experimental import pallas as pl
from jax.experimental.pallas import tpu as pltpu
from jax.sharding import PartitionSpec as P

ITERS = 3
TEACHER_TEMP = 0.07
STUDENT_TEMP = 0.1
NORM_EPS = 1e-06
GRAD_SCALE = 1.0 / 128.0
EMPTY = 2.0
LANES = 128
F32 = jnp.float32
BF16 = jnp.bfloat16
AXES = ("img", "proto")

VMEM = pl.BlockSpec(memory_space=pltpu.VMEM)
HBM = pl.BlockSpec(memory_space=pltpu.HBM)


def call(body, outs, *args, flops=0, moved=0, exps=0, limit=24, specs=None, out_specs=None, scratch=()):
    return pl.pallas_call(
        body,
        out_shape=outs,
        in_specs=specs or [VMEM] * len(args),
        out_specs=out_specs or tuple(VMEM for _ in outs),
        scratch_shapes=scratch,
        compiler_params=pltpu.CompilerParams(vmem_limit_bytes=limit * 1024 * 1024),
        cost_estimate=pl.CostEstimate(flops=flops, bytes_accessed=moved, transcendentals=exps),
    )(*args)


def near(x):
    return pltpu.with_memory_space_constraint(x, pltpu.VMEM)


def far(x):
    return pltpu.with_memory_space_constraint(x, pltpu.HBM)


def dot(a, b, dims, precision=None):
    return lax.dot_general(a, b, (dims, ((), ())), precision=precision, preferred_element_type=F32)


def iota(shape, dim):
    return lax.broadcasted_iota(jnp.int32, shape, dim)


def add_all(parts):
    return functools.reduce(jnp.add, parts)


def to_column(vector, rows):
    parts = [jnp.broadcast_to(vector[i : i + 1], (LANES, LANES)).T for i in range(vector.shape[0])]
    return jnp.concatenate(parts, axis=0)[:rows]


def to_tiles(part, width):
    rows = part.shape[0]
    if width > rows:
        part = jnp.concatenate([part, jnp.zeros((width - rows, LANES), F32)], axis=0)
    row = jnp.sum(part.T, axis=0, keepdims=True)
    return jnp.concatenate([row[:, i : i + LANES] for i in range(0, width, LANES)], axis=0)


def split(tiles):
    high = tiles.astype(BF16).astype(F32)
    return [high, tiles - high]


def fold(x):
    return add_all([x[:, i : i + LANES] for i in range(0, x.shape[1], LANES)])


def spread(col, width):
    return jnp.concatenate([col] * (width // LANES), axis=1)


def chunks(columns):
    step = min(512, columns)
    return [slice(at, at + step) for at in range(0, columns, step)]


def over_chunks(columns, body, start):
    for at in chunks(columns):
        start = body(at, start)
    return start


def start_load(source, target, sems):
    parts = chunks(target.shape[1])
    copies = [pltpu.make_async_copy(source.at[:, at], target.at[:, at], sems.at[i]) for i, at in enumerate(parts)]
    for copy in copies:
        copy.start()
    return copies


def inverse_norms(w):
    w = w.astype(F32)
    return 1.0 / jnp.sqrt(jnp.sum(w * w, axis=0, keepdims=True) + NORM_EPS)


def odd_half():
    return lax.rem(lax.axis_index("proto"), 2)


def select_kernel(mask_hbm, stu_hbm, tea_hbm, sent_out, unit_out, norm_out, mask_ref, stu_ref, tea_ref, sems):
    pairs = ((mask_hbm, mask_ref), (tea_hbm, tea_ref), (stu_hbm, stu_ref))
    copies = [pltpu.make_async_copy(*pair, sems.at[i]) for i, pair in enumerate(pairs)]
    for copy in copies:
        copy.start()
    copies[0].wait()
    own, feat = unit_out.shape
    patches = mask_ref.shape[1]
    slot = iota((own, patches), 0) + lax.axis_index("proto") * own
    mask = jnp.broadcast_to(mask_ref[...].astype(F32), (own, patches))
    upto = (iota((patches, patches), 0) <= iota((patches, patches), 1)).astype(BF16)
    rank = dot(mask.astype(BF16), upto, ((1,), (0,)))
    pick = jnp.where((rank == slot.astype(F32) + 1.0) & (mask > 0.5), 1.0, 0.0).astype(BF16)
    valid = slot[:, :1].astype(F32) < rank[:, patches - 1 :]
    for copy, source, at in ((copies[1], tea_ref, 0), (copies[2], stu_ref, feat)):
        copy.wait()
        rows = dot(pick, source[0], ((1,), (0,)))
        norm = jnp.sqrt(jnp.sum(rows * rows, axis=1, keepdims=True) + NORM_EPS)
        unit = (rows / norm).astype(BF16)
        sent = jnp.where(valid, unit.astype(F32), EMPTY).astype(BF16)
        sent_out[:, :, at : at + feat] = jnp.broadcast_to(sent[None], (sent_out.shape[0], own, feat))
        if source is stu_ref:
            unit_out[...] = unit.astype(F32)
            norm_out[...] = jnp.broadcast_to(norm, norm_out.shape)


def norms_kernel(tea_hbm, tea_w, inv_out, sems):
    copies = start_load(tea_hbm, tea_w, sems)
    for copy, at in zip(copies, chunks(tea_w.shape[1])):
        copy.wait()
        inv_out[:, at] = inverse_norms(tea_w[:, at])


def in_order(mine, other, h, at, feat):
    return jnp.where(odd_half() == h, mine[:, at : at + feat], other[:, at : at + feat])


def slot_flags(data):
    return jnp.where(data[:, :LANES].astype(F32) < 1.5, 1.0, 0.0).astype(BF16)


def packing(flags, hot_out):
    rows = hot_out.shape[0]
    half = flags[0].shape[0]
    step = min(256, half)
    before = jnp.zeros((1, 1), F32)
    upto = (iota((step, step), 0) <= iota((step, step), 1)).astype(BF16)
    same = (iota((step, step), 0) == iota((step, step), 1)).astype(BF16)
    row = iota((rows, step), 0).astype(F32) + 1.0
    for h in range(2):
        for c in range(0, half, step):
            part = flags[h][c : c + step]
            place = before + dot(part, upto, ((0,), (0,)))[:1]
            held = dot(part, same, ((0,), (0,)))[:1]
            hot = jnp.where((row == place) & (held > 0.5), 1.0, 0.0).astype(BF16)
            hot_out[:, h * half + c : h * half + c + step] = hot
            before = place[:, step - 1 :]


def pack_rows(hot, mine, other, at, feat):
    half = mine.shape[0]
    parts = [
        dot(hot[:, h * half : (h + 1) * half], in_order(mine, other, h, at, feat), ((1,), (0,))) for h in range(2)
    ]
    return add_all(parts).astype(BF16)


def first_kernel(mine, other, tea_w, inv, kernel_out, sent_out, hot_out):
    rows = kernel_out.shape[0]
    feat = tea_w.shape[0]
    packing([slot_flags(in_order(mine, other, h, 0, LANES)) for h in range(2)], hot_out)
    x = pack_rows(hot_out, mine, other, 0, feat)

    def body(at, acc):
        z = dot(x, tea_w[:, at], ((1,), (0,)))
        k = jnp.exp(z * (inv[:, at] * (1.0 / TEACHER_TEMP)))
        kernel_out[:, at] = k
        c = 1.0 / jnp.sum(k, axis=0, keepdims=True)
        return acc + fold(k * c)

    acc = over_chunks(tea_w.shape[1], body, jnp.zeros((rows, LANES), F32))
    tiles = to_tiles(acc, sent_out.shape[1] * LANES)
    sent_out[...] = jnp.broadcast_to(tiles[None], sent_out.shape)


def spots(hot, sums, at, half):
    return dot(hot[:, at : at + half], sums, ((0,), (1,)))


def halves(hot, sums, keep_out, give_out):
    half = keep_out.shape[0]
    low, high = spots(hot, sums, 0, half), spots(hot, sums, half, half)
    odd = odd_half() == 1
    keep_out[...] = jnp.where(odd, high, low)
    give_out[...] = jnp.where(odd, low, high).astype(BF16)


def student_kernel(mine, other, stu_w, hot, inv_out, logits_out, part_out, xt_out, keep_out, give_out, pulls):
    rows, columns = logits_out.shape
    feat = stu_w.shape[0]
    x = pack_rows(hot, mine, other, feat, feat)
    xt_out[...] = x.astype(F32).T.astype(BF16)

    def body(at, acc):
        w = stu_w[:, at]
        n = inverse_norms(w)
        inv_out[:, at] = n
        l = dot(x, w, ((1,), (0,))) * (n * (1.0 / STUDENT_TEMP))
        logits_out[:, at] = l
        p = jnp.exp(l)
        pulls[:, at] = (p * n).astype(BF16)
        return acc + fold(p)

    acc = over_chunks(columns, body, jnp.zeros((rows, LANES), F32))
    part_out[...] = to_tiles(acc, part_out.shape[0] * LANES)
    pull = dot(stu_w[...], pulls[...], ((1,), (1,)))
    halves(hot, pull.astype(BF16), keep_out, give_out)


def row_weights(mine, other, hot, own_out, weight_out, protos):
    devices = lax.axis_size(AXES)
    half = mine.shape[0]
    each = half // devices
    per_image = each * protos
    step = min(256, half)
    count, images = [], []
    block = iota((step, step), 0) // per_image
    same = (block == iota((step, step), 1) // per_image).astype(BF16)
    for c in range(0, half, step):
        flags = [slot_flags(ref[c : c + step, :LANES]).astype(F32) for ref in (mine, other)]
        held = dot(same, (flags[0] + flags[1]).astype(BF16), ((1,), (0,)))
        for h in range(2):
            count.append(dot(hot[:, h * half + c : h * half + c + step], held.astype(BF16), ((1,), (0,))))
        first = (iota(held.shape, 0) % per_image == 0) & (held > 0.5)
        images.append(jnp.sum(first.astype(F32), axis=0, keepdims=True))
    weight_out[...] = 1.0 / (jnp.maximum(add_all(count), 1.0) * add_all(images))

    own = own_out.shape[0]
    me = lax.axis_index("img") * protos + lax.axis_index("proto")
    q = iota((own, 2 * half), 0)
    spot = q // each * half + me * each + q % each
    mark = (iota((own, 2 * half), 1) == spot).astype(BF16)
    own_out[...] = dot(mark, hot[...], ((1,), (1,)))


def fill(sent_out, keep, got, vectors):
    devices, each, wide = sent_out.shape
    feat = keep.shape[1]
    sent_out[:, :, :feat] = (keep[...] + got[...].astype(F32)).reshape(devices, each, feat).astype(BF16)
    tiles = add_all_rows([part for vector in vectors for part in split(vector)], each, (wide - feat) // LANES)
    sent_out[:, :, feat:] = jnp.broadcast_to(tiles[None], (devices, each, wide - feat)).astype(BF16)


def add_all_rows(parts, each, groups):
    tiles = jnp.concatenate(parts, axis=0)
    spare = each * groups - tiles.shape[0]
    if spare:
        tiles = jnp.concatenate([tiles, jnp.zeros((spare, LANES), F32)], axis=0)
    return jnp.concatenate([tiles[g * each : (g + 1) * each] for g in range(groups)], axis=1)


def vectors_of(got, feat, width, count):
    _, each, wide = got.shape
    sums = jnp.sum(got[:, :, feat:].astype(F32), axis=0)
    tiles = jnp.concatenate([sums[:, g : g + LANES] for g in range(0, wide - feat, LANES)], axis=0)
    m = width // LANES
    return [tiles[2 * v * m : (2 * v + 1) * m] + tiles[(2 * v + 1) * m : (2 * v + 2) * m] for v in range(count)]


def slots_of(got, feat):
    devices, each, _ = got.shape
    parts = got[:, :, :feat].astype(F32).reshape(devices // 2, 2, each, feat)
    return jnp.sum(parts, axis=0).reshape(2 * each, feat)


def sweep_kernel(got, kernel, part, keep, give, sent_out):
    rows, columns = kernel.shape
    scale = to_column(1.0 / jnp.sum(got[...], axis=0), rows)
    wide = spread(scale, chunks(columns)[0].stop)

    def body(at, acc):
        k = kernel[:, at]
        c = 1.0 / jnp.sum(k * wide, axis=0, keepdims=True)
        return acc + fold(k * c)

    acc = over_chunks(columns, body, jnp.zeros((rows, LANES), F32))
    fill(sent_out, keep, give, [to_tiles(acc, part.shape[0] * LANES), part[...]])


def last_sweep_kernel(got, kernel, xt, stu_w, inv, hot, scaled_out, total_out, cross_out, keep_out, give_out, pushes):
    rows, columns = kernel.shape
    feat = stu_w.shape[0]
    width = total_out.shape[0] * LANES
    (total,) = vectors_of(got, feat, width, 1)
    scale = to_column(1.0 / total, rows)
    wide = spread(scale, chunks(columns)[0].stop)

    def body(at, acc):
        k = kernel[:, at]
        kc = k * (1.0 / jnp.sum(k * wide, axis=0, keepdims=True))
        scaled_out[:, at] = kc
        pushes[:, at] = (kc * inv[:, at]).astype(BF16)
        return acc + fold(kc)

    acc = over_chunks(columns, body, jnp.zeros((rows, LANES), F32))
    total_out[...] = to_tiles(acc, width)
    push = dot(stu_w[...], pushes[...], ((1,), (1,)))
    halves(hot, push.astype(BF16), keep_out, give_out)
    cross = jnp.sum(push * xt[...].astype(F32), axis=0, keepdims=True) * (1.0 / STUDENT_TEMP)
    if width > rows:
        cross = jnp.concatenate([cross, jnp.zeros((1, width - rows), F32)], axis=1)
    cross_out[...] = jnp.concatenate([cross[:, i : i + LANES] for i in range(0, width, LANES)], axis=0)


def fill_kernel(keep, got, total, cross, sent_out):
    fill(sent_out, keep, got, [total[...], cross[...]])


def prepare_kernel(
    got, scaled, logits, inv, mine, other, hot, pull_out, push_out, rise_out, log_out, own_out, weight_out, *, scale, protos
):
    rows, columns = scaled.shape
    feat = rise_out.shape[1]
    width = -(-rows // LANES) * LANES
    _, partition = vectors_of(got, feat, width, 2)
    partition = to_column(partition, rows)
    row_weights(mine, other, hot, own_out, weight_out, protos)
    share = weight_out[...]
    log_out[...] = jnp.log(partition)
    factor = share * (rows / STUDENT_TEMP)
    step = chunks(columns)[0].stop
    grow, shrink = spread(factor / partition, step), spread(factor, step)

    def body(at, _):
        n = inv[:, at] * scale
        pull_out[:, at] = grow * jnp.exp(logits[:, at]) * n
        push_out[:, at] = shrink * scaled[:, at] * n
        return 0

    over_chunks(columns, body, 0)
    held = dot(own_out[...], factor / partition, ((1,), (0,)), lax.Precision.HIGHEST)
    rise_out[...] = slots_of(got, feat) * held[:, :1]


def final_kernel(
    got,
    pull,
    push,
    logits,
    inv,
    stu_w,
    xt,
    weight,
    own,
    rise,
    log_part,
    unit,
    norm,
    out_hbm,
    rows_hbm,
    loss_hbm,
    out,
    rows_out,
    loss_out,
    sems,
):
    rows, columns = pull.shape
    feat = xt.shape[0]
    width = -(-rows // LANES) * LANES
    total, cross = vectors_of(got, feat, width, 2)
    scale = to_column(1.0 / total, rows)
    parts = chunks(columns)
    wide = spread(scale, parts[0].stop)
    copies = []

    def send(source, target):
        copies.append(pltpu.make_async_copy(source, target, sems.at[len(copies)]))
        copies[-1].start()

    for at in parts:
        g = pull[:, at] - wide * push[:, at]
        along = jnp.sum(g * logits[:, at], axis=0, keepdims=True) * (inv[:, at] * STUDENT_TEMP)
        out[:, at] = dot(xt[...], g.astype(BF16), ((1,), (0,))) - stu_w[:, at].astype(F32) * along
        send(out.at[:, at], out_hbm.at[:, at])
    share = weight[...]
    loss = jnp.sum(share * (log_part[...] - to_column(cross, rows) * scale), axis=0, keepdims=True)
    loss_out[...] = loss[:, :1]
    send(loss_out, loss_hbm)
    held = dot(own[...], share * (rows / STUDENT_TEMP) * scale, ((1,), (0,)), lax.Precision.HIGHEST)
    full = rise[...] - slots_of(got, feat) * held[:, :1]
    u = unit[...]
    rows_out[...] = (full - u * jnp.sum(u * full, axis=1, keepdims=True)) / norm[:, :1]
    send(rows_out, rows_hbm)
    for copy in copies:
        copy.wait()


def shards(student_feats, teacher_feats, student_weight, teacher_weight, patch_masks):
    devices = lax.axis_size(AXES)
    protos = lax.axis_size("proto")
    images, patches, feat = student_feats.shape
    assert images == 1 and protos % 2 == 0
    columns = student_weight.shape[1]
    own = patches // 2 // protos
    each = own // 2
    half = each * devices
    rows = 2 * half * 5 // 16
    tiles = -(-rows // LANES)
    wide = feat + LANES * -(-4 * tiles // each)
    big = rows * columns
    exchange = functools.partial(lax.all_to_all, axis_name=AXES, split_axis=0, concat_axis=0)
    swap = functools.partial(lax.ppermute, axis_name="proto", perm=[(p, p ^ 1) for p in range(protos)])
    vector = pltpu.VMEM((tiles, LANES), F32)
    matrix = pltpu.VMEM((rows, columns), F32)
    column = pltpu.VMEM((rows, LANES), F32)
    line = pltpu.VMEM((1, columns), F32)
    block, small = pltpu.VMEM((half, feat), F32), pltpu.VMEM((half, feat), BF16)
    payload = pltpu.VMEM((devices, each, wide), BF16)

    sent, unit, norm = call(
        select_kernel,
        (
            pltpu.VMEM((devices // 2, own, 2 * feat), BF16),
            pltpu.VMEM((own, feat), F32),
            pltpu.VMEM((own, LANES), F32),
        ),
        far(patch_masks),
        far(student_feats),
        far(teacher_feats),
        specs=[HBM] * 3,
        scratch=[
            pltpu.VMEM(patch_masks.shape, patch_masks.dtype),
            pltpu.VMEM(student_feats.shape, BF16),
            pltpu.VMEM(teacher_feats.shape, BF16),
            pltpu.SemaphoreType.DMA((3,)),
        ],
    )
    mine = exchange(sent.reshape(devices, each, 2 * feat)).reshape(half, 2 * feat)
    mine, teacher_weight = lax.optimization_barrier((mine, teacher_weight))
    other = near(swap(mine))
    mine = near(mine)
    tea_w, tea_inv = call(
        norms_kernel,
        (pltpu.VMEM(teacher_weight.shape, BF16), line),
        far(teacher_weight),
        flops=2 * feat * columns,
        moved=4 * feat * columns,
        specs=[HBM],
        scratch=[pltpu.SemaphoreType.DMA((len(chunks(columns)),))],
    )
    kernel, sent, hot = call(
        first_kernel,
        (matrix, pltpu.VMEM((devices, tiles, LANES), F32), pltpu.VMEM((rows, 2 * half), BF16)),
        mine,
        other,
        tea_w,
        tea_inv,
        flops=2 * big * feat,
        moved=4 * big,
        exps=big,
    )
    got = near(exchange(sent))
    mine, other, sent = lax.optimization_barrier((mine, other, sent))
    stu_inv, logits, part, xt, keep, give = call(
        student_kernel,
        (line, matrix, vector, pltpu.VMEM((feat, rows), BF16), block, small),
        mine,
        other,
        student_weight,
        hot,
        flops=4 * big * feat,
        moved=4 * big,
        exps=big,
        scratch=[pltpu.VMEM((rows, columns), BF16)],
    )
    give = near(swap(give))
    (sent,) = call(sweep_kernel, (payload,), got, kernel, part, keep, give, flops=4 * big, moved=4 * big)
    swept = near(exchange(sent))
    scaled, total, cross, keep, give = call(
        last_sweep_kernel,
        (matrix, vector, vector, block, small),
        swept,
        kernel,
        xt,
        student_weight,
        stu_inv,
        hot,
        flops=2 * big * feat,
        moved=12 * big,
        scratch=[pltpu.VMEM((rows, columns), BF16)],
    )
    give = near(swap(give))
    pull, push, rise, log_part, own_hot, weight = call(
        functools.partial(prepare_kernel, scale=columns * devices * GRAD_SCALE, protos=protos),
        (matrix, matrix, pltpu.VMEM((own, feat), F32), column, pltpu.VMEM((own, rows), F32), column),
        swept,
        scaled,
        logits,
        stu_inv,
        mine,
        other,
        hot,
        flops=4 * big,
        moved=16 * big,
        exps=big,
    )
    keep, pull, push, rise, log_part = lax.optimization_barrier((keep, pull, push, rise, log_part))
    (sent,) = call(fill_kernel, (payload,), keep, give, total, cross)
    got = near(exchange(sent))
    grad_weight, grad_rows, loss = call(
        final_kernel,
        (
            jax.ShapeDtypeStruct((feat, columns), F32),
            jax.ShapeDtypeStruct((own, feat), F32),
            jax.ShapeDtypeStruct((1, 1), F32),
        ),
        got,
        pull,
        push,
        logits,
        stu_inv,
        student_weight,
        xt,
        weight,
        own_hot,
        rise,
        log_part,
        unit,
        norm,
        flops=2 * big * feat,
        moved=8 * feat * columns,
        out_specs=(HBM, HBM, HBM),
        scratch=[
            pltpu.VMEM((feat, columns), F32),
            pltpu.VMEM((own, feat), F32),
            pltpu.VMEM((1, 1), F32),
            pltpu.SemaphoreType.DMA((len(chunks(columns)) + 2,)),
        ],
    )
    return loss.reshape(()), grad_weight, grad_rows


def solution(mesh):
    placed = (
        P("img", None, None),
        P("img", None, None),
        P(None, AXES),
        P(None, AXES),
        P("img", None),
    )
    return jax.shard_map(
        shards,
        mesh=mesh,
        in_specs=placed,
        out_specs=(P(), P(None, AXES), P(AXES, None)),
        check_vma=False,
    )
```

```python
import functools

import jax
import jax.numpy as jnp
from jax import lax
from jax.experimental import pallas as pl
from jax.experimental.pallas import tpu as pltpu
from jax.sharding import PartitionSpec as P

ITERS = 3
TEACHER_TEMP = 0.07
STUDENT_TEMP = 0.1
NORM_EPS = 1e-06
GRAD_SCALE = 1.0 / 128.0
EMPTY = 2.0
LANES = 128
F32 = jnp.float32
BF16 = jnp.bfloat16
AXES = ("img", "proto")

VMEM = pl.BlockSpec(memory_space=pltpu.VMEM)
HBM = pl.BlockSpec(memory_space=pltpu.HBM)


def call(body, outs, *args, flops=0, moved=0, exps=0, limit=24, specs=None, out_specs=None, scratch=()):
    return pl.pallas_call(
        body,
        out_shape=outs,
        in_specs=specs or [VMEM] * len(args),
        out_specs=out_specs or tuple(VMEM for _ in outs),
        scratch_shapes=scratch,
        compiler_params=pltpu.CompilerParams(vmem_limit_bytes=limit * 1024 * 1024),
        cost_estimate=pl.CostEstimate(flops=flops, bytes_accessed=moved, transcendentals=exps),
    )(*args)


def near(x):
    return pltpu.with_memory_space_constraint(x, pltpu.VMEM)


def far(x):
    return pltpu.with_memory_space_constraint(x, pltpu.HBM)


def dot(a, b, dims, precision=None):
    return lax.dot_general(a, b, (dims, ((), ())), precision=precision, preferred_element_type=F32)


def iota(shape, dim):
    return lax.broadcasted_iota(jnp.int32, shape, dim)


def add_all(parts):
    return functools.reduce(jnp.add, parts)


def widen(row):
    spare = -row.shape[1] % LANES
    return jnp.concatenate([row, jnp.zeros((1, spare), F32)], axis=1) if spare else row


def tiles_of(row):
    row = widen(row)
    return [row[:, i : i + LANES] for i in range(0, row.shape[1], LANES)]


def to_column(row):
    parts = [jnp.broadcast_to(tile, (LANES, LANES)).T for tile in tiles_of(row)]
    return jnp.concatenate(parts, axis=0)[: row.shape[1]]


def to_row(part):
    rows = part.shape[0]
    spare = -rows % LANES
    if spare:
        part = jnp.concatenate([part, jnp.zeros((spare, LANES), F32)], axis=0)
    return jnp.sum(part.T, axis=0, keepdims=True)[:, :rows]


def lay_out(vectors, each, wide):
    parts = []
    for vector in vectors:
        high = vector.astype(BF16).astype(F32)
        parts += [high, vector - high]
    tiles = tiles_of(jnp.concatenate(parts, axis=1))
    tiles += [jnp.zeros((1, LANES), F32)] * (each * wide // LANES - len(tiles))
    groups = [jnp.concatenate(tiles[g : g + each], axis=0) for g in range(0, len(tiles), each)]
    return jnp.concatenate(groups, axis=1)


def read_out(got, start, rows, count):
    _, each, wide = got.shape
    sums = jnp.sum(got[:, :, start:].astype(F32), axis=0)
    line = jnp.concatenate([sums[i : i + 1, g : g + LANES] for g in range(0, wide - start, LANES) for i in range(each)], axis=1)
    parts = [line[:, p * rows : (p + 1) * rows] for p in range(2 * count)]
    return [parts[2 * v] + parts[2 * v + 1] for v in range(count)]


def fold(x):
    return add_all([x[:, i : i + LANES] for i in range(0, x.shape[1], LANES)])


def spread(col, width):
    return jnp.concatenate([col] * (width // LANES), axis=1)


def chunks(columns):
    step = min(512, columns)
    return [slice(at, at + step) for at in range(0, columns, step)]


def over_chunks(columns, body, start):
    for at in chunks(columns):
        start = body(at, start)
    return start


def start_load(source, target, sems):
    parts = chunks(target.shape[1])
    copies = [pltpu.make_async_copy(source.at[:, at], target.at[:, at], sems.at[i]) for i, at in enumerate(parts)]
    for copy in copies:
        copy.start()
    return copies


def inverse_norms(w):
    w = w.astype(F32)
    return 1.0 / jnp.sqrt(jnp.sum(w * w, axis=0, keepdims=True) + NORM_EPS)


def odd_half():
    return lax.rem(lax.axis_index("proto"), 2)


def select_kernel(mask_hbm, stu_hbm, tea_hbm, sent_out, unit_out, norm_out, mask_ref, stu_ref, tea_ref, sems):
    pairs = ((mask_hbm, mask_ref), (tea_hbm, tea_ref), (stu_hbm, stu_ref))
    copies = [pltpu.make_async_copy(*pair, sems.at[i]) for i, pair in enumerate(pairs)]
    for copy in copies:
        copy.start()
    copies[0].wait()
    own, feat = unit_out.shape
    patches = mask_ref.shape[1]
    slot = iota((own, patches), 0) + lax.axis_index("proto") * own
    mask = jnp.broadcast_to(mask_ref[...].astype(F32), (own, patches))
    upto = (iota((patches, patches), 0) <= iota((patches, patches), 1)).astype(BF16)
    rank = dot(mask.astype(BF16), upto, ((1,), (0,)))
    pick = jnp.where((rank == slot.astype(F32) + 1.0) & (mask > 0.5), 1.0, 0.0).astype(BF16)
    valid = slot[:, :1].astype(F32) < rank[:, patches - 1 :]
    for copy, source in ((copies[1], tea_ref), (copies[2], stu_ref)):
        copy.wait()
        rows = dot(pick, source[0], ((1,), (0,)))
        norm = jnp.sqrt(jnp.sum(rows * rows, axis=1, keepdims=True) + NORM_EPS)
        unit = (rows / norm).astype(BF16)
        if source is tea_ref:
            sent = jnp.where(valid, unit.astype(F32), EMPTY).astype(BF16)
            sent_out[...] = jnp.broadcast_to(sent[None], sent_out.shape)
        else:
            unit_out[...] = unit.astype(F32)
            norm_out[...] = jnp.broadcast_to(norm, norm_out.shape)


def norms_kernel(tea_hbm, tea_w, inv_out, sems):
    copies = start_load(tea_hbm, tea_w, sems)
    for copy, at in zip(copies, chunks(tea_w.shape[1])):
        copy.wait()
        inv_out[:, at] = inverse_norms(tea_w[:, at])


def in_order(mine, other, h):
    return jnp.where(odd_half() == h, mine, other)


def slot_flags(data):
    return jnp.where(data[:, :LANES].astype(F32) < 1.5, 1.0, 0.0).astype(BF16)


def packing(flags, hot_out):
    rows = hot_out.shape[0]
    half = flags[0].shape[0]
    step = min(256, half)
    before = jnp.zeros((1, 1), F32)
    upto = (iota((step, step), 0) <= iota((step, step), 1)).astype(BF16)
    same = (iota((step, step), 0) == iota((step, step), 1)).astype(BF16)
    row = iota((rows, step), 0).astype(F32) + 1.0
    for h in range(2):
        for c in range(0, half, step):
            part = flags[h][c : c + step]
            place = before + dot(part, upto, ((0,), (0,)))[:1]
            held = dot(part, same, ((0,), (0,)))[:1]
            hot = jnp.where((row == place) & (held > 0.5), 1.0, 0.0).astype(BF16)
            hot_out[:, h * half + c : h * half + c + step] = hot
            before = place[:, step - 1 :]


def blocks(half):
    step = min(256, half)
    return [(at, at + step) for at in range(0, half, step)]


def pack_rows(hot, read_mine, read_other, half):
    parts = []
    for start, stop in blocks(half):
        mine, other = read_mine(start, stop), read_other(start, stop)
        for h in range(2):
            parts.append(dot(hot[:, h * half + start : h * half + stop], in_order(mine, other, h), ((1,), (0,))))
    return add_all(parts).astype(BF16)


def first_kernel(mine, other, tea_w, inv, unit, kernel_out, sent_out, hot_out):
    rows = kernel_out.shape[0]
    devices, each, wide = sent_out.shape
    feat = tea_w.shape[0]
    packing([slot_flags(in_order(mine[:, :LANES], other[:, :LANES], h)) for h in range(2)], hot_out)
    x = pack_rows(hot_out, lambda a, b: mine[a:b], lambda a, b: other[a:b], mine.shape[0])
    held = unit[...].reshape(1, 2, each, feat)
    sent_out[:, :, :feat] = jnp.broadcast_to(held, (devices // 2, 2, each, feat)).reshape(devices, each, feat).astype(BF16)

    def body(at, acc):
        z = dot(x, tea_w[:, at], ((1,), (0,)))
        k = jnp.exp(z * (inv[:, at] * (1.0 / TEACHER_TEMP)))
        kernel_out[:, at] = k
        c = 1.0 / jnp.sum(k, axis=0, keepdims=True)
        return acc + fold(k * c)

    acc = over_chunks(tea_w.shape[1], body, jnp.zeros((rows, LANES), F32))
    tiles = lay_out([to_row(acc)], each, wide - feat)
    sent_out[:, :, feat:] = jnp.broadcast_to(tiles[None], (devices, each, wide - feat)).astype(BF16)


def spots(hot, sums, start, stop):
    return dot(hot[:, start:stop], sums, ((0,), (1,)))


def halves(hot, sums, at, keep_out, give_out):
    half = keep_out.shape[0]
    odd = odd_half() == 1
    lanes = slice(at, at + sums.shape[0])
    for start, stop in blocks(half):
        low, high = spots(hot, sums, start, stop), spots(hot, sums, half + start, half + stop)
        keep_out[start:stop, lanes] = jnp.where(odd, high, low)
        give_out[start:stop, lanes] = jnp.where(odd, low, high).astype(BF16)


def row_weights(mine, other, hot, own_out, weight_out, protos):
    devices = lax.axis_size(AXES)
    half = mine.shape[0]
    each = half // devices
    per_image = each * protos
    step = min(256, half)
    count, images = [], []
    block = iota((step, step), 0) // per_image
    same = (block == iota((step, step), 1) // per_image).astype(BF16)
    for c in range(0, half, step):
        flags = [slot_flags(ref[c : c + step, :LANES]).astype(F32) for ref in (mine, other)]
        held = dot(same, (flags[0] + flags[1]).astype(BF16), ((1,), (0,)))
        for h in range(2):
            count.append(dot(hot[:, h * half + c : h * half + c + step], held.astype(BF16), ((1,), (0,))))
        first = (iota(held.shape, 0) % per_image == 0) & (held > 0.5)
        images.append(jnp.sum(first.astype(F32), axis=0, keepdims=True))
    weight_out[...] = 1.0 / (jnp.maximum(add_all(count), 1.0) * add_all(images))

    own = own_out.shape[0]
    me = lax.axis_index("img") * protos + lax.axis_index("proto")
    q = iota((own, 2 * half), 0)
    spot = q // each * half + me * each + q % each
    mark = (iota((own, 2 * half), 1) == spot).astype(BF16)
    own_out[...] = dot(mark, hot[...], ((1,), (1,)))


def slots_of(got, feat):
    devices, each, _ = got.shape
    parts = got[:, :, :feat].astype(F32).reshape(devices // 2, 2, each, feat)
    return jnp.sum(parts, axis=0).reshape(2 * each, feat)


def sweep_kernel(got, kernel, sent_out, *, feat):
    rows, columns = kernel.shape
    (total,) = read_out(got, feat, rows, 1)
    wide = spread(to_column(1.0 / total), chunks(columns)[0].stop)

    def body(at, acc):
        k = kernel[:, at]
        c = 1.0 / jnp.sum(k * wide, axis=0, keepdims=True)
        return acc + fold(k * c)

    acc = over_chunks(columns, body, jnp.zeros((rows, LANES), F32))
    tiles = jnp.concatenate(tiles_of(to_row(acc)), axis=0)
    sent_out[...] = jnp.broadcast_to(tiles[None], sent_out.shape)


def student_kernel(
    got,
    kernel,
    mine,
    other,
    hot,
    stu_w,
    inv_out,
    logits_out,
    scaled_out,
    xt_out,
    sums_out,
    keep_out,
    give_out,
    pulls,
    pushes,
):
    rows, columns = logits_out.shape
    feat = stu_w.shape[0]
    half = keep_out.shape[0]
    each = mine.shape[1]

    def reader(ref):
        def read(start, stop):
            part = ref[start // each : stop // each, :, :feat].astype(F32)
            return part.reshape(stop - start, feat).astype(BF16)

        return read

    x = pack_rows(hot, reader(mine), reader(other), half)
    xt = x.astype(F32).T
    xt_out[...] = xt.astype(BF16)
    sums = jnp.sum(got[...], axis=0)
    total = jnp.concatenate([sums[i : i + 1] for i in range(sums.shape[0])], axis=1)[:, :rows]
    wide = spread(to_column(1.0 / total), chunks(columns)[0].stop)

    def student(at, acc):
        w = stu_w[:, at]
        n = inverse_norms(w)
        inv_out[:, at] = n
        l = dot(x, w, ((1,), (0,))) * (n * (1.0 / STUDENT_TEMP))
        logits_out[:, at] = l
        p = jnp.exp(l)
        pulls[:, at] = (p * n).astype(BF16)
        return acc + fold(p)

    def sweep(at, acc):
        k = kernel[:, at]
        kc = k * (1.0 / jnp.sum(k * wide, axis=0, keepdims=True))
        scaled_out[:, at] = kc
        pushes[:, at] = (kc * inv_out[:, at]).astype(BF16)
        return acc + fold(kc)

    zero = jnp.zeros((rows, LANES), F32)
    part = over_chunks(columns, student, zero)
    pull = dot(stu_w[...], pulls[...], ((1,), (1,)))
    total = over_chunks(columns, sweep, zero)
    push = dot(stu_w[...], pushes[...], ((1,), (1,)))
    halves(hot, pull.astype(BF16), 0, keep_out, give_out)
    halves(hot, push.astype(BF16), feat, keep_out, give_out)
    cross = jnp.sum(push * xt, axis=0, keepdims=True) * (1.0 / STUDENT_TEMP)
    sums_out[...] = lay_out([to_row(part), to_row(total), cross], *sums_out.shape)


def prepare_kernel(
    scaled, logits, inv, mine, other, hot, pull_out, push_out, own_out, weight_out, *, scale, protos
):
    rows, columns = scaled.shape
    row_weights(mine, other, hot, own_out, weight_out, protos)
    factor = spread(weight_out[...] * (rows / STUDENT_TEMP), chunks(columns)[0].stop)

    def body(at, _):
        n = inv[:, at] * scale
        pull_out[:, at] = factor * jnp.exp(logits[:, at]) * n
        push_out[:, at] = factor * scaled[:, at] * n
        return 0

    over_chunks(columns, body, 0)


def fill_kernel(keep, give, sums, sent_out):
    devices, each, wide = sent_out.shape
    both = keep.shape[1]
    sent_out[:, :, :both] = (keep[...] + give[...].astype(F32)).reshape(devices, each, both).astype(BF16)
    sent_out[:, :, both:] = jnp.broadcast_to(sums[...][None], (devices, each, wide - both)).astype(BF16)


def final_kernel(
    got,
    pull,
    push,
    logits,
    inv,
    stu_w,
    xt,
    weight,
    own,
    unit,
    norm,
    out_hbm,
    rows_hbm,
    loss_hbm,
    out,
    rows_out,
    loss_out,
    sems,
):
    rows, columns = pull.shape
    feat = xt.shape[0]
    partition, total, cross = read_out(got, 2 * feat, rows, 3)
    parts = chunks(columns)
    raise_by, lower_by = to_column(1.0 / partition), to_column(1.0 / total)
    grow, shrink = spread(raise_by, parts[0].stop), spread(lower_by, parts[0].stop)
    copies = []

    def send(source, target):
        copies.append(pltpu.make_async_copy(source, target, sems.at[len(copies)]))
        copies[-1].start()

    for at in parts:
        g = grow * pull[:, at] - shrink * push[:, at]
        along = jnp.sum(g * logits[:, at], axis=0, keepdims=True) * (inv[:, at] * STUDENT_TEMP)
        out[:, at] = dot(xt[...], g.astype(BF16), ((1,), (0,))) - stu_w[:, at].astype(F32) * along
        send(out.at[:, at], out_hbm.at[:, at])
    share = weight[...]
    loss = jnp.sum(share * to_column(jnp.log(partition) - cross / total), axis=0, keepdims=True)
    loss_out[...] = loss[:, :1]
    send(loss_out, loss_hbm)
    factors = jnp.concatenate([raise_by, lower_by], axis=1) * spread(share * (rows / STUDENT_TEMP), 2 * LANES)
    held = dot(own[...], factors, ((1,), (0,)), lax.Precision.HIGHEST)
    sums = slots_of(got, 2 * feat)
    full = sums[:, :feat] * held[:, :1] - sums[:, feat:] * held[:, LANES : LANES + 1]
    u = unit[...]
    rows_out[...] = (full - u * jnp.sum(u * full, axis=1, keepdims=True)) / norm[:, :1]
    send(rows_out, rows_hbm)
    for copy in copies:
        copy.wait()


def shards(student_feats, teacher_feats, student_weight, teacher_weight, patch_masks):
    devices = lax.axis_size(AXES)
    protos = lax.axis_size("proto")
    images, patches, feat = student_feats.shape
    assert images == 1 and protos % 2 == 0
    columns = student_weight.shape[1]
    own = patches // 2 // protos
    each = own // 2
    half = each * devices
    rows = 2 * half * 5 // 16
    tiles = -(-rows // LANES)
    extra = lambda parts: LANES * -(-parts * rows // (each * LANES))
    big = rows * columns
    exchange = functools.partial(lax.all_to_all, axis_name=AXES, split_axis=0, concat_axis=0)
    swap = functools.partial(lax.ppermute, axis_name="proto", perm=[(p, p ^ 1) for p in range(protos)])
    matrix = pltpu.VMEM((rows, columns), F32)
    column = pltpu.VMEM((rows, LANES), F32)
    line = pltpu.VMEM((1, columns), F32)

    sent, unit, norm = call(
        select_kernel,
        (
            pltpu.VMEM((devices // 2, own, feat), BF16),
            pltpu.VMEM((own, feat), F32),
            pltpu.VMEM((own, LANES), F32),
        ),
        far(patch_masks),
        far(student_feats),
        far(teacher_feats),
        specs=[HBM] * 3,
        scratch=[
            pltpu.VMEM(patch_masks.shape, patch_masks.dtype),
            pltpu.VMEM(student_feats.shape, BF16),
            pltpu.VMEM(teacher_feats.shape, BF16),
            pltpu.SemaphoreType.DMA((3,)),
        ],
    )
    mine = exchange(sent.reshape(devices, each, feat)).reshape(half, feat)
    mine, teacher_weight = lax.optimization_barrier((mine, teacher_weight))
    other = near(swap(mine))
    mine = near(mine)
    tea_w, tea_inv = call(
        norms_kernel,
        (pltpu.VMEM(teacher_weight.shape, BF16), line),
        far(teacher_weight),
        flops=2 * feat * columns,
        moved=4 * feat * columns,
        specs=[HBM],
        scratch=[pltpu.SemaphoreType.DMA((len(chunks(columns)),))],
    )
    kernel, sent, hot = call(
        first_kernel,
        (matrix, pltpu.VMEM((devices, each, feat + extra(2)), BF16), pltpu.VMEM((rows, 2 * half), BF16)),
        mine,
        other,
        tea_w,
        tea_inv,
        unit,
        flops=2 * big * feat,
        moved=4 * big,
        exps=big,
    )
    stu_mine = exchange(sent)
    stu_other = near(swap(stu_mine))
    stu_mine = near(stu_mine)
    (sent,) = call(
        functools.partial(sweep_kernel, feat=feat),
        (pltpu.VMEM((devices, tiles, LANES), F32),),
        stu_mine,
        kernel,
        flops=4 * big,
        moved=4 * big,
    )
    got = near(exchange(sent))
    stu_inv, logits, scaled, xt, sums, keep, give = call(
        student_kernel,
        (
            line,
            matrix,
            matrix,
            pltpu.VMEM((feat, rows), BF16),
            pltpu.VMEM((each, extra(6)), F32),
            pltpu.VMEM((half, 2 * feat), F32),
            pltpu.VMEM((half, 2 * feat), BF16),
        ),
        got,
        kernel,
        stu_mine,
        stu_other,
        hot,
        student_weight,
        flops=6 * big * feat,
        moved=12 * big,
        exps=big,
        scratch=[pltpu.VMEM((rows, columns), BF16), pltpu.VMEM((rows, columns), BF16)],
        limit=22 + half // 112,
    )
    give = near(swap(give))
    pull, push, own_hot, weight = call(
        functools.partial(prepare_kernel, scale=columns * devices * GRAD_SCALE, protos=protos),
        (matrix, matrix, pltpu.VMEM((own, rows), F32), column),
        scaled,
        logits,
        stu_inv,
        mine,
        other,
        hot,
        flops=4 * big,
        moved=16 * big,
        exps=big,
    )
    keep, pull, push, own_hot, weight = lax.optimization_barrier((keep, pull, push, own_hot, weight))
    (sent,) = call(fill_kernel, (pltpu.VMEM((devices, each, 2 * feat + extra(6)), BF16),), keep, give, sums)
    got = near(exchange(sent))
    grad_weight, grad_rows, loss = call(
        final_kernel,
        (
            jax.ShapeDtypeStruct((feat, columns), F32),
            jax.ShapeDtypeStruct((own, feat), F32),
            jax.ShapeDtypeStruct((1, 1), F32),
        ),
        got,
        pull,
        push,
        logits,
        stu_inv,
        student_weight,
        xt,
        weight,
        own_hot,
        unit,
        norm,
        flops=2 * big * feat,
        moved=8 * feat * columns,
        out_specs=(HBM, HBM, HBM),
        scratch=[
            pltpu.VMEM((feat, columns), F32),
            pltpu.VMEM((own, feat), F32),
            pltpu.VMEM((1, 1), F32),
            pltpu.SemaphoreType.DMA((len(chunks(columns)) + 2,)),
        ],
    )
    return loss.reshape(()), grad_weight, grad_rows


def solution(mesh):
    placed = (
        P("img", None, None),
        P("img", None, None),
        P(None, AXES),
        P(None, AXES),
        P("img", None),
    )
    return jax.shard_map(
        shards,
        mesh=mesh,
        in_specs=placed,
        out_specs=(P(), P(None, AXES), P(AXES, None)),
        check_vma=False,
    )
```

```python
import functools

import jax
import jax.numpy as jnp
from jax import lax
from jax.experimental import pallas as pl
from jax.experimental.pallas import tpu as pltpu
from jax.sharding import PartitionSpec as P

ITERS = 3
TEACHER_TEMP = 0.07
STUDENT_TEMP = 0.1
NORM_EPS = 1e-06
GRAD_SCALE = 1.0 / 128.0
EMPTY = 2.0
LANES = 128
QUAD = 4
F32 = jnp.float32
BF16 = jnp.bfloat16
AXES = ("img", "proto")

VMEM = pl.BlockSpec(memory_space=pltpu.VMEM)
HBM = pl.BlockSpec(memory_space=pltpu.HBM)


def call(body, outs, *args, flops=0, moved=0, exps=0, limit=24, specs=None, out_specs=None, scratch=()):
    return pl.pallas_call(
        body,
        out_shape=outs,
        in_specs=specs or [VMEM] * len(args),
        out_specs=out_specs or tuple(VMEM for _ in outs),
        scratch_shapes=scratch,
        compiler_params=pltpu.CompilerParams(vmem_limit_bytes=limit * 1024 * 1024),
        cost_estimate=pl.CostEstimate(flops=flops, bytes_accessed=moved, transcendentals=exps),
    )(*args)


def near(x):
    return pltpu.with_memory_space_constraint(x, pltpu.VMEM)


def far(x):
    return pltpu.with_memory_space_constraint(x, pltpu.HBM)


def dot(a, b, dims, precision=None):
    return lax.dot_general(a, b, (dims, ((), ())), precision=precision, preferred_element_type=F32)


def iota(shape, dim):
    return lax.broadcasted_iota(jnp.int32, shape, dim)


def add_all(parts):
    return functools.reduce(jnp.add, parts)


def widen(row):
    spare = -row.shape[1] % LANES
    return jnp.concatenate([row, jnp.zeros((1, spare), F32)], axis=1) if spare else row


def tiles_of(row):
    row = widen(row)
    return [row[:, i : i + LANES] for i in range(0, row.shape[1], LANES)]


def to_row(part):
    rows = part.shape[0]
    spare = -rows % LANES
    if spare:
        part = jnp.concatenate([part, jnp.zeros((spare, LANES), F32)], axis=0)
    return jnp.sum(part.T, axis=0, keepdims=True)[:, :rows]


def lay_out(vectors, each, wide):
    parts = []
    for vector in vectors:
        high = vector.astype(BF16).astype(F32)
        parts += [high, vector - high]
    tiles = tiles_of(jnp.concatenate(parts, axis=1))
    tiles += [jnp.zeros((1, LANES), F32)] * (each * wide // LANES - len(tiles))
    groups = [jnp.concatenate(tiles[g : g + each], axis=0) for g in range(0, len(tiles), each)]
    return jnp.concatenate(groups, axis=1)


def read_out(sums, rows, count):
    lines = sums.shape[0]
    turned = [sums[:, g : g + LANES].T for g in range(0, sums.shape[1], LANES)]

    def column(at, stop):
        parts = []
        while at < stop:
            line, lane = divmod(at, LANES)
            until = min(LANES, lane + stop - at)
            parts.append(turned[line // lines][lane:until, line % lines : line % lines + 1])
            at += until - lane
        return jnp.concatenate(parts, axis=0)

    return [jnp.broadcast_to(column(v * rows, (v + 1) * rows), (rows, LANES)) for v in range(count)]


def read_pairs(got, start, rows, count):
    parts = read_out(jnp.sum(got[:, :, start:].astype(F32), axis=0), rows, 2 * count)
    return [parts[2 * v] + parts[2 * v + 1] for v in range(count)]


def fold(x):
    return add_all([x[:, i : i + LANES] for i in range(0, x.shape[1], LANES)])


def spread(col, width):
    return jnp.concatenate([col] * (width // LANES), axis=1)


def chunks(columns, step=512):
    step = min(step, columns)
    return [slice(at, at + step) for at in range(0, columns, step)]


def over_chunks(columns, body, start):
    for at in chunks(columns):
        start = body(at, start)
    return start


def start_load(source, target, sems):
    parts = chunks(target.shape[1])
    copies = [pltpu.make_async_copy(source.at[:, at], target.at[:, at], sems.at[i]) for i, at in enumerate(parts)]
    for copy in copies:
        copy.start()
    return copies


def inverse_norms(w):
    w = w.astype(F32)
    return 1.0 / jnp.sqrt(jnp.sum(w * w, axis=0, keepdims=True) + NORM_EPS)


def odd_half():
    return lax.rem(lax.axis_index("proto"), 2)


def own_slots(mask_ref, feats_ref, own):
    patches = mask_ref.shape[1]
    slot = iota((own, patches), 0) + lax.axis_index("proto") * own
    mask = jnp.broadcast_to(mask_ref[...].astype(F32), (own, patches))
    upto = (iota((patches, patches), 0) <= iota((patches, patches), 1)).astype(BF16)
    rank = dot(mask.astype(BF16), upto, ((1,), (0,)))
    pick = jnp.where((rank == slot.astype(F32) + 1.0) & (mask > 0.5), 1.0, 0.0).astype(BF16)
    valid = slot[:, :1].astype(F32) < rank[:, patches - 1 :]
    rows = dot(pick, feats_ref[0], ((1,), (0,)))
    norm = jnp.sqrt(jnp.sum(rows * rows, axis=1, keepdims=True) + NORM_EPS)
    return (rows / norm).astype(BF16).astype(F32), norm, valid


def teacher_kernel(mask_hbm, stu_hbm, tea_hbm, sent_out, mask_out, stu_out, tea_ref, sems):
    pairs = ((mask_hbm, mask_out), (tea_hbm, tea_ref), (stu_hbm, stu_out))
    copies = [pltpu.make_async_copy(*pair, sems.at[i]) for i, pair in enumerate(pairs)]
    for copy in copies:
        copy.start()
    for copy in copies[:2]:
        copy.wait()
    unit, _, valid = own_slots(mask_out, tea_ref, sent_out.shape[1])
    sent_out[...] = jnp.broadcast_to(jnp.where(valid, unit, EMPTY).astype(BF16)[None], sent_out.shape)
    copies[2].wait()


def norms_kernel(mask_ref, stu_ref, tea_hbm, tea_w, inv_out, unit_out, norm_out, sems):
    copies = start_load(tea_hbm, tea_w, sems)
    unit, norm, _ = own_slots(mask_ref, stu_ref, unit_out.shape[0])
    unit_out[...] = unit
    norm_out[...] = jnp.broadcast_to(norm, norm_out.shape)
    for copy, at in zip(copies, chunks(tea_w.shape[1])):
        copy.wait()
        inv_out[:, at] = inverse_norms(tea_w[:, at])


def in_order(mine, other, h):
    return jnp.where(odd_half() == h, mine, other)


def slot_flags(data):
    return jnp.where(data[:, :LANES].astype(F32) < 1.5, 1.0, 0.0).astype(BF16)


def packing(flags, hot_out):
    rows = hot_out.shape[0]
    half = flags[0].shape[0]
    step = min(256, half)
    before = jnp.zeros((1, 1), F32)
    upto = (iota((step, step), 0) <= iota((step, step), 1)).astype(BF16)
    same = (iota((step, step), 0) == iota((step, step), 1)).astype(BF16)
    row = iota((rows, step), 0).astype(F32) + 1.0
    for h in range(2):
        for c in range(0, half, step):
            part = flags[h][c : c + step]
            place = before + dot(part, upto, ((0,), (0,)))[:1]
            held = dot(part, same, ((0,), (0,)))[:1]
            hot = jnp.where((row == place) & (held > 0.5), 1.0, 0.0).astype(BF16)
            hot_out[:, h * half + c : h * half + c + step] = hot
            before = place[:, step - 1 :]


def blocks(half):
    step = min(256, half)
    return [(at, at + step) for at in range(0, half, step)]


def pack_rows(hot, read_mine, read_other, half):
    parts = []
    for start, stop in blocks(half):
        mine, other = read_mine(start, stop), read_other(start, stop)
        for h in range(2):
            parts.append(dot(hot[:, h * half + start : h * half + stop], in_order(mine, other, h), ((1,), (0,))))
    return add_all(parts).astype(BF16)


def quads(each, feat):
    return [(row, lane) for lane in range(0, feat, LANES) for row in range(0, each, QUAD)]


def first_kernel(mine, other, tea_w, inv, unit, kernel_out, sent_out, hot_out):
    rows = kernel_out.shape[0]
    peers, _, groups, _, _ = sent_out.shape
    feat = tea_w.shape[0]
    packing([slot_flags(in_order(mine[:, :LANES], other[:, :LANES], h)) for h in range(2)], hot_out)
    x = pack_rows(hot_out, lambda a, b: mine[a:b], lambda a, b: other[a:b], mine.shape[0])
    each = unit.shape[0] // 2
    for h in range(2):
        for g, (row, lane) in enumerate(quads(each, feat)):
            part = unit[h * each + row : h * each + row + QUAD, lane : lane + LANES]
            sent_out[:, h, g] = jnp.broadcast_to(part[None], (peers, QUAD, LANES)).astype(BF16)

    def body(at, acc):
        z = dot(x, tea_w[:, at], ((1,), (0,)))
        k = jnp.exp(z * (inv[:, at] * (1.0 / TEACHER_TEMP)))
        kernel_out[:, at] = k
        c = 1.0 / jnp.sum(k, axis=0, keepdims=True)
        return acc + fold(k * c)

    acc = over_chunks(tea_w.shape[1], body, jnp.zeros((rows, LANES), F32))
    held = len(quads(each, feat))
    tiles = lay_out([to_row(acc)], QUAD, (groups - held) * LANES)
    for g in range(groups - held):
        tile = tiles[:, g * LANES : (g + 1) * LANES]
        for h in range(2):
            sent_out[:, h, held + g] = jnp.broadcast_to(tile[None], (peers, QUAD, LANES)).astype(BF16)


def spots(hot, sums, start, stop):
    return dot(hot[:, start:stop], sums, ((0,), (1,)))


def halves(hot, sums, at, keep_out, give_out):
    half = keep_out.shape[0]
    odd = odd_half() == 1
    lanes = slice(at, at + sums.shape[0])
    for start, stop in blocks(half):
        low, high = spots(hot, sums, start, stop), spots(hot, sums, half + start, half + stop)
        keep_out[start:stop, lanes] = jnp.where(odd, high, low)
        give_out[start:stop, lanes] = jnp.where(odd, low, high).astype(BF16)


def row_weights(mine, other, hot, own_out, weight_out, protos):
    devices = lax.axis_size(AXES)
    half = mine.shape[0]
    each = half // devices
    per_image = each * protos
    step = min(256, half)
    count, images = [], []
    block = iota((step, step), 0) // per_image
    same = (block == iota((step, step), 1) // per_image).astype(BF16)
    for c in range(0, half, step):
        flags = [slot_flags(ref[c : c + step, :LANES]).astype(F32) for ref in (mine, other)]
        held = dot(same, (flags[0] + flags[1]).astype(BF16), ((1,), (0,)))
        for h in range(2):
            count.append(dot(hot[:, h * half + c : h * half + c + step], held.astype(BF16), ((1,), (0,))))
        first = (iota(held.shape, 0) % per_image == 0) & (held > 0.5)
        images.append(jnp.sum(first.astype(F32), axis=0, keepdims=True))
    weight_out[...] = 1.0 / (jnp.maximum(add_all(count), 1.0) * add_all(images))

    own = own_out.shape[0]
    me = lax.axis_index("img") * protos + lax.axis_index("proto")
    q = iota((own, 2 * half), 0)
    spot = q // each * half + me * each + q % each
    mark = (iota((own, 2 * half), 1) == spot).astype(BF16)
    own_out[...] = dot(mark, hot[...], ((1,), (1,)))


def slots_of(got, feat):
    devices, each, _ = got.shape
    parts = got[:, :, :feat].astype(F32).reshape(devices // 2, 2, each, feat)
    return jnp.sum(parts, axis=0).reshape(2 * each, feat)


def sweep_kernel(got, kernel, sent_out, *, held):
    rows, columns = kernel.shape
    sums = [jnp.sum(got[:, g].astype(F32), axis=0) for g in range(held, got.shape[1])]
    high, low = read_out(jnp.concatenate(sums, axis=1), rows, 2)
    total = high + low
    wide = spread(1.0 / total, chunks(columns)[0].stop)

    def body(at, acc):
        k = kernel[:, at]
        c = 1.0 / jnp.sum(k * wide, axis=0, keepdims=True)
        return acc + fold(k * c)

    acc = over_chunks(columns, body, jnp.zeros((rows, LANES), F32))
    tiles = jnp.concatenate(tiles_of(to_row(acc)), axis=0)
    sent_out[...] = jnp.broadcast_to(tiles[None], sent_out.shape)


def student_kernel(
    got,
    kernel,
    mine,
    other,
    hot,
    stu_w,
    inv_out,
    logits_out,
    scaled_out,
    xt_out,
    sums_out,
    keep_out,
    give_out,
    pulls,
    pushes,
):
    rows, columns = logits_out.shape
    feat = stu_w.shape[0]
    half = keep_out.shape[0]
    each = half // lax.axis_size(AXES)

    def reader(ref):
        def read(start, stop):
            peers = slice(start // each, stop // each)
            parts = [ref[peers, g].astype(F32) for g in range(len(quads(each, feat)))]
            deep = each // QUAD
            lanes = [jnp.concatenate(parts[g : g + deep], axis=1) for g in range(0, len(parts), deep)]
            return jnp.concatenate([part.reshape(stop - start, LANES) for part in lanes], axis=1).astype(BF16)

        return read

    x = pack_rows(hot, reader(mine), reader(other), half)
    xt = x.astype(F32).T
    xt_out[...] = xt.astype(BF16)
    (total,) = read_out(jnp.sum(got[...], axis=0), rows, 1)
    wide = spread(1.0 / total, chunks(columns)[0].stop)

    def student(at, acc):
        w = stu_w[:, at]
        n = inverse_norms(w)
        inv_out[:, at] = n
        l = dot(x, w, ((1,), (0,))) * (n * (1.0 / STUDENT_TEMP))
        logits_out[:, at] = l
        p = jnp.exp(l)
        pulls[:, at] = (p * n).astype(BF16)
        return acc + fold(p)

    def sweep(at, acc):
        k = kernel[:, at]
        kc = k * (1.0 / jnp.sum(k * wide, axis=0, keepdims=True))
        scaled_out[:, at] = kc
        pushes[:, at] = (kc * inv_out[:, at]).astype(BF16)
        return acc + fold(kc)

    zero = jnp.zeros((rows, LANES), F32)
    part = over_chunks(columns, student, zero)
    pull = dot(stu_w[...], pulls[...], ((1,), (1,)))
    total = over_chunks(columns, sweep, zero)
    push = dot(pushes[...], stu_w[...], ((1,), (1,))).T
    halves(hot, pull.astype(BF16), 0, keep_out, give_out)
    halves(hot, push.astype(BF16), feat, keep_out, give_out)
    cross = jnp.sum(push * xt, axis=0, keepdims=True) * (1.0 / STUDENT_TEMP)
    sums_out[...] = lay_out([to_row(part), to_row(total), cross], *sums_out.shape)


def prepare_kernel(
    scaled, logits, inv, mine, other, hot, pull_out, push_out, own_out, weight_out, *, scale, protos
):
    rows, columns = scaled.shape
    row_weights(mine, other, hot, own_out, weight_out, protos)
    factor = spread(weight_out[...] * (rows / STUDENT_TEMP), chunks(columns)[0].stop)

    def body(at, _):
        n = inv[:, at] * scale
        pull_out[:, at] = factor * jnp.exp(logits[:, at]) * n
        push_out[:, at] = factor * scaled[:, at] * n
        return 0

    over_chunks(columns, body, 0)


def fill_kernel(keep, give, sums, sent_out):
    devices, each, wide = sent_out.shape
    both = keep.shape[1]
    sent_out[:, :, :both] = (keep[...] + give[...].astype(F32)).reshape(devices, each, both).astype(BF16)
    sent_out[:, :, both:] = jnp.broadcast_to(sums[...][None], (devices, each, wide - both)).astype(BF16)


def final_kernel(
    got,
    pull,
    push,
    logits,
    inv,
    stu_w,
    xt,
    weight,
    own,
    unit,
    norm,
    out_hbm,
    rows_hbm,
    loss_hbm,
    out,
    rows_out,
    loss_out,
    sems,
):
    rows, columns = pull.shape
    feat = xt.shape[0]
    partition, total, cross = read_pairs(got, 2 * feat, rows, 3)
    parts = chunks(columns, 256)
    raise_by, lower_by = 1.0 / partition, 1.0 / total
    grow, shrink = spread(raise_by, parts[0].stop), spread(lower_by, parts[0].stop)
    copies = []

    def send(source, target):
        copies.append(pltpu.make_async_copy(source, target, sems.at[len(copies)]))
        copies[-1].start()

    def gradient(at):
        g = grow * pull[:, at] - shrink * push[:, at]
        along = jnp.sum(g * logits[:, at], axis=0, keepdims=True) * (inv[:, at] * STUDENT_TEMP)
        return g.astype(BF16), along

    ready = gradient(parts[0])
    for at, following in zip(parts, parts[1:] + [None]):
        g, along = ready
        direct = dot(xt[...], g, ((1,), (0,)))
        if following is not None:
            ready = gradient(following)
        out[:, at] = direct - stu_w[:, at].astype(F32) * along
        send(out.at[:, at], out_hbm.at[:, at])
    share = weight[...]
    loss = jnp.sum(share * (jnp.log(partition) - cross * lower_by), axis=0, keepdims=True)
    loss_out[...] = loss[:, :1]
    send(loss_out, loss_hbm)
    factors = jnp.concatenate([raise_by, lower_by], axis=1) * spread(share * (rows / STUDENT_TEMP), 2 * LANES)
    held = dot(own[...], factors, ((1,), (0,)), lax.Precision.HIGHEST)
    sums = slots_of(got, 2 * feat)
    full = sums[:, :feat] * held[:, :1] - sums[:, feat:] * held[:, LANES : LANES + 1]
    u = unit[...]
    rows_out[...] = (full - u * jnp.sum(u * full, axis=1, keepdims=True)) / norm[:, :1]
    send(rows_out, rows_hbm)
    for copy in copies:
        copy.wait()


def shards(student_feats, teacher_feats, student_weight, teacher_weight, patch_masks):
    devices = lax.axis_size(AXES)
    protos = lax.axis_size("proto")
    images, patches, feat = student_feats.shape
    assert images == 1 and protos % 2 == 0
    columns = student_weight.shape[1]
    own = patches // 2 // protos
    each = own // 2
    half = each * devices
    rows = 2 * half * 5 // 16
    tiles = -(-rows // LANES)
    extra = lambda parts: LANES * -(-parts * rows // (each * LANES))
    held = len(quads(each, feat))
    big = rows * columns
    exchange = functools.partial(lax.all_to_all, axis_name=AXES, split_axis=0, concat_axis=0)
    swap = functools.partial(lax.ppermute, axis_name="proto", perm=[(p, p ^ 1) for p in range(protos)])
    matrix = pltpu.VMEM((rows, columns), F32)
    column = pltpu.VMEM((rows, LANES), F32)
    line = pltpu.VMEM((1, columns), F32)

    flags = pltpu.VMEM(patch_masks.shape, patch_masks.dtype)
    feats = pltpu.VMEM(student_feats.shape, BF16)
    sent, flags, feats = call(
        teacher_kernel,
        (pltpu.VMEM((devices // 2, own, feat), BF16), flags, feats),
        far(patch_masks),
        far(student_feats),
        far(teacher_feats),
        specs=[HBM] * 3,
        scratch=[feats, pltpu.SemaphoreType.DMA((3,))],
    )
    mine = exchange(sent.reshape(devices, each, feat)).reshape(half, feat)
    mine, teacher_weight = lax.optimization_barrier((mine, teacher_weight))
    other = near(swap(mine))
    mine = near(mine)
    tea_w, tea_inv, unit, norm = call(
        norms_kernel,
        (
            pltpu.VMEM(teacher_weight.shape, BF16),
            line,
            pltpu.VMEM((own, feat), F32),
            pltpu.VMEM((own, LANES), F32),
        ),
        flags,
        feats,
        far(teacher_weight),
        flops=2 * feat * columns,
        moved=4 * feat * columns,
        specs=[VMEM, VMEM, HBM],
        scratch=[pltpu.SemaphoreType.DMA((len(chunks(columns)),))],
    )
    kernel, sent, hot = call(
        first_kernel,
        (
            matrix,
            pltpu.VMEM((devices // 2, 2, held + -(-2 * rows // (QUAD * LANES)), QUAD, LANES), BF16),
            pltpu.VMEM((rows, 2 * half), BF16),
        ),
        mine,
        other,
        tea_w,
        tea_inv,
        unit,
        flops=2 * big * feat,
        moved=4 * big,
        exps=big,
    )
    stu_mine = exchange(sent.reshape(devices, *sent.shape[2:]))
    stu_other = near(swap(stu_mine))
    stu_mine = near(stu_mine)
    (sent,) = call(
        functools.partial(sweep_kernel, held=held),
        (pltpu.VMEM((devices, tiles, LANES), F32),),
        stu_mine,
        kernel,
        flops=4 * big,
        moved=4 * big,
    )
    got = near(exchange(sent))
    stu_inv, logits, scaled, xt, sums, keep, give = call(
        student_kernel,
        (
            line,
            matrix,
            matrix,
            pltpu.VMEM((feat, rows), BF16),
            pltpu.VMEM((each, extra(6)), F32),
            pltpu.VMEM((half, 2 * feat), F32),
            pltpu.VMEM((half, 2 * feat), BF16),
        ),
        got,
        kernel,
        stu_mine,
        stu_other,
        hot,
        student_weight,
        flops=6 * big * feat,
        moved=12 * big,
        exps=big,
        scratch=[pltpu.VMEM((rows, columns), BF16), pltpu.VMEM((rows, columns), BF16)],
        limit=22 + half // 112,
    )
    give = near(swap(give))
    pull, push, own_hot, weight = call(
        functools.partial(prepare_kernel, scale=columns * devices * GRAD_SCALE, protos=protos),
        (matrix, matrix, pltpu.VMEM((own, rows), F32), column),
        scaled,
        logits,
        stu_inv,
        mine,
        other,
        hot,
        flops=4 * big,
        moved=16 * big,
        exps=big,
    )
    keep, pull, push, own_hot, weight = lax.optimization_barrier((keep, pull, push, own_hot, weight))
    (sent,) = call(fill_kernel, (pltpu.VMEM((devices, each, 2 * feat + extra(6)), BF16),), keep, give, sums)
    got = near(exchange(sent))
    grad_weight, grad_rows, loss = call(
        final_kernel,
        (
            jax.ShapeDtypeStruct((feat, columns), F32),
            jax.ShapeDtypeStruct((own, feat), F32),
            jax.ShapeDtypeStruct((1, 1), F32),
        ),
        got,
        pull,
        push,
        logits,
        stu_inv,
        student_weight,
        xt,
        weight,
        own_hot,
        unit,
        norm,
        flops=2 * big * feat,
        moved=8 * feat * columns,
        out_specs=(HBM, HBM, HBM),
        scratch=[
            pltpu.VMEM((feat, columns), F32),
            pltpu.VMEM((own, feat), F32),
            pltpu.VMEM((1, 1), F32),
            pltpu.SemaphoreType.DMA((len(chunks(columns, 256)) + 2,)),
        ],
    )
    return loss.reshape(()), grad_weight, grad_rows


def solution(mesh):
    placed = (
        P("img", None, None),
        P("img", None, None),
        P(None, AXES),
        P(None, AXES),
        P("img", None),
    )
    return jax.shard_map(
        shards,
        mesh=mesh,
        in_specs=placed,
        out_specs=(P(), P(None, AXES), P(AXES, None)),
        check_vma=False,
    )
```

```python
import functools

import jax
import jax.numpy as jnp
from jax import lax
from jax.experimental import pallas as pl
from jax.experimental.pallas import tpu as pltpu
from jax.sharding import PartitionSpec as P

ITERS = 3
TEACHER_TEMP = 0.07
STUDENT_TEMP = 0.1
NORM_EPS = 1e-06
GRAD_SCALE = 1.0 / 128.0
EMPTY = 2.0
LANES = 128
QUAD = 4
F32 = jnp.float32
BF16 = jnp.bfloat16
AXES = ("img", "proto")

VMEM = pl.BlockSpec(memory_space=pltpu.VMEM)
HBM = pl.BlockSpec(memory_space=pltpu.HBM)


def call(body, outs, *args, flops=0, moved=0, exps=0, limit=24, specs=None, out_specs=None, scratch=()):
    return pl.pallas_call(
        body,
        out_shape=outs,
        in_specs=specs or [VMEM] * len(args),
        out_specs=out_specs or tuple(VMEM for _ in outs),
        scratch_shapes=scratch,
        compiler_params=pltpu.CompilerParams(vmem_limit_bytes=limit * 1024 * 1024),
        cost_estimate=pl.CostEstimate(flops=flops, bytes_accessed=moved, transcendentals=exps),
    )(*args)


def near(x):
    return pltpu.with_memory_space_constraint(x, pltpu.VMEM)


def far(x):
    return pltpu.with_memory_space_constraint(x, pltpu.HBM)


def dot(a, b, dims, precision=None):
    return lax.dot_general(a, b, (dims, ((), ())), precision=precision, preferred_element_type=F32)


def iota(shape, dim):
    return lax.broadcasted_iota(jnp.int32, shape, dim)


def add_all(parts):
    return functools.reduce(jnp.add, parts)


def widen(row):
    spare = -row.shape[1] % LANES
    return jnp.concatenate([row, jnp.zeros((1, spare), F32)], axis=1) if spare else row


def tiles_of(row):
    row = widen(row)
    return [row[:, i : i + LANES] for i in range(0, row.shape[1], LANES)]


def to_row(part):
    rows = part.shape[0]
    spare = -rows % LANES
    if spare:
        part = jnp.concatenate([part, jnp.zeros((spare, LANES), F32)], axis=0)
    return jnp.sum(part.T, axis=0, keepdims=True)[:, :rows]


def split(vector):
    high = vector.astype(BF16).astype(F32)
    return [high, vector - high]


def lay_out(vectors, lines, wide):
    tiles = tiles_of(jnp.concatenate(vectors, axis=1))
    tiles += [jnp.zeros((1, LANES), F32)] * (lines * wide // LANES - len(tiles))
    groups = [jnp.concatenate(tiles[g : g + lines], axis=0) for g in range(0, len(tiles), lines)]
    return jnp.concatenate(groups, axis=1)


def read_out(sums, rows, count):
    lines = sums.shape[0]
    turned = [sums[:, g : g + LANES].T for g in range(0, sums.shape[1], LANES)]

    def column(at, stop):
        parts = []
        while at < stop:
            line, lane = divmod(at, LANES)
            until = min(LANES, lane + stop - at)
            parts.append(turned[line // lines][lane:until, line % lines : line % lines + 1])
            at += until - lane
        return jnp.concatenate(parts, axis=0)

    return [jnp.broadcast_to(column(v * rows, (v + 1) * rows), (rows, LANES)) for v in range(count)]


def fold(x):
    return add_all([x[:, i : i + LANES] for i in range(0, x.shape[1], LANES)])


def spread(col, width):
    return jnp.concatenate([col] * (width // LANES), axis=1)


def chunks(columns, step=512):
    step = min(step, columns)
    return [slice(at, at + step) for at in range(0, columns, step)]


def over_chunks(columns, body, start):
    for at in chunks(columns):
        start = body(at, start)
    return start


def start_load(source, target, sems, first=0):
    copies = []
    for i, at in enumerate(chunks(target.shape[1])):
        place = source.at[:, first + at.start : first + at.stop]
        copies.append(pltpu.make_async_copy(place, target.at[:, at], sems.at[i]))
    for copy in copies:
        copy.start()
    return copies


def inverse_norms(w):
    w = w.astype(F32)
    return 1.0 / jnp.sqrt(jnp.sum(w * w, axis=0, keepdims=True) + NORM_EPS)


def odd_half():
    return lax.rem(lax.axis_index("proto"), 2)


def own_slots(mask_ref, feats_ref, own):
    patches = mask_ref.shape[1]
    slot = iota((own, patches), 0) + lax.axis_index("proto") * own
    mask = jnp.broadcast_to(mask_ref[...].astype(F32), (own, patches))
    upto = (iota((patches, patches), 0) <= iota((patches, patches), 1)).astype(BF16)
    rank = dot(mask.astype(BF16), upto, ((1,), (0,)))
    pick = jnp.where((rank == slot.astype(F32) + 1.0) & (mask > 0.5), 1.0, 0.0).astype(BF16)
    valid = slot[:, :1].astype(F32) < rank[:, patches - 1 :]
    rows = dot(pick, feats_ref[0], ((1,), (0,)))
    norm = jnp.sqrt(jnp.sum(rows * rows, axis=1, keepdims=True) + NORM_EPS)
    return (rows / norm).astype(BF16).astype(F32), norm, valid


def teacher_kernel(mask_hbm, stu_hbm, tea_hbm, w_hbm, sent_out, mask_out, stu_out, early_w, tea_ref, sems, w_sems):
    pairs = ((mask_hbm, mask_out), (tea_hbm, tea_ref), (stu_hbm, stu_out))
    copies = [pltpu.make_async_copy(*pair, sems.at[i]) for i, pair in enumerate(pairs)]
    for copy in copies:
        copy.start()
    loads = start_load(w_hbm, early_w, w_sems)
    for copy in copies[:2]:
        copy.wait()
    unit, _, valid = own_slots(mask_out, tea_ref, sent_out.shape[1])
    sent_out[...] = jnp.broadcast_to(jnp.where(valid, unit, EMPTY).astype(BF16)[None], sent_out.shape)
    for copy in copies[2:] + loads:
        copy.wait()


def norms_kernel(mask_ref, stu_ref, early_w, w_hbm, late_w, inv_out, unit_out, norm_out, sems):
    early = early_w.shape[1]
    copies = start_load(w_hbm, late_w, sems, early)
    unit, norm, _ = own_slots(mask_ref, stu_ref, unit_out.shape[0])
    unit_out[...] = unit
    norm_out[...] = jnp.broadcast_to(norm, norm_out.shape)
    for at in chunks(early):
        inv_out[:, at] = inverse_norms(early_w[:, at])
    for copy, at in zip(copies, chunks(late_w.shape[1])):
        copy.wait()
        inv_out[:, early + at.start : early + at.stop] = inverse_norms(late_w[:, at])


def in_order(mine, other, h):
    return jnp.where(odd_half() == h, mine, other)


def slot_flags(data):
    return jnp.where(data[:, :LANES].astype(F32) < 1.5, 1.0, 0.0).astype(BF16)


def packing(flags, hot_out):
    rows = hot_out.shape[0]
    half = flags[0].shape[0]
    step = min(256, half)
    before = jnp.zeros((1, 1), F32)
    upto = (iota((step, step), 0) <= iota((step, step), 1)).astype(BF16)
    same = (iota((step, step), 0) == iota((step, step), 1)).astype(BF16)
    row = iota((rows, step), 0).astype(F32) + 1.0
    for h in range(2):
        for c in range(0, half, step):
            part = flags[h][c : c + step]
            place = before + dot(part, upto, ((0,), (0,)))[:1]
            held = dot(part, same, ((0,), (0,)))[:1]
            hot = jnp.where((row == place) & (held > 0.5), 1.0, 0.0).astype(BF16)
            hot_out[:, h * half + c : h * half + c + step] = hot
            before = place[:, step - 1 :]


def blocks(half):
    step = min(256, half)
    return [(at, at + step) for at in range(0, half, step)]


def pack_rows(hot, read_mine, read_other, half):
    parts = []
    for start, stop in blocks(half):
        mine, other = read_mine(start, stop), read_other(start, stop)
        for h in range(2):
            parts.append(dot(hot[:, h * half + start : h * half + stop], in_order(mine, other, h), ((1,), (0,))))
    return add_all(parts).astype(BF16)


def quads(each, feat):
    return [(row, lane) for lane in range(0, feat, LANES) for row in range(0, each, QUAD)]


def first_kernel(mine, other, early_w, late_w, inv, unit, kernel_out, sent_out, hot_out):
    rows = kernel_out.shape[0]
    peers, _, groups, _, _ = sent_out.shape
    feat = late_w.shape[0]
    packing([slot_flags(in_order(mine[:, :LANES], other[:, :LANES], h)) for h in range(2)], hot_out)
    x = pack_rows(hot_out, lambda a, b: mine[a:b], lambda a, b: other[a:b], mine.shape[0])
    each = unit.shape[0] // 2
    for h in range(2):
        for g, (row, lane) in enumerate(quads(each, feat)):
            part = unit[h * each + row : h * each + row + QUAD, lane : lane + LANES]
            sent_out[:, h, g] = jnp.broadcast_to(part[None], (peers, QUAD, LANES)).astype(BF16)

    acc = jnp.zeros((rows, LANES), F32)
    for w, first in ((early_w, 0), (late_w, early_w.shape[1])):
        for part in chunks(w.shape[1]):
            at = slice(first + part.start, first + part.stop)
            z = dot(x, w[:, part], ((1,), (0,)))
            k = jnp.exp(z * (inv[:, at] * (1.0 / TEACHER_TEMP)))
            kernel_out[:, at] = k
            c = 1.0 / jnp.sum(k, axis=0, keepdims=True)
            acc = acc + fold(k * c)
    held = len(quads(each, feat))
    tiles = lay_out(split(to_row(acc)), QUAD, (groups - held) * LANES)
    for g in range(groups - held):
        tile = tiles[:, g * LANES : (g + 1) * LANES]
        for h in range(2):
            sent_out[:, h, held + g] = jnp.broadcast_to(tile[None], (peers, QUAD, LANES)).astype(BF16)


def spots(hot, sums, start, stop):
    return dot(hot[:, start:stop], sums, ((0,), (1,)))


def halves(hot, sums, at, keep_out, give_out):
    half = keep_out.shape[0]
    odd = odd_half() == 1
    lanes = slice(at, at + sums.shape[0])
    for start, stop in blocks(half):
        low, high = spots(hot, sums, start, stop), spots(hot, sums, half + start, half + stop)
        keep_out[start:stop, lanes] = jnp.where(odd, high, low)
        give_out[start:stop, lanes] = jnp.where(odd, low, high).astype(BF16)


def row_weights(mine, other, hot, own_out, weight_out, protos):
    devices = lax.axis_size(AXES)
    half = mine.shape[0]
    each = half // devices
    per_image = each * protos
    step = min(256, half)
    count, images = [], []
    block = iota((step, step), 0) // per_image
    same = (block == iota((step, step), 1) // per_image).astype(BF16)
    for c in range(0, half, step):
        flags = [slot_flags(ref[c : c + step, :LANES]).astype(F32) for ref in (mine, other)]
        held = dot(same, (flags[0] + flags[1]).astype(BF16), ((1,), (0,)))
        for h in range(2):
            count.append(dot(hot[:, h * half + c : h * half + c + step], held.astype(BF16), ((1,), (0,))))
        first = (iota(held.shape, 0) % per_image == 0) & (held > 0.5)
        images.append(jnp.sum(first.astype(F32), axis=0, keepdims=True))
    weight_out[...] = 1.0 / (jnp.maximum(add_all(count), 1.0) * add_all(images))

    own = own_out.shape[0]
    me = lax.axis_index("img") * protos + lax.axis_index("proto")
    q = iota((own, 2 * half), 0)
    spot = q // each * half + me * each + q % each
    mark = (iota((own, 2 * half), 1) == spot).astype(BF16)
    own_out[...] = dot(mark, hot[...], ((1,), (1,)))


def sweep_kernel(got, kernel, sent_out, *, held):
    rows, columns = kernel.shape
    sums = [jnp.sum(got[:, g].astype(F32), axis=0) for g in range(held, got.shape[1])]
    high, low = read_out(jnp.concatenate(sums, axis=1), rows, 2)
    total = high + low
    wide = spread(1.0 / total, chunks(columns)[0].stop)

    def body(at, acc):
        k = kernel[:, at]
        c = 1.0 / jnp.sum(k * wide, axis=0, keepdims=True)
        return acc + fold(k * c)

    acc = over_chunks(columns, body, jnp.zeros((rows, LANES), F32))
    tiles = jnp.concatenate(tiles_of(to_row(acc)), axis=0)
    sent_out[...] = jnp.broadcast_to(tiles[None], sent_out.shape)


def student_kernel(
    got,
    kernel,
    mine,
    other,
    hot,
    stu_w,
    inv_out,
    logits_out,
    scaled_out,
    xt_out,
    sums_out,
    keep_out,
    give_out,
    pulls,
    pushes,
):
    rows, columns = logits_out.shape
    feat = stu_w.shape[0]
    half = keep_out.shape[0]
    each = half // lax.axis_size(AXES)

    def reader(ref):
        def read(start, stop):
            peers = slice(start // each, stop // each)
            parts = [ref[peers, g].astype(F32) for g in range(len(quads(each, feat)))]
            deep = each // QUAD
            lanes = [jnp.concatenate(parts[g : g + deep], axis=1) for g in range(0, len(parts), deep)]
            return jnp.concatenate([part.reshape(stop - start, LANES) for part in lanes], axis=1).astype(BF16)

        return read

    x = pack_rows(hot, reader(mine), reader(other), half)
    xt = x.astype(F32).T
    xt_out[...] = xt.astype(BF16)
    (total,) = read_out(jnp.sum(got[...], axis=0), rows, 1)
    wide = spread(1.0 / total, chunks(columns)[0].stop)

    def student(at, acc):
        w = stu_w[:, at]
        n = inverse_norms(w)
        inv_out[:, at] = n
        l = dot(x, w, ((1,), (0,))) * (n * (1.0 / STUDENT_TEMP))
        logits_out[:, at] = l
        p = jnp.exp(l)
        pulls[:, at] = (p * n).astype(BF16)
        return acc + fold(p)

    def sweep(at, acc):
        k = kernel[:, at]
        kc = k * (1.0 / jnp.sum(k * wide, axis=0, keepdims=True))
        scaled_out[:, at] = kc
        pushes[:, at] = (kc * inv_out[:, at]).astype(BF16)
        return acc + fold(kc)

    zero = jnp.zeros((rows, LANES), F32)
    part = over_chunks(columns, student, zero)
    pull = dot(stu_w[...], pulls[...], ((1,), (1,)))
    total = over_chunks(columns, sweep, zero)
    push = dot(pushes[...], stu_w[...], ((1,), (1,))).T
    halves(hot, pull.astype(BF16), 0, keep_out, give_out)
    halves(hot, push.astype(BF16), feat, keep_out, give_out)
    cross = jnp.sum(push * xt, axis=0, keepdims=True) * (1.0 / STUDENT_TEMP)
    sums_out[...] = lay_out([to_row(part), to_row(total), cross], *sums_out.shape)


def prepare_kernel(
    scaled, logits, inv, mine, other, hot, pull_out, push_out, own_out, weight_out, *, scale, protos
):
    rows, columns = scaled.shape
    row_weights(mine, other, hot, own_out, weight_out, protos)
    factor = spread(weight_out[...] * (rows / STUDENT_TEMP), chunks(columns)[0].stop)

    def body(at, _):
        n = inv[:, at] * scale
        pull_out[:, at] = factor * jnp.exp(logits[:, at]) * n
        push_out[:, at] = factor * scaled[:, at] * n
        return 0

    over_chunks(columns, body, 0)


def fill_kernel(keep, give, sums, sent_out):
    devices, groups, _, _ = sent_out.shape
    half, both = keep.shape
    each = half // devices
    pair = keep[...] + give[...].astype(F32)
    places = quads(each, both)
    for g, (row, lane) in enumerate(places):
        part = pair[:, lane : lane + LANES].reshape(devices, each, LANES)
        sent_out[:, g] = part[:, row : row + QUAD].astype(BF16)
    for g in range(len(places), groups):
        at = (g - len(places)) * LANES
        sent_out[:, g] = jnp.broadcast_to(sums[:, at : at + LANES][None], (devices, QUAD, LANES)).astype(BF16)


def slots_of(got, each, both):
    sums = [jnp.sum(got[:, :, g].astype(F32), axis=0) for g in range(len(quads(each, both)))]
    deep = each // QUAD
    lanes = [
        jnp.concatenate([sums[g + i][h] for h in range(2) for i in range(deep)], axis=0) for g in range(0, len(sums), deep)
    ]
    return jnp.concatenate(lanes, axis=1)


def final_kernel(
    got,
    pull,
    push,
    logits,
    inv,
    stu_w,
    xt,
    weight,
    own,
    unit,
    norm,
    out_hbm,
    rows_hbm,
    loss_hbm,
    out,
    rows_out,
    loss_out,
    sems,
):
    rows, columns = pull.shape
    feat = xt.shape[0]
    each = unit.shape[0] // 2
    held = len(quads(each, 2 * feat))
    sums = [jnp.sum(got[:, :, g].astype(F32), axis=(0, 1)) for g in range(held, got.shape[2])]
    partition, total, cross = read_out(jnp.concatenate(sums, axis=1), rows, 3)
    parts = chunks(columns, 256)
    raise_by, lower_by = 1.0 / partition, 1.0 / total
    grow, shrink = spread(raise_by, parts[0].stop), spread(lower_by, parts[0].stop)
    copies = []

    def send(source, target):
        copies.append(pltpu.make_async_copy(source, target, sems.at[len(copies)]))
        copies[-1].start()

    def gradient(at):
        g = grow * pull[:, at] - shrink * push[:, at]
        along = jnp.sum(g * logits[:, at], axis=0, keepdims=True) * (inv[:, at] * STUDENT_TEMP)
        return g.astype(BF16), along

    ready = gradient(parts[0])
    for at, following in zip(parts, parts[1:] + [None]):
        g, along = ready
        direct = dot(xt[...], g, ((1,), (0,)))
        if following is not None:
            ready = gradient(following)
        out[:, at] = direct - stu_w[:, at].astype(F32) * along
        send(out.at[:, at], out_hbm.at[:, at])
    share = weight[...]
    loss = jnp.sum(share * (jnp.log(partition) - cross * lower_by), axis=0, keepdims=True)
    loss_out[...] = loss[:, :1]
    send(loss_out, loss_hbm)
    factors = jnp.concatenate([raise_by, lower_by], axis=1) * spread(share * (rows / STUDENT_TEMP), 2 * LANES)
    scale = dot(own[...], factors, ((1,), (0,)), lax.Precision.HIGHEST)
    sums = slots_of(got, each, 2 * feat)
    full = sums[:, :feat] * scale[:, :1] - sums[:, feat:] * scale[:, LANES : LANES + 1]
    u = unit[...]
    rows_out[...] = (full - u * jnp.sum(u * full, axis=1, keepdims=True)) / norm[:, :1]
    send(rows_out, rows_hbm)
    for copy in copies:
        copy.wait()


def shards(student_feats, teacher_feats, student_weight, teacher_weight, patch_masks):
    devices = lax.axis_size(AXES)
    protos = lax.axis_size("proto")
    images, patches, feat = student_feats.shape
    assert images == 1 and protos % 2 == 0
    columns = student_weight.shape[1]
    own = patches // 2 // protos
    each = own // 2
    half = each * devices
    rows = 2 * half * 5 // 16
    tiles = -(-rows // LANES)
    spare = lambda parts: -(-parts * rows // (QUAD * LANES))
    held = len(quads(each, feat))
    big = rows * columns
    exchange = functools.partial(lax.all_to_all, axis_name=AXES, split_axis=0, concat_axis=0)
    swap = functools.partial(lax.ppermute, axis_name="proto", perm=[(p, p ^ 1) for p in range(protos)])
    matrix = pltpu.VMEM((rows, columns), F32)
    column = pltpu.VMEM((rows, LANES), F32)
    line = pltpu.VMEM((1, columns), F32)

    flags = pltpu.VMEM(patch_masks.shape, patch_masks.dtype)
    feats = pltpu.VMEM(student_feats.shape, BF16)
    early = columns * 3 // 8 // LANES * LANES
    early_w, late_w = pltpu.VMEM((feat, early), BF16), pltpu.VMEM((feat, columns - early), BF16)
    sent, flags, feats, early_w = call(
        teacher_kernel,
        (pltpu.VMEM((devices // 2, own, feat), BF16), flags, feats, early_w),
        far(patch_masks),
        far(student_feats),
        far(teacher_feats),
        far(teacher_weight),
        specs=[HBM] * 4,
        scratch=[feats, pltpu.SemaphoreType.DMA((3,)), pltpu.SemaphoreType.DMA((len(chunks(early)),))],
    )
    mine = exchange(sent.reshape(devices, each, feat)).reshape(half, feat)
    mine, teacher_weight = lax.optimization_barrier((mine, teacher_weight))
    other = near(swap(mine))
    mine = near(mine)
    late_w, tea_inv, unit, norm = call(
        norms_kernel,
        (
            late_w,
            line,
            pltpu.VMEM((own, feat), F32),
            pltpu.VMEM((own, LANES), F32),
        ),
        flags,
        feats,
        early_w,
        far(teacher_weight),
        flops=2 * feat * columns,
        moved=4 * feat * columns,
        specs=[VMEM, VMEM, VMEM, HBM],
        scratch=[pltpu.SemaphoreType.DMA((len(chunks(columns - early)),))],
    )
    kernel, sent, hot = call(
        first_kernel,
        (
            matrix,
            pltpu.VMEM((devices // 2, 2, held + spare(2), QUAD, LANES), BF16),
            pltpu.VMEM((rows, 2 * half), BF16),
        ),
        mine,
        other,
        early_w,
        late_w,
        tea_inv,
        unit,
        flops=2 * big * feat,
        moved=4 * big,
        exps=big,
    )
    stu_mine = exchange(sent.reshape(devices, *sent.shape[2:]))
    stu_other = near(swap(stu_mine))
    stu_mine = near(stu_mine)
    (sent,) = call(
        functools.partial(sweep_kernel, held=held),
        (pltpu.VMEM((devices, tiles, LANES), F32),),
        stu_mine,
        kernel,
        flops=4 * big,
        moved=4 * big,
    )
    got = near(exchange(sent))
    stu_inv, logits, scaled, xt, sums, keep, give = call(
        student_kernel,
        (
            line,
            matrix,
            matrix,
            pltpu.VMEM((feat, rows), BF16),
            pltpu.VMEM((QUAD, spare(3) * LANES), F32),
            pltpu.VMEM((half, 2 * feat), F32),
            pltpu.VMEM((half, 2 * feat), BF16),
        ),
        got,
        kernel,
        stu_mine,
        stu_other,
        hot,
        student_weight,
        flops=6 * big * feat,
        moved=12 * big,
        exps=big,
        scratch=[pltpu.VMEM((rows, columns), BF16), pltpu.VMEM((rows, columns), BF16)],
        limit=22 + half // 112,
    )
    give = near(swap(give))
    pull, push, own_hot, weight = call(
        functools.partial(prepare_kernel, scale=columns * devices * GRAD_SCALE, protos=protos),
        (matrix, matrix, pltpu.VMEM((own, rows), F32), column),
        scaled,
        logits,
        stu_inv,
        mine,
        other,
        hot,
        flops=4 * big,
        moved=16 * big,
        exps=big,
    )
    keep, pull, push, own_hot, weight = lax.optimization_barrier((keep, pull, push, own_hot, weight))
    payload = pltpu.VMEM((devices, 2 * held + spare(3), QUAD, LANES), BF16)
    (sent,) = call(fill_kernel, (payload,), keep, give, sums)
    got = exchange(sent)
    got = near(got.reshape(devices // 2, 2, *got.shape[1:]))
    grad_weight, grad_rows, loss = call(
        final_kernel,
        (
            jax.ShapeDtypeStruct((feat, columns), F32),
            jax.ShapeDtypeStruct((own, feat), F32),
            jax.ShapeDtypeStruct((1, 1), F32),
        ),
        got,
        pull,
        push,
        logits,
        stu_inv,
        student_weight,
        xt,
        weight,
        own_hot,
        unit,
        norm,
        flops=2 * big * feat,
        moved=8 * feat * columns,
        out_specs=(HBM, HBM, HBM),
        scratch=[
            pltpu.VMEM((feat, columns), F32),
            pltpu.VMEM((own, feat), F32),
            pltpu.VMEM((1, 1), F32),
            pltpu.SemaphoreType.DMA((len(chunks(columns, 256)) + 2,)),
        ],
    )
    return loss.reshape(()), grad_weight, grad_rows


def solution(mesh):
    placed = (
        P("img", None, None),
        P("img", None, None),
        P(None, AXES),
        P(None, AXES),
        P("img", None),
    )
    return jax.shard_map(
        shards,
        mesh=mesh,
        in_specs=placed,
        out_specs=(P(), P(None, AXES), P(AXES, None)),
        check_vma=False,
    )
```

```python
import functools

import jax
import jax.numpy as jnp
from jax import lax
from jax.experimental import pallas as pl
from jax.experimental.pallas import tpu as pltpu
from jax.sharding import PartitionSpec as P

ITERS = 3
TEACHER_TEMP = 0.07
STUDENT_TEMP = 0.1
NORM_EPS = 1e-06
GRAD_SCALE = 1.0 / 128.0
EMPTY = 2.0
LANES = 128
QUAD = 4
F32 = jnp.float32
BF16 = jnp.bfloat16
AXES = ("img", "proto")

VMEM = pl.BlockSpec(memory_space=pltpu.VMEM)
HBM = pl.BlockSpec(memory_space=pltpu.HBM)


def call(body, outs, *args, flops=0, moved=0, exps=0, limit=24, specs=None, out_specs=None, scratch=()):
    return pl.pallas_call(
        body,
        out_shape=outs,
        in_specs=specs or [VMEM] * len(args),
        out_specs=out_specs or tuple(VMEM for _ in outs),
        scratch_shapes=scratch,
        compiler_params=pltpu.CompilerParams(vmem_limit_bytes=limit * 1024 * 1024),
        cost_estimate=pl.CostEstimate(flops=flops, bytes_accessed=moved, transcendentals=exps),
    )(*args)


def near(x):
    return pltpu.with_memory_space_constraint(x, pltpu.VMEM)


def far(x):
    return pltpu.with_memory_space_constraint(x, pltpu.HBM)


def dot(a, b, dims, precision=None):
    return lax.dot_general(a, b, (dims, ((), ())), precision=precision, preferred_element_type=F32)


def iota(shape, dim):
    return lax.broadcasted_iota(jnp.int32, shape, dim)


def add_all(parts):
    return functools.reduce(jnp.add, parts)


def widen(row):
    spare = -row.shape[1] % LANES
    return jnp.concatenate([row, jnp.zeros((1, spare), F32)], axis=1) if spare else row


def tiles_of(row):
    row = widen(row)
    return [row[:, i : i + LANES] for i in range(0, row.shape[1], LANES)]


def to_row(part):
    rows = part.shape[0]
    spare = -rows % LANES
    if spare:
        part = jnp.concatenate([part, jnp.zeros((spare, LANES), F32)], axis=0)
    return jnp.sum(part.T, axis=0, keepdims=True)[:, :rows]


def split(vector):
    high = vector.astype(BF16).astype(F32)
    return [high, vector - high]


def lay_out(vectors, lines, wide):
    tiles = tiles_of(jnp.concatenate(vectors, axis=1))
    tiles += [jnp.zeros((1, LANES), F32)] * (lines * wide // LANES - len(tiles))
    groups = [jnp.concatenate(tiles[g : g + lines], axis=0) for g in range(0, len(tiles), lines)]
    return jnp.concatenate(groups, axis=1)


def read_out(sums, rows, count):
    lines = sums.shape[0]
    turned = [sums[:, g : g + LANES].T for g in range(0, sums.shape[1], LANES)]

    def column(at, stop):
        parts = []
        while at < stop:
            line, lane = divmod(at, LANES)
            until = min(LANES, lane + stop - at)
            parts.append(turned[line // lines][lane:until, line % lines : line % lines + 1])
            at += until - lane
        return jnp.concatenate(parts, axis=0)

    return [jnp.broadcast_to(column(v * rows, (v + 1) * rows), (rows, LANES)) for v in range(count)]


def fold(x):
    return add_all([x[:, i : i + LANES] for i in range(0, x.shape[1], LANES)])


def spread(col, width):
    return jnp.concatenate([col] * (width // LANES), axis=1)


def chunks(columns, step=512):
    step = min(step, columns)
    return [slice(at, at + step) for at in range(0, columns, step)]


def over_chunks(columns, body, start):
    for at in chunks(columns):
        start = body(at, start)
    return start


def start_load(source, target, sems, first=0):
    copies = []
    for i, at in enumerate(chunks(target.shape[1])):
        place = source.at[:, first + at.start : first + at.stop]
        copies.append(pltpu.make_async_copy(place, target.at[:, at], sems.at[i]))
    for copy in copies:
        copy.start()
    return copies


def inverse_norms(w):
    w = w.astype(F32)
    return 1.0 / jnp.sqrt(jnp.sum(w * w, axis=0, keepdims=True) + NORM_EPS)


def odd_half():
    return lax.rem(lax.axis_index("proto"), 2)


def own_slots(mask_ref, feats_ref, own):
    patches = mask_ref.shape[1]
    slot = iota((own, patches), 0) + lax.axis_index("proto") * own
    mask = jnp.broadcast_to(mask_ref[...].astype(F32), (own, patches))
    upto = (iota((patches, patches), 0) <= iota((patches, patches), 1)).astype(BF16)
    rank = dot(mask.astype(BF16), upto, ((1,), (0,)))
    pick = jnp.where((rank == slot.astype(F32) + 1.0) & (mask > 0.5), 1.0, 0.0).astype(BF16)
    valid = slot[:, :1].astype(F32) < rank[:, patches - 1 :]
    rows = dot(pick, feats_ref[0], ((1,), (0,)))
    norm = jnp.sqrt(jnp.sum(rows * rows, axis=1, keepdims=True) + NORM_EPS)
    return (rows / norm).astype(BF16).astype(F32), norm, valid


def teacher_kernel(mask_hbm, stu_hbm, tea_hbm, w_hbm, sent_out, mask_out, stu_out, early_w, tea_ref, sems, w_sems):
    pairs = ((mask_hbm, mask_out), (tea_hbm, tea_ref), (stu_hbm, stu_out))
    copies = [pltpu.make_async_copy(*pair, sems.at[i]) for i, pair in enumerate(pairs)]
    for copy in copies:
        copy.start()
    loads = start_load(w_hbm, early_w, w_sems)
    for copy in copies[:2]:
        copy.wait()
    unit, _, valid = own_slots(mask_out, tea_ref, sent_out.shape[1])
    sent_out[...] = jnp.broadcast_to(jnp.where(valid, unit, EMPTY).astype(BF16)[None], sent_out.shape)
    for copy in copies[2:] + loads:
        copy.wait()


def norms_kernel(mask_ref, stu_ref, early_w, w_hbm, late_w, inv_out, unit_out, norm_out, sems):
    early = early_w.shape[1]
    copies = start_load(w_hbm, late_w, sems, early)
    unit, norm, _ = own_slots(mask_ref, stu_ref, unit_out.shape[0])
    unit_out[...] = unit
    norm_out[...] = jnp.broadcast_to(norm, norm_out.shape)
    for at in chunks(early):
        inv_out[:, at] = inverse_norms(early_w[:, at])
    for copy, at in zip(copies, chunks(late_w.shape[1])):
        copy.wait()
        inv_out[:, early + at.start : early + at.stop] = inverse_norms(late_w[:, at])


def in_order(mine, other, h):
    return jnp.where(odd_half() == h, mine, other)


def slot_flags(data):
    return jnp.where(data[:, :LANES].astype(F32) < 1.5, 1.0, 0.0).astype(BF16)


def packing(flags, hot_out):
    rows = hot_out.shape[0]
    half = flags[0].shape[0]
    step = min(256, half)
    before = jnp.zeros((1, 1), F32)
    upto = (iota((step, step), 0) <= iota((step, step), 1)).astype(BF16)
    same = (iota((step, step), 0) == iota((step, step), 1)).astype(BF16)
    row = iota((rows, step), 0).astype(F32) + 1.0
    for h in range(2):
        for c in range(0, half, step):
            part = flags[h][c : c + step]
            place = before + dot(part, upto, ((0,), (0,)))[:1]
            held = dot(part, same, ((0,), (0,)))[:1]
            hot = jnp.where((row == place) & (held > 0.5), 1.0, 0.0).astype(BF16)
            hot_out[:, h * half + c : h * half + c + step] = hot
            before = place[:, step - 1 :]


def blocks(half):
    step = min(256, half)
    return [(at, at + step) for at in range(0, half, step)]


def pack_rows(hot, read_mine, read_other, half):
    parts = []
    for start, stop in blocks(half):
        mine, other = read_mine(start, stop), read_other(start, stop)
        for h in range(2):
            parts.append(dot(hot[:, h * half + start : h * half + stop], in_order(mine, other, h), ((1,), (0,))))
    return add_all(parts).astype(BF16)


def quads(each, feat):
    return [(row, lane) for lane in range(0, feat, LANES) for row in range(0, each, QUAD)]


def first_kernel(mine, other, early_w, late_w, inv, unit, kernel_out, sent_out, hot_out):
    rows = kernel_out.shape[0]
    peers, _, groups, _, _ = sent_out.shape
    feat = late_w.shape[0]
    packing([slot_flags(in_order(mine[:, :LANES], other[:, :LANES], h)) for h in range(2)], hot_out)
    x = pack_rows(hot_out, lambda a, b: mine[a:b], lambda a, b: other[a:b], mine.shape[0])
    each = unit.shape[0] // 2
    for h in range(2):
        for g, (row, lane) in enumerate(quads(each, feat)):
            part = unit[h * each + row : h * each + row + QUAD, lane : lane + LANES]
            sent_out[:, h, g] = jnp.broadcast_to(part[None], (peers, QUAD, LANES)).astype(BF16)

    acc = jnp.zeros((rows, LANES), F32)
    for w, first in ((early_w, 0), (late_w, early_w.shape[1])):
        for part in chunks(w.shape[1]):
            at = slice(first + part.start, first + part.stop)
            z = dot(x, w[:, part], ((1,), (0,)))
            k = jnp.exp(z * (inv[:, at] * (1.0 / TEACHER_TEMP)))
            kernel_out[:, at] = k
            c = 1.0 / jnp.sum(k, axis=0, keepdims=True)
            acc = acc + fold(k * c)
    held = len(quads(each, feat))
    tiles = lay_out(split(to_row(acc)), QUAD, (groups - held) * LANES)
    for g in range(groups - held):
        tile = tiles[:, g * LANES : (g + 1) * LANES]
        for h in range(2):
            sent_out[:, h, held + g] = jnp.broadcast_to(tile[None], (peers, QUAD, LANES)).astype(BF16)


def spots(hot, sums, start, stop):
    return dot(hot[:, start:stop], sums, ((0,), (0,)))


def halves(hot, sums, at, keep_out, give_out):
    half = keep_out.shape[0]
    odd = odd_half() == 1
    lanes = slice(at, at + sums.shape[1])
    for start, stop in blocks(half):
        low, high = spots(hot, sums, start, stop), spots(hot, sums, half + start, half + stop)
        keep_out[start:stop, lanes] = jnp.where(odd, high, low)
        give_out[start:stop, lanes] = jnp.where(odd, low, high).astype(BF16)


def row_weights(mine, other, hot, own_out, weight_out, protos):
    devices = lax.axis_size(AXES)
    half = mine.shape[0]
    each = half // devices
    per_image = each * protos
    step = min(256, half)
    count, images = [], []
    block = iota((step, step), 0) // per_image
    same = (block == iota((step, step), 1) // per_image).astype(BF16)
    for c in range(0, half, step):
        flags = [slot_flags(ref[c : c + step, :LANES]).astype(F32) for ref in (mine, other)]
        held = dot(same, (flags[0] + flags[1]).astype(BF16), ((1,), (0,)))
        for h in range(2):
            count.append(dot(hot[:, h * half + c : h * half + c + step], held.astype(BF16), ((1,), (0,))))
        first = (iota(held.shape, 0) % per_image == 0) & (held > 0.5)
        images.append(jnp.sum(first.astype(F32), axis=0, keepdims=True))
    weight_out[...] = 1.0 / (jnp.maximum(add_all(count), 1.0) * add_all(images))

    own = own_out.shape[0]
    me = lax.axis_index("img") * protos + lax.axis_index("proto")
    q = iota((own, 2 * half), 0)
    spot = q // each * half + me * each + q % each
    mark = (iota((own, 2 * half), 1) == spot).astype(BF16)
    own_out[...] = dot(mark, hot[...], ((1,), (1,)))


def sweep_kernel(got, kernel, sent_out, *, held):
    rows, columns = kernel.shape
    sums = [jnp.sum(got[:, g].astype(F32), axis=0) for g in range(held, got.shape[1])]
    high, low = read_out(jnp.concatenate(sums, axis=1), rows, 2)
    total = high + low
    wide = spread(1.0 / total, chunks(columns)[0].stop)

    def body(at, acc):
        k = kernel[:, at]
        c = 1.0 / jnp.sum(k * wide, axis=0, keepdims=True)
        return acc + fold(k * c)

    acc = over_chunks(columns, body, jnp.zeros((rows, LANES), F32))
    tiles = jnp.concatenate(tiles_of(to_row(acc)), axis=0)
    sent_out[...] = jnp.broadcast_to(tiles[None], sent_out.shape)


def student_kernel(
    got,
    kernel,
    mine,
    other,
    hot,
    stu_w,
    inv_out,
    logits_out,
    scaled_out,
    xt_out,
    sums_out,
    keep_out,
    give_out,
    stack,
):
    rows, columns = logits_out.shape
    feat = stu_w.shape[0]
    half = keep_out.shape[0]
    each = half // lax.axis_size(AXES)

    def reader(ref):
        def read(start, stop):
            peers = slice(start // each, stop // each)
            parts = [ref[peers, g].astype(F32) for g in range(len(quads(each, feat)))]
            deep = each // QUAD
            lanes = [jnp.concatenate(parts[g : g + deep], axis=1) for g in range(0, len(parts), deep)]
            return jnp.concatenate([part.reshape(stop - start, LANES) for part in lanes], axis=1).astype(BF16)

        return read

    x = pack_rows(hot, reader(mine), reader(other), half)
    xt = x.astype(F32).T
    xt_out[...] = xt.astype(BF16)
    (total,) = read_out(jnp.sum(got[...], axis=0), rows, 1)
    wide = spread(1.0 / total, chunks(columns)[0].stop)

    def student(at, acc):
        w = stu_w[:, at]
        n = inverse_norms(w)
        inv_out[:, at] = n
        l = dot(x, w, ((1,), (0,))) * (n * (1.0 / STUDENT_TEMP))
        logits_out[:, at] = l
        p = jnp.exp(l)
        stack[:rows, at] = (p * n).astype(BF16)
        return acc + fold(p)

    def sweep(at, acc):
        k = kernel[:, at]
        kc = k * (1.0 / jnp.sum(k * wide, axis=0, keepdims=True))
        scaled_out[:, at] = kc
        stack[rows:, at] = (kc * inv_out[:, at]).astype(BF16)
        return acc + fold(kc)

    zero = jnp.zeros((rows, LANES), F32)
    part = over_chunks(columns, student, zero)
    total = over_chunks(columns, sweep, zero)
    sums = dot(stack[...], stu_w[...], ((1,), (1,)))
    pull, push = sums[:rows], sums[rows:]
    halves(hot, pull.astype(BF16), 0, keep_out, give_out)
    halves(hot, push.astype(BF16), feat, keep_out, give_out)
    cross = to_row(fold(push * x.astype(F32))) * (1.0 / STUDENT_TEMP)
    sums_out[...] = lay_out([to_row(part), to_row(total), cross], *sums_out.shape)


def prepare_kernel(
    scaled, logits, inv, mine, other, hot, pull_out, push_out, own_out, weight_out, *, scale, protos
):
    rows, columns = scaled.shape
    row_weights(mine, other, hot, own_out, weight_out, protos)
    factor = spread(weight_out[...] * (rows / STUDENT_TEMP), chunks(columns)[0].stop)

    def body(at, _):
        n = inv[:, at] * scale
        pull_out[:, at] = factor * jnp.exp(logits[:, at]) * n
        push_out[:, at] = factor * scaled[:, at] * n
        return 0

    over_chunks(columns, body, 0)


def fill_kernel(keep, give, sums, sent_out):
    devices, groups, _, _ = sent_out.shape
    half, both = keep.shape
    each = half // devices
    pair = keep[...] + give[...].astype(F32)
    places = quads(each, both)
    for g, (row, lane) in enumerate(places):
        part = pair[:, lane : lane + LANES].reshape(devices, each, LANES)
        sent_out[:, g] = part[:, row : row + QUAD].astype(BF16)
    for g in range(len(places), groups):
        at = (g - len(places)) * LANES
        sent_out[:, g] = jnp.broadcast_to(sums[:, at : at + LANES][None], (devices, QUAD, LANES)).astype(BF16)


def slots_of(got, each, both):
    sums = [jnp.sum(got[:, :, g].astype(F32), axis=0) for g in range(len(quads(each, both)))]
    deep = each // QUAD
    lanes = [
        jnp.concatenate([sums[g + i][h] for h in range(2) for i in range(deep)], axis=0) for g in range(0, len(sums), deep)
    ]
    return jnp.concatenate(lanes, axis=1)


def final_kernel(
    got,
    pull,
    push,
    logits,
    inv,
    stu_w,
    xt,
    weight,
    own,
    unit,
    norm,
    out_hbm,
    rows_hbm,
    loss_hbm,
    out,
    rows_out,
    loss_out,
    sems,
):
    rows, columns = pull.shape
    feat = xt.shape[0]
    each = unit.shape[0] // 2
    held = len(quads(each, 2 * feat))
    sums = [jnp.sum(got[:, :, g].astype(F32), axis=(0, 1)) for g in range(held, got.shape[2])]
    partition, total, cross = read_out(jnp.concatenate(sums, axis=1), rows, 3)
    parts = chunks(columns, 256)
    raise_by, lower_by = 1.0 / partition, 1.0 / total
    grow, shrink = spread(raise_by, parts[0].stop), spread(lower_by, parts[0].stop)
    copies = []

    def send(source, target):
        copies.append(pltpu.make_async_copy(source, target, sems.at[len(copies)]))
        copies[-1].start()

    def gradient(at):
        g = grow * pull[:, at] - shrink * push[:, at]
        along = jnp.sum(g * logits[:, at], axis=0, keepdims=True) * (inv[:, at] * STUDENT_TEMP)
        return g.astype(BF16), along

    ready = gradient(parts[0])
    for at, following in zip(parts, parts[1:] + [None]):
        g, along = ready
        direct = dot(xt[...], g, ((1,), (0,)))
        if following is not None:
            ready = gradient(following)
        out[:, at] = direct - stu_w[:, at].astype(F32) * along
        send(out.at[:, at], out_hbm.at[:, at])
    share = weight[...]
    loss = jnp.sum(share * (jnp.log(partition) - cross * lower_by), axis=0, keepdims=True)
    loss_out[...] = loss[:, :1]
    send(loss_out, loss_hbm)
    factors = jnp.concatenate([raise_by, lower_by], axis=1) * spread(share * (rows / STUDENT_TEMP), 2 * LANES)
    scale = dot(own[...], factors, ((1,), (0,)), lax.Precision.HIGHEST)
    sums = slots_of(got, each, 2 * feat)
    full = sums[:, :feat] * scale[:, :1] - sums[:, feat:] * scale[:, LANES : LANES + 1]
    u = unit[...]
    rows_out[...] = (full - u * jnp.sum(u * full, axis=1, keepdims=True)) / norm[:, :1]
    send(rows_out, rows_hbm)
    for copy in copies:
        copy.wait()


def shards(student_feats, teacher_feats, student_weight, teacher_weight, patch_masks):
    devices = lax.axis_size(AXES)
    protos = lax.axis_size("proto")
    images, patches, feat = student_feats.shape
    assert images == 1 and protos % 2 == 0
    columns = student_weight.shape[1]
    own = patches // 2 // protos
    each = own // 2
    half = each * devices
    rows = 2 * half * 5 // 16
    tiles = -(-rows // LANES)
    spare = lambda parts: -(-parts * rows // (QUAD * LANES))
    held = len(quads(each, feat))
    big = rows * columns
    exchange = functools.partial(lax.all_to_all, axis_name=AXES, split_axis=0, concat_axis=0)
    swap = functools.partial(lax.ppermute, axis_name="proto", perm=[(p, p ^ 1) for p in range(protos)])
    matrix = pltpu.VMEM((rows, columns), F32)
    column = pltpu.VMEM((rows, LANES), F32)
    line = pltpu.VMEM((1, columns), F32)

    flags = pltpu.VMEM(patch_masks.shape, patch_masks.dtype)
    feats = pltpu.VMEM(student_feats.shape, BF16)
    early = columns * 3 // 8 // LANES * LANES
    early_w, late_w = pltpu.VMEM((feat, early), BF16), pltpu.VMEM((feat, columns - early), BF16)
    sent, flags, feats, early_w = call(
        teacher_kernel,
        (pltpu.VMEM((devices // 2, own, feat), BF16), flags, feats, early_w),
        far(patch_masks),
        far(student_feats),
        far(teacher_feats),
        far(teacher_weight),
        specs=[HBM] * 4,
        scratch=[feats, pltpu.SemaphoreType.DMA((3,)), pltpu.SemaphoreType.DMA((len(chunks(early)),))],
    )
    mine = exchange(sent.reshape(devices, each, feat)).reshape(half, feat)
    mine, teacher_weight = lax.optimization_barrier((mine, teacher_weight))
    other = near(swap(mine))
    mine = near(mine)
    late_w, tea_inv, unit, norm = call(
        norms_kernel,
        (
            late_w,
            line,
            pltpu.VMEM((own, feat), F32),
            pltpu.VMEM((own, LANES), F32),
        ),
        flags,
        feats,
        early_w,
        far(teacher_weight),
        flops=2 * feat * columns,
        moved=4 * feat * columns,
        specs=[VMEM, VMEM, VMEM, HBM],
        scratch=[pltpu.SemaphoreType.DMA((len(chunks(columns - early)),))],
    )
    kernel, sent, hot = call(
        first_kernel,
        (
            matrix,
            pltpu.VMEM((devices // 2, 2, held + spare(2), QUAD, LANES), BF16),
            pltpu.VMEM((rows, 2 * half), BF16),
        ),
        mine,
        other,
        early_w,
        late_w,
        tea_inv,
        unit,
        flops=2 * big * feat,
        moved=4 * big,
        exps=big,
    )
    stu_mine = exchange(sent.reshape(devices, *sent.shape[2:]))
    stu_other = near(swap(stu_mine))
    stu_mine = near(stu_mine)
    (sent,) = call(
        functools.partial(sweep_kernel, held=held),
        (pltpu.VMEM((devices, tiles, LANES), F32),),
        stu_mine,
        kernel,
        flops=4 * big,
        moved=4 * big,
    )
    got = near(exchange(sent))
    stu_inv, logits, scaled, xt, sums, keep, give = call(
        student_kernel,
        (
            line,
            matrix,
            matrix,
            pltpu.VMEM((feat, rows), BF16),
            pltpu.VMEM((QUAD, spare(3) * LANES), F32),
            pltpu.VMEM((half, 2 * feat), F32),
            pltpu.VMEM((half, 2 * feat), BF16),
        ),
        got,
        kernel,
        stu_mine,
        stu_other,
        hot,
        student_weight,
        flops=6 * big * feat,
        moved=12 * big,
        exps=big,
        scratch=[pltpu.VMEM((2 * rows, columns), BF16)],
        limit=22 + half // 112,
    )
    give = near(swap(give))
    pull, push, own_hot, weight = call(
        functools.partial(prepare_kernel, scale=columns * devices * GRAD_SCALE, protos=protos),
        (matrix, matrix, pltpu.VMEM((own, rows), F32), column),
        scaled,
        logits,
        stu_inv,
        mine,
        other,
        hot,
        flops=4 * big,
        moved=16 * big,
        exps=big,
    )
    keep, pull, push, own_hot, weight = lax.optimization_barrier((keep, pull, push, own_hot, weight))
    payload = pltpu.VMEM((devices, 2 * held + spare(3), QUAD, LANES), BF16)
    (sent,) = call(fill_kernel, (payload,), keep, give, sums)
    got = exchange(sent)
    got = near(got.reshape(devices // 2, 2, *got.shape[1:]))
    grad_weight, grad_rows, loss = call(
        final_kernel,
        (
            jax.ShapeDtypeStruct((feat, columns), F32),
            jax.ShapeDtypeStruct((own, feat), F32),
            jax.ShapeDtypeStruct((1, 1), F32),
        ),
        got,
        pull,
        push,
        logits,
        stu_inv,
        student_weight,
        xt,
        weight,
        own_hot,
        unit,
        norm,
        flops=2 * big * feat,
        moved=8 * feat * columns,
        out_specs=(HBM, HBM, HBM),
        scratch=[
            pltpu.VMEM((feat, columns), F32),
            pltpu.VMEM((own, feat), F32),
            pltpu.VMEM((1, 1), F32),
            pltpu.SemaphoreType.DMA((len(chunks(columns, 256)) + 2,)),
        ],
    )
    return loss.reshape(()), grad_weight, grad_rows


def solution(mesh):
    placed = (
        P("img", None, None),
        P("img", None, None),
        P(None, AXES),
        P(None, AXES),
        P("img", None),
    )
    return jax.shard_map(
        shards,
        mesh=mesh,
        in_specs=placed,
        out_specs=(P(), P(None, AXES), P(AXES, None)),
        check_vma=False,
    )
```

```python
import functools

import jax
import jax.numpy as jnp
from jax import lax
from jax.experimental import pallas as pl
from jax.experimental.pallas import tpu as pltpu
from jax.sharding import PartitionSpec as P

ITERS = 3
TEACHER_TEMP = 0.07
STUDENT_TEMP = 0.1
NORM_EPS = 1e-06
GRAD_SCALE = 1.0 / 128.0
EMPTY = 2.0
LANES = 128
QUAD = 4
F32 = jnp.float32
BF16 = jnp.bfloat16
AXES = ("img", "proto")

VMEM = pl.BlockSpec(memory_space=pltpu.VMEM)
HBM = pl.BlockSpec(memory_space=pltpu.HBM)


def call(body, outs, *args, flops=0, moved=0, exps=0, limit=24, specs=None, out_specs=None, scratch=()):
    return pl.pallas_call(
        body,
        out_shape=outs,
        in_specs=specs or [VMEM] * len(args),
        out_specs=out_specs or tuple(VMEM for _ in outs),
        scratch_shapes=scratch,
        compiler_params=pltpu.CompilerParams(vmem_limit_bytes=limit * 1024 * 1024),
        cost_estimate=pl.CostEstimate(flops=flops, bytes_accessed=moved, transcendentals=exps),
    )(*args)


def near(x):
    return pltpu.with_memory_space_constraint(x, pltpu.VMEM)


def far(x):
    return pltpu.with_memory_space_constraint(x, pltpu.HBM)


def dot(a, b, dims, precision=None):
    return lax.dot_general(a, b, (dims, ((), ())), precision=precision, preferred_element_type=F32)


def iota(shape, dim):
    return lax.broadcasted_iota(jnp.int32, shape, dim)


def add_all(parts):
    return functools.reduce(jnp.add, parts)


def widen(row):
    spare = -row.shape[1] % LANES
    return jnp.concatenate([row, jnp.zeros((1, spare), F32)], axis=1) if spare else row


def tiles_of(row):
    row = widen(row)
    return [row[:, i : i + LANES] for i in range(0, row.shape[1], LANES)]


def to_row(part):
    rows = part.shape[0]
    spare = -rows % LANES
    if spare:
        part = jnp.concatenate([part, jnp.zeros((spare, LANES), F32)], axis=0)
    return jnp.sum(part.T, axis=0, keepdims=True)[:, :rows]


def split(vector):
    high = vector.astype(BF16).astype(F32)
    return [high, vector - high]


def lay_out(vectors, lines, wide):
    tiles = tiles_of(jnp.concatenate(vectors, axis=1))
    tiles += [jnp.zeros((1, LANES), F32)] * (lines * wide // LANES - len(tiles))
    groups = [jnp.concatenate(tiles[g : g + lines], axis=0) for g in range(0, len(tiles), lines)]
    return jnp.concatenate(groups, axis=1)


def read_out(sums, rows, count):
    lines = sums.shape[0]
    turned = [sums[:, g : g + LANES].T for g in range(0, sums.shape[1], LANES)]

    def column(at, stop):
        parts = []
        while at < stop:
            line, lane = divmod(at, LANES)
            until = min(LANES, lane + stop - at)
            parts.append(turned[line // lines][lane:until, line % lines : line % lines + 1])
            at += until - lane
        return jnp.concatenate(parts, axis=0)

    return [jnp.broadcast_to(column(v * rows, (v + 1) * rows), (rows, LANES)) for v in range(count)]


def fold(x):
    return add_all([x[:, i : i + LANES] for i in range(0, x.shape[1], LANES)])


def spread(col, width):
    return jnp.concatenate([col] * (width // LANES), axis=1)


def chunks(columns, step=512):
    step = min(step, columns)
    return [slice(at, at + step) for at in range(0, columns, step)]


def over_chunks(columns, body, start):
    for at in chunks(columns):
        start = body(at, start)
    return start


def start_load(source, target, sems, first=0):
    copies = []
    for i, at in enumerate(chunks(target.shape[1])):
        place = source.at[:, first + at.start : first + at.stop]
        copies.append(pltpu.make_async_copy(place, target.at[:, at], sems.at[i]))
    for copy in copies:
        copy.start()
    return copies


def inverse_norms(w):
    w = w.astype(F32)
    return 1.0 / jnp.sqrt(jnp.sum(w * w, axis=0, keepdims=True) + NORM_EPS)


def odd_half():
    return lax.rem(lax.axis_index("proto"), 2)


def own_slots(mask_ref, feats_ref, own):
    patches = mask_ref.shape[1]
    slot = iota((own, patches), 0) + lax.axis_index("proto") * own
    mask = jnp.broadcast_to(mask_ref[...].astype(F32), (own, patches))
    upto = (iota((patches, patches), 0) <= iota((patches, patches), 1)).astype(BF16)
    rank = dot(mask.astype(BF16), upto, ((1,), (0,)))
    pick = jnp.where((rank == slot.astype(F32) + 1.0) & (mask > 0.5), 1.0, 0.0).astype(BF16)
    valid = slot[:, :1].astype(F32) < rank[:, patches - 1 :]
    rows = dot(pick, feats_ref[0], ((1,), (0,)))
    norm = jnp.sqrt(jnp.sum(rows * rows, axis=1, keepdims=True) + NORM_EPS)
    return (rows / norm).astype(BF16).astype(F32), norm, valid


def teacher_kernel(mask_hbm, stu_hbm, tea_hbm, w_hbm, sent_out, mask_out, stu_out, early_w, tea_ref, sems, w_sems):
    pairs = ((mask_hbm, mask_out), (tea_hbm, tea_ref), (stu_hbm, stu_out))
    copies = [pltpu.make_async_copy(*pair, sems.at[i]) for i, pair in enumerate(pairs)]
    for copy in copies:
        copy.start()
    loads = start_load(w_hbm, early_w, w_sems)
    for copy in copies[:2]:
        copy.wait()
    unit, _, valid = own_slots(mask_out, tea_ref, sent_out.shape[1])
    sent_out[...] = jnp.broadcast_to(jnp.where(valid, unit, EMPTY).astype(BF16)[None], sent_out.shape)
    for copy in copies[2:] + loads:
        copy.wait()


def norms_kernel(mask_ref, stu_ref, early_w, w_hbm, late_w, inv_out, unit_out, norm_out, sems):
    early = early_w.shape[1]
    copies = start_load(w_hbm, late_w, sems, early)
    unit, norm, _ = own_slots(mask_ref, stu_ref, unit_out.shape[0])
    unit_out[...] = unit
    norm_out[...] = jnp.broadcast_to(norm, norm_out.shape)
    for at in chunks(early):
        inv_out[:, at] = inverse_norms(early_w[:, at])
    for copy, at in zip(copies, chunks(late_w.shape[1])):
        copy.wait()
        inv_out[:, early + at.start : early + at.stop] = inverse_norms(late_w[:, at])


def in_order(mine, other, h):
    return jnp.where(odd_half() == h, mine, other)


def slot_flags(data):
    return jnp.where(data[:, :LANES].astype(F32) < 1.5, 1.0, 0.0).astype(BF16)


def packing(flags, hot_out):
    rows = hot_out.shape[0]
    half = flags[0].shape[0]
    step = min(256, half)
    before = jnp.zeros((1, 1), F32)
    upto = (iota((step, step), 0) <= iota((step, step), 1)).astype(BF16)
    same = (iota((step, step), 0) == iota((step, step), 1)).astype(BF16)
    row = iota((rows, step), 0).astype(F32) + 1.0
    for h in range(2):
        for c in range(0, half, step):
            part = flags[h][c : c + step]
            place = before + dot(part, upto, ((0,), (0,)))[:1]
            held = dot(part, same, ((0,), (0,)))[:1]
            hot = jnp.where((row == place) & (held > 0.5), 1.0, 0.0).astype(BF16)
            hot_out[:, h * half + c : h * half + c + step] = hot
            before = place[:, step - 1 :]


def blocks(half):
    step = min(256, half)
    return [(at, at + step) for at in range(0, half, step)]


def pack_rows(hot, read_mine, read_other, half):
    parts = []
    for start, stop in blocks(half):
        mine, other = read_mine(start, stop), read_other(start, stop)
        for h in range(2):
            parts.append(dot(hot[:, h * half + start : h * half + stop], in_order(mine, other, h), ((1,), (0,))))
    return add_all(parts).astype(BF16)


def quads(each, feat):
    return [(row, lane) for lane in range(0, feat, LANES) for row in range(0, each, QUAD)]


def first_kernel(mine, other, early_w, late_w, inv, unit, kernel_out, sent_out, hot_out):
    rows = kernel_out.shape[0]
    peers, _, groups, _, _ = sent_out.shape
    feat = late_w.shape[0]
    packing([slot_flags(in_order(mine[:, :LANES], other[:, :LANES], h)) for h in range(2)], hot_out)
    x = pack_rows(hot_out, lambda a, b: mine[a:b], lambda a, b: other[a:b], mine.shape[0])
    each = unit.shape[0] // 2
    for h in range(2):
        for g, (row, lane) in enumerate(quads(each, feat)):
            part = unit[h * each + row : h * each + row + QUAD, lane : lane + LANES]
            sent_out[:, h, g] = jnp.broadcast_to(part[None], (peers, QUAD, LANES)).astype(BF16)

    acc = jnp.zeros((rows, LANES), F32)
    for w, first in ((early_w, 0), (late_w, early_w.shape[1])):
        for part in chunks(w.shape[1]):
            at = slice(first + part.start, first + part.stop)
            z = dot(x, w[:, part], ((1,), (0,)))
            k = jnp.exp(z * (inv[:, at] * (1.0 / TEACHER_TEMP)))
            kernel_out[:, at] = k
            c = 1.0 / jnp.sum(k, axis=0, keepdims=True)
            acc = acc + fold(k * c)
    held = len(quads(each, feat))
    tiles = lay_out(split(to_row(acc)), QUAD, (groups - held) * LANES)
    for g in range(groups - held):
        tile = tiles[:, g * LANES : (g + 1) * LANES]
        for h in range(2):
            sent_out[:, h, held + g] = jnp.broadcast_to(tile[None], (peers, QUAD, LANES)).astype(BF16)


def row_weights(mine, other, hot, own_out, weight_out, protos):
    devices = lax.axis_size(AXES)
    half = mine.shape[0]
    each = half // devices
    per_image = each * protos
    step = min(256, half)
    count, images = [], []
    block = iota((step, step), 0) // per_image
    same = (block == iota((step, step), 1) // per_image).astype(BF16)
    for c in range(0, half, step):
        flags = [slot_flags(ref[c : c + step, :LANES]).astype(F32) for ref in (mine, other)]
        held = dot(same, (flags[0] + flags[1]).astype(BF16), ((1,), (0,)))
        for h in range(2):
            count.append(dot(hot[:, h * half + c : h * half + c + step], held.astype(BF16), ((1,), (0,))))
        first = (iota(held.shape, 0) % per_image == 0) & (held > 0.5)
        images.append(jnp.sum(first.astype(F32), axis=0, keepdims=True))
    weight_out[...] = 1.0 / (jnp.maximum(add_all(count), 1.0) * add_all(images))

    own = own_out.shape[0]
    me = lax.axis_index("img") * protos + lax.axis_index("proto")
    q = iota((own, 2 * half), 0)
    spot = q // each * half + me * each + q % each
    mark = (iota((own, 2 * half), 1) == spot).astype(BF16)
    own_out[...] = dot(mark, hot[...], ((1,), (1,)))


def sweep_kernel(got, kernel, sent_out, *, held):
    rows, columns = kernel.shape
    sums = [jnp.sum(got[:, g].astype(F32), axis=0) for g in range(held, got.shape[1])]
    high, low = read_out(jnp.concatenate(sums, axis=1), rows, 2)
    total = high + low
    wide = spread(1.0 / total, chunks(columns)[0].stop)

    def body(at, acc):
        k = kernel[:, at]
        c = 1.0 / jnp.sum(k * wide, axis=0, keepdims=True)
        return acc + fold(k * c)

    acc = over_chunks(columns, body, jnp.zeros((rows, LANES), F32))
    tiles = jnp.concatenate(tiles_of(to_row(acc)), axis=0)
    sent_out[...] = jnp.broadcast_to(tiles[None], sent_out.shape)


def student_kernel(
    got,
    kernel,
    mine,
    other,
    hot,
    stu_w,
    inv_out,
    logits_out,
    scaled_out,
    xt_out,
    vectors_out,
    keep_out,
    give_out,
    stack,
):
    rows, columns = logits_out.shape
    feat = stu_w.shape[0]
    half = hot.shape[1] // 2
    each = half // lax.axis_size(AXES)

    def reader(ref):
        def read(start, stop):
            peers = slice(start // each, stop // each)
            parts = [ref[peers, g].astype(F32) for g in range(len(quads(each, feat)))]
            deep = each // QUAD
            lanes = [jnp.concatenate(parts[g : g + deep], axis=1) for g in range(0, len(parts), deep)]
            return jnp.concatenate([part.reshape(stop - start, LANES) for part in lanes], axis=1).astype(BF16)

        return read

    x = pack_rows(hot, reader(mine), reader(other), half)
    xt = x.astype(F32).T
    xt_out[...] = xt.astype(BF16)
    (total,) = read_out(jnp.sum(got[...], axis=0), rows, 1)
    wide = spread(1.0 / total, chunks(columns)[0].stop)

    def student(at, acc):
        w = stu_w[:, at]
        n = inverse_norms(w)
        inv_out[:, at] = n
        l = dot(x, w, ((1,), (0,))) * (n * (1.0 / STUDENT_TEMP))
        logits_out[:, at] = l
        p = jnp.exp(l)
        stack[:rows, at] = (p * n).astype(BF16)
        return acc + fold(p)

    def sweep(at, acc):
        k = kernel[:, at]
        kc = k * (1.0 / jnp.sum(k * wide, axis=0, keepdims=True))
        scaled_out[:, at] = kc
        stack[rows:, at] = (kc * inv_out[:, at]).astype(BF16)
        return acc + fold(kc)

    zero = jnp.zeros((rows, LANES), F32)
    part = over_chunks(columns, student, zero)
    total = over_chunks(columns, sweep, zero)
    sums = dot(stack[...], stu_w[...], ((1,), (1,)))
    for part_of, lanes in ((sums[:rows], slice(0, feat)), (sums[rows:], slice(feat, 2 * feat))):
        keep_out[:, lanes] = part_of
        give_out[:, lanes] = part_of.astype(BF16)
    cross = to_row(fold(sums[rows:] * x.astype(F32))) * (1.0 / STUDENT_TEMP)
    vectors_out[...] = lay_out([to_row(part), to_row(total), cross], *vectors_out.shape)


def prepare_kernel(
    scaled, logits, inv, mine, other, hot, pull_out, push_out, own_out, weight_out, *, scale, protos
):
    rows, columns = scaled.shape
    row_weights(mine, other, hot, own_out, weight_out, protos)
    factor = spread(weight_out[...] * (rows / STUDENT_TEMP), chunks(columns)[0].stop)

    def body(at, _):
        n = inv[:, at] * scale
        pull_out[:, at] = factor * jnp.exp(logits[:, at]) * n
        push_out[:, at] = factor * scaled[:, at] * n
        return 0

    over_chunks(columns, body, 0)


def fill_kernel(keep, give, hot, vectors, sent_out):
    devices, groups, _, _ = sent_out.shape
    half, both = hot.shape[1] // 2, keep.shape[1]
    each = half // devices
    pair = (keep[...] + give[...].astype(F32)).astype(BF16)
    places = quads(each, both)
    for start, stop in blocks(half):
        own = jnp.where(odd_half() == 1, hot[:, half + start : half + stop], hot[:, start:stop])
        slots = dot(own, pair, ((0,), (0,)))
        peers = slice(start // each, stop // each)
        for g, (row, lane) in enumerate(places):
            part = slots[:, lane : lane + LANES].reshape((stop - start) // each, each, LANES)
            sent_out[peers, g] = part[:, row : row + QUAD].astype(BF16)
    for g in range(len(places), groups):
        at = (g - len(places)) * LANES
        sent_out[:, g] = jnp.broadcast_to(vectors[:, at : at + LANES][None], (devices, QUAD, LANES)).astype(BF16)


def slots_of(got, each, both):
    sums = [jnp.sum(got[:, :, g].astype(F32), axis=0) for g in range(len(quads(each, both)))]
    deep = each // QUAD
    lanes = [
        jnp.concatenate([sums[g + i][h] for h in range(2) for i in range(deep)], axis=0) for g in range(0, len(sums), deep)
    ]
    return jnp.concatenate(lanes, axis=1)


def final_kernel(
    got,
    pull,
    push,
    logits,
    inv,
    stu_w,
    xt,
    weight,
    own,
    unit,
    norm,
    out_hbm,
    rows_hbm,
    loss_hbm,
    out,
    rows_out,
    loss_out,
    sems,
):
    rows, columns = pull.shape
    feat = xt.shape[0]
    each = unit.shape[0] // 2
    held = len(quads(each, 2 * feat))
    sums = [jnp.sum(got[:, :, g].astype(F32), axis=(0, 1)) for g in range(held, got.shape[2])]
    partition, total, cross = read_out(jnp.concatenate(sums, axis=1), rows, 3)
    parts = chunks(columns, 256)
    raise_by, lower_by = 1.0 / partition, 1.0 / total
    grow, shrink = spread(raise_by, parts[0].stop), spread(lower_by, parts[0].stop)
    copies = []

    def send(source, target):
        copies.append(pltpu.make_async_copy(source, target, sems.at[len(copies)]))
        copies[-1].start()

    def gradient(at):
        g = grow * pull[:, at] - shrink * push[:, at]
        along = jnp.sum(g * logits[:, at], axis=0, keepdims=True) * (inv[:, at] * STUDENT_TEMP)
        return g.astype(BF16), along

    ready = gradient(parts[0])
    for at, following in zip(parts, parts[1:] + [None]):
        g, along = ready
        direct = dot(xt[...], g, ((1,), (0,)))
        if following is not None:
            ready = gradient(following)
        out[:, at] = direct - stu_w[:, at].astype(F32) * along
        send(out.at[:, at], out_hbm.at[:, at])
    share = weight[...]
    loss = jnp.sum(share * (jnp.log(partition) - cross * lower_by), axis=0, keepdims=True)
    loss_out[...] = loss[:, :1]
    send(loss_out, loss_hbm)
    factors = jnp.concatenate([raise_by, lower_by], axis=1) * spread(share * (rows / STUDENT_TEMP), 2 * LANES)
    scale = dot(own[...], factors, ((1,), (0,)), lax.Precision.HIGHEST)
    sums = slots_of(got, each, 2 * feat)
    full = sums[:, :feat] * scale[:, :1] - sums[:, feat:] * scale[:, LANES : LANES + 1]
    u = unit[...]
    rows_out[...] = (full - u * jnp.sum(u * full, axis=1, keepdims=True)) / norm[:, :1]
    send(rows_out, rows_hbm)
    for copy in copies:
        copy.wait()


def shards(student_feats, teacher_feats, student_weight, teacher_weight, patch_masks):
    devices = lax.axis_size(AXES)
    protos = lax.axis_size("proto")
    images, patches, feat = student_feats.shape
    assert images == 1 and protos % 2 == 0
    columns = student_weight.shape[1]
    own = patches // 2 // protos
    each = own // 2
    half = each * devices
    rows = 2 * half * 5 // 16
    tiles = -(-rows // LANES)
    spare = lambda parts: -(-parts * rows // (QUAD * LANES))
    held = len(quads(each, feat))
    big = rows * columns
    exchange = functools.partial(lax.all_to_all, axis_name=AXES, split_axis=0, concat_axis=0)
    swap = functools.partial(lax.ppermute, axis_name="proto", perm=[(p, p ^ 1) for p in range(protos)])
    matrix = pltpu.VMEM((rows, columns), F32)
    column = pltpu.VMEM((rows, LANES), F32)
    line = pltpu.VMEM((1, columns), F32)

    flags = pltpu.VMEM(patch_masks.shape, patch_masks.dtype)
    feats = pltpu.VMEM(student_feats.shape, BF16)
    early = columns * 3 // 8 // LANES * LANES
    early_w, late_w = pltpu.VMEM((feat, early), BF16), pltpu.VMEM((feat, columns - early), BF16)
    sent, flags, feats, early_w = call(
        teacher_kernel,
        (pltpu.VMEM((devices // 2, own, feat), BF16), flags, feats, early_w),
        far(patch_masks),
        far(student_feats),
        far(teacher_feats),
        far(teacher_weight),
        specs=[HBM] * 4,
        scratch=[feats, pltpu.SemaphoreType.DMA((3,)), pltpu.SemaphoreType.DMA((len(chunks(early)),))],
    )
    mine = exchange(sent.reshape(devices, each, feat)).reshape(half, feat)
    mine, teacher_weight = lax.optimization_barrier((mine, teacher_weight))
    other = near(swap(mine))
    mine = near(mine)
    late_w, tea_inv, unit, norm = call(
        norms_kernel,
        (
            late_w,
            line,
            pltpu.VMEM((own, feat), F32),
            pltpu.VMEM((own, LANES), F32),
        ),
        flags,
        feats,
        early_w,
        far(teacher_weight),
        flops=2 * feat * columns,
        moved=4 * feat * columns,
        specs=[VMEM, VMEM, VMEM, HBM],
        scratch=[pltpu.SemaphoreType.DMA((len(chunks(columns - early)),))],
    )
    kernel, sent, hot = call(
        first_kernel,
        (
            matrix,
            pltpu.VMEM((devices // 2, 2, held + spare(2), QUAD, LANES), BF16),
            pltpu.VMEM((rows, 2 * half), BF16),
        ),
        mine,
        other,
        early_w,
        late_w,
        tea_inv,
        unit,
        flops=2 * big * feat,
        moved=4 * big,
        exps=big,
    )
    stu_mine = exchange(sent.reshape(devices, *sent.shape[2:]))
    stu_other = near(swap(stu_mine))
    stu_mine = near(stu_mine)
    (sent,) = call(
        functools.partial(sweep_kernel, held=held),
        (pltpu.VMEM((devices, tiles, LANES), F32),),
        stu_mine,
        kernel,
        flops=4 * big,
        moved=4 * big,
    )
    got = near(exchange(sent))
    stu_inv, logits, scaled, xt, sums, keep, give = call(
        student_kernel,
        (
            line,
            matrix,
            matrix,
            pltpu.VMEM((feat, rows), BF16),
            pltpu.VMEM((QUAD, spare(3) * LANES), F32),
            pltpu.VMEM((rows, 2 * feat), F32),
            pltpu.VMEM((rows, 2 * feat), BF16),
        ),
        got,
        kernel,
        stu_mine,
        stu_other,
        hot,
        student_weight,
        flops=6 * big * feat,
        moved=12 * big,
        exps=big,
        scratch=[pltpu.VMEM((2 * rows, columns), BF16)],
        limit=22 + half // 112,
    )
    give = near(swap(give))
    pull, push, own_hot, weight = call(
        functools.partial(prepare_kernel, scale=columns * devices * GRAD_SCALE, protos=protos),
        (matrix, matrix, pltpu.VMEM((own, rows), F32), column),
        scaled,
        logits,
        stu_inv,
        mine,
        other,
        hot,
        flops=4 * big,
        moved=16 * big,
        exps=big,
    )
    keep, pull, push, own_hot, weight = lax.optimization_barrier((keep, pull, push, own_hot, weight))
    payload = pltpu.VMEM((devices, 2 * held + spare(3), QUAD, LANES), BF16)
    (sent,) = call(fill_kernel, (payload,), keep, give, hot, sums)
    got = exchange(sent)
    got = near(got.reshape(devices // 2, 2, *got.shape[1:]))
    grad_weight, grad_rows, loss = call(
        final_kernel,
        (
            jax.ShapeDtypeStruct((feat, columns), F32),
            jax.ShapeDtypeStruct((own, feat), F32),
            jax.ShapeDtypeStruct((1, 1), F32),
        ),
        got,
        pull,
        push,
        logits,
        stu_inv,
        student_weight,
        xt,
        weight,
        own_hot,
        unit,
        norm,
        flops=2 * big * feat,
        moved=8 * feat * columns,
        out_specs=(HBM, HBM, HBM),
        scratch=[
            pltpu.VMEM((feat, columns), F32),
            pltpu.VMEM((own, feat), F32),
            pltpu.VMEM((1, 1), F32),
            pltpu.SemaphoreType.DMA((len(chunks(columns, 256)) + 2,)),
        ],
    )
    return loss.reshape(()), grad_weight, grad_rows


def solution(mesh):
    placed = (
        P("img", None, None),
        P("img", None, None),
        P(None, AXES),
        P(None, AXES),
        P("img", None),
    )
    return jax.shard_map(
        shards,
        mesh=mesh,
        in_specs=placed,
        out_specs=(P(), P(None, AXES), P(AXES, None)),
        check_vma=False,
    )
```

```python
import functools

import jax
import jax.numpy as jnp
from jax import lax
from jax.experimental import pallas as pl
from jax.experimental.pallas import tpu as pltpu
from jax.sharding import PartitionSpec as P

ITERS = 3
TEACHER_TEMP = 0.07
STUDENT_TEMP = 0.1
NORM_EPS = 1e-06
GRAD_SCALE = 1.0 / 128.0
EMPTY = 2.0
LANES = 128
QUAD = 4
F32 = jnp.float32
BF16 = jnp.bfloat16
AXES = ("img", "proto")

VMEM = pl.BlockSpec(memory_space=pltpu.VMEM)
HBM = pl.BlockSpec(memory_space=pltpu.HBM)


def call(body, outs, *args, flops=0, moved=0, exps=0, limit=24, specs=None, out_specs=None, scratch=()):
    return pl.pallas_call(
        body,
        out_shape=outs,
        in_specs=specs or [VMEM] * len(args),
        out_specs=out_specs or tuple(VMEM for _ in outs),
        scratch_shapes=scratch,
        compiler_params=pltpu.CompilerParams(vmem_limit_bytes=limit * 1024 * 1024),
        cost_estimate=pl.CostEstimate(flops=flops, bytes_accessed=moved, transcendentals=exps),
    )(*args)


def near(x):
    return pltpu.with_memory_space_constraint(x, pltpu.VMEM)


def far(x):
    return pltpu.with_memory_space_constraint(x, pltpu.HBM)


def dot(a, b, dims, precision=None):
    return lax.dot_general(a, b, (dims, ((), ())), precision=precision, preferred_element_type=F32)


def iota(shape, dim):
    return lax.broadcasted_iota(jnp.int32, shape, dim)


def add_all(parts):
    return functools.reduce(jnp.add, parts)


def widen(row):
    spare = -row.shape[1] % LANES
    return jnp.concatenate([row, jnp.zeros((1, spare), F32)], axis=1) if spare else row


def tiles_of(row):
    row = widen(row)
    return [row[:, i : i + LANES] for i in range(0, row.shape[1], LANES)]


def to_row(part):
    rows = part.shape[0]
    spare = -rows % LANES
    if spare:
        part = jnp.concatenate([part, jnp.zeros((spare, LANES), F32)], axis=0)
    return jnp.sum(part.T, axis=0, keepdims=True)[:, :rows]


def split(vector):
    high = vector.astype(BF16).astype(F32)
    return [high, vector - high]


def lay_out(vectors, lines, wide):
    tiles = tiles_of(jnp.concatenate(vectors, axis=1))
    tiles += [jnp.zeros((1, LANES), F32)] * (lines * wide // LANES - len(tiles))
    groups = [jnp.concatenate(tiles[g : g + lines], axis=0) for g in range(0, len(tiles), lines)]
    return jnp.concatenate(groups, axis=1)


def read_out(sums, rows, count):
    lines = sums.shape[0]
    turned = [sums[:, g : g + LANES].T for g in range(0, sums.shape[1], LANES)]

    def column(at, stop):
        parts = []
        while at < stop:
            line, lane = divmod(at, LANES)
            until = min(LANES, lane + stop - at)
            parts.append(turned[line // lines][lane:until, line % lines : line % lines + 1])
            at += until - lane
        return jnp.concatenate(parts, axis=0)

    return [jnp.broadcast_to(column(v * rows, (v + 1) * rows), (rows, LANES)) for v in range(count)]


def fold(x):
    return add_all([x[:, i : i + LANES] for i in range(0, x.shape[1], LANES)])


def spread(col, width):
    return jnp.concatenate([col] * (width // LANES), axis=1)


def chunks(columns, step=512):
    step = min(step, columns)
    return [slice(at, at + step) for at in range(0, columns, step)]


def over_chunks(columns, body, start):
    for at in chunks(columns):
        start = body(at, start)
    return start


def start_load(source, target, sems, first=0):
    copies = []
    for i, at in enumerate(chunks(target.shape[1])):
        place = source.at[:, first + at.start : first + at.stop]
        copies.append(pltpu.make_async_copy(place, target.at[:, at], sems.at[i]))
    for copy in copies:
        copy.start()
    return copies


def inverse_norms(w):
    w = w.astype(F32)
    return 1.0 / jnp.sqrt(jnp.sum(w * w, axis=0, keepdims=True) + NORM_EPS)


def odd_half():
    return lax.rem(lax.axis_index("proto"), 2)


def own_slots(mask_ref, feats_ref, own):
    patches = mask_ref.shape[1]
    slot = iota((own, patches), 0) + lax.axis_index("proto") * own
    mask = jnp.broadcast_to(mask_ref[...].astype(F32), (own, patches))
    upto = (iota((patches, patches), 0) <= iota((patches, patches), 1)).astype(BF16)
    rank = dot(mask.astype(BF16), upto, ((1,), (0,)))
    pick = jnp.where((rank == slot.astype(F32) + 1.0) & (mask > 0.5), 1.0, 0.0).astype(BF16)
    valid = slot[:, :1].astype(F32) < rank[:, patches - 1 :]
    rows = dot(pick, feats_ref[0], ((1,), (0,)))
    norm = jnp.sqrt(jnp.sum(rows * rows, axis=1, keepdims=True) + NORM_EPS)
    return (rows / norm).astype(BF16).astype(F32), norm, valid


def teacher_kernel(mask_hbm, stu_hbm, tea_hbm, w_hbm, sent_out, mask_out, stu_out, early_w, tea_ref, sems, w_sems):
    pairs = ((mask_hbm, mask_out), (tea_hbm, tea_ref), (stu_hbm, stu_out))
    copies = [pltpu.make_async_copy(*pair, sems.at[i]) for i, pair in enumerate(pairs)]
    for copy in copies:
        copy.start()
    loads = start_load(w_hbm, early_w, w_sems)
    for copy in copies[:2]:
        copy.wait()
    unit, _, valid = own_slots(mask_out, tea_ref, sent_out.shape[1])
    sent_out[...] = jnp.broadcast_to(jnp.where(valid, unit, EMPTY).astype(BF16)[None], sent_out.shape)
    for copy in copies[2:] + loads:
        copy.wait()


def norms_kernel(mask_ref, stu_ref, early_w, w_hbm, late_w, inv_out, unit_out, norm_out, sems):
    early = early_w.shape[1]
    copies = start_load(w_hbm, late_w, sems, early)
    unit, norm, _ = own_slots(mask_ref, stu_ref, unit_out.shape[0])
    unit_out[...] = unit
    norm_out[...] = jnp.broadcast_to(norm, norm_out.shape)
    for at in chunks(early):
        inv_out[:, at] = inverse_norms(early_w[:, at])
    for copy, at in zip(copies, chunks(late_w.shape[1])):
        copy.wait()
        inv_out[:, early + at.start : early + at.stop] = inverse_norms(late_w[:, at])


def in_order(mine, other, h):
    return jnp.where(odd_half() == h, mine, other)


def slot_flags(data):
    return jnp.where(data[:, :LANES].astype(F32) < 1.5, 1.0, 0.0).astype(BF16)


def packing(flags, hot_out):
    rows = hot_out.shape[0]
    half = flags[0].shape[0]
    step = min(256, half)
    before = jnp.zeros((1, 1), F32)
    upto = (iota((step, step), 0) <= iota((step, step), 1)).astype(BF16)
    same = (iota((step, step), 0) == iota((step, step), 1)).astype(BF16)
    row = iota((rows, step), 0).astype(F32) + 1.0
    for h in range(2):
        for c in range(0, half, step):
            part = flags[h][c : c + step]
            place = before + dot(part, upto, ((0,), (0,)))[:1]
            held = dot(part, same, ((0,), (0,)))[:1]
            hot = jnp.where((row == place) & (held > 0.5), 1.0, 0.0).astype(BF16)
            hot_out[:, h * half + c : h * half + c + step] = hot
            before = place[:, step - 1 :]


def blocks(half):
    step = min(256, half)
    return [(at, at + step) for at in range(0, half, step)]


def pack_rows(hot, read_mine, read_other, half):
    parts = []
    for start, stop in blocks(half):
        mine, other = read_mine(start, stop), read_other(start, stop)
        for h in range(2):
            parts.append(dot(hot[:, h * half + start : h * half + stop], in_order(mine, other, h), ((1,), (0,))))
    return add_all(parts).astype(BF16)


def quads(each, feat):
    return [(row, lane) for lane in range(0, feat, LANES) for row in range(0, each, QUAD)]


def first_kernel(mine, other, early_w, late_w, inv, unit, kernel_out, sent_out, hot_out):
    rows = kernel_out.shape[0]
    peers, _, groups, _, _ = sent_out.shape
    feat = late_w.shape[0]
    packing([slot_flags(in_order(mine[:, :LANES], other[:, :LANES], h)) for h in range(2)], hot_out)
    x = pack_rows(hot_out, lambda a, b: mine[a:b], lambda a, b: other[a:b], mine.shape[0])
    each = unit.shape[0] // 2
    for h in range(2):
        for g, (row, lane) in enumerate(quads(each, feat)):
            part = unit[h * each + row : h * each + row + QUAD, lane : lane + LANES]
            sent_out[:, h, g] = jnp.broadcast_to(part[None], (peers, QUAD, LANES)).astype(BF16)

    acc = jnp.zeros((rows, LANES), F32)
    for w, first in ((early_w, 0), (late_w, early_w.shape[1])):
        for part in chunks(w.shape[1]):
            at = slice(first + part.start, first + part.stop)
            z = dot(x, w[:, part], ((1,), (0,)))
            k = jnp.exp(z * (inv[:, at] * (1.0 / TEACHER_TEMP)))
            kernel_out[:, at] = k
            c = 1.0 / jnp.sum(k, axis=0, keepdims=True)
            acc = acc + fold(k * c)
    held = len(quads(each, feat))
    tiles = lay_out(split(widen(to_row(acc))), QUAD, (groups - held) * LANES)
    for g in range(groups - held):
        tile = tiles[:, g * LANES : (g + 1) * LANES]
        for h in range(2):
            sent_out[:, h, held + g] = jnp.broadcast_to(tile[None], (peers, QUAD, LANES)).astype(BF16)


def row_weights(mine, other, hot, own_out, weight_out, protos):
    devices = lax.axis_size(AXES)
    half = mine.shape[0]
    each = half // devices
    per_image = each * protos
    step = min(256, half)
    count, images = [], []
    block = iota((step, step), 0) // per_image
    same = (block == iota((step, step), 1) // per_image).astype(BF16)
    for c in range(0, half, step):
        flags = [slot_flags(ref[c : c + step, :LANES]).astype(F32) for ref in (mine, other)]
        held = dot(same, (flags[0] + flags[1]).astype(BF16), ((1,), (0,)))
        for h in range(2):
            count.append(dot(hot[:, h * half + c : h * half + c + step], held.astype(BF16), ((1,), (0,))))
        first = (iota(held.shape, 0) % per_image == 0) & (held > 0.5)
        images.append(jnp.sum(first.astype(F32), axis=0, keepdims=True))
    weight_out[...] = 1.0 / (jnp.maximum(add_all(count), 1.0) * add_all(images))

    own = own_out.shape[0]
    me = lax.axis_index("img") * protos + lax.axis_index("proto")
    q = iota((own, 2 * half), 0)
    spot = q // each * half + me * each + q % each
    mark = (iota((own, 2 * half), 1) == spot).astype(BF16)
    own_out[...] = dot(mark, hot[...], ((1,), (1,)))


def sweep_kernel(got, kernel, sent_out, *, held):
    rows, columns = kernel.shape
    sums = [jnp.sum(got[:, g].astype(F32), axis=0) for g in range(held, got.shape[1])]
    width = -(-rows // LANES) * LANES
    high, low = read_out(jnp.concatenate(sums, axis=1), width, 2)
    total = (high + low)[:rows]
    wide = spread(1.0 / total, chunks(columns)[0].stop)

    def body(at, acc):
        k = kernel[:, at]
        c = 1.0 / jnp.sum(k * wide, axis=0, keepdims=True)
        return acc + fold(k * c)

    acc = over_chunks(columns, body, jnp.zeros((rows, LANES), F32))
    tiles = jnp.concatenate(tiles_of(to_row(acc)), axis=0)
    sent_out[...] = jnp.broadcast_to(tiles[None], sent_out.shape)


def student_kernel(
    got,
    kernel,
    mine,
    other,
    hot,
    stu_w,
    inv_out,
    logits_out,
    scaled_out,
    xt_out,
    vectors_out,
    keep_out,
    give_out,
    stack,
):
    rows, columns = logits_out.shape
    feat = stu_w.shape[0]
    half = hot.shape[1] // 2
    each = half // lax.axis_size(AXES)

    def reader(ref):
        def read(start, stop):
            peers = slice(start // each, stop // each)
            parts = [ref[peers, g].astype(F32) for g in range(len(quads(each, feat)))]
            deep = each // QUAD
            lanes = [jnp.concatenate(parts[g : g + deep], axis=1) for g in range(0, len(parts), deep)]
            return jnp.concatenate([part.reshape(stop - start, LANES) for part in lanes], axis=1).astype(BF16)

        return read

    x = pack_rows(hot, reader(mine), reader(other), half)
    xt = x.astype(F32).T
    xt_out[...] = xt.astype(BF16)
    (total,) = read_out(jnp.sum(got[...], axis=0), rows, 1)
    wide = spread(1.0 / total, chunks(columns)[0].stop)

    def student(at, acc):
        w = stu_w[:, at]
        n = inv_out[:, at]
        l = dot(x, w, ((1,), (0,))) * (n * (1.0 / STUDENT_TEMP))
        logits_out[:, at] = l
        p = jnp.exp(l)
        stack[:rows, at] = (p * n).astype(BF16)
        return acc + fold(p)

    def sweep(at, acc):
        k = kernel[:, at]
        kc = k * (1.0 / jnp.sum(k * wide, axis=0, keepdims=True))
        scaled_out[:, at] = kc
        n = inverse_norms(stu_w[:, at])
        inv_out[:, at] = n
        stack[rows:, at] = (kc * n).astype(BF16)
        return acc + fold(kc)

    zero = jnp.zeros((rows, LANES), F32)
    total = over_chunks(columns, sweep, zero)
    part = over_chunks(columns, student, zero)
    sums = dot(stack[...], stu_w[...], ((1,), (1,)))
    for part_of, lanes in ((sums[:rows], slice(0, feat)), (sums[rows:], slice(feat, 2 * feat))):
        keep_out[:, lanes] = part_of
        give_out[:, lanes] = part_of.astype(BF16)
    cross = to_row(fold(sums[rows:] * x.astype(F32))) * (1.0 / STUDENT_TEMP)
    vectors_out[...] = lay_out([to_row(part), to_row(total), cross], *vectors_out.shape)


def prepare_kernel(
    scaled, logits, inv, mine, other, hot, pull_out, push_out, own_out, weight_out, *, scale, protos
):
    rows, columns = scaled.shape
    row_weights(mine, other, hot, own_out, weight_out, protos)
    factor = spread(weight_out[...] * (rows / STUDENT_TEMP), chunks(columns)[0].stop)

    def body(at, _):
        n = inv[:, at] * scale
        pull_out[:, at] = factor * jnp.exp(logits[:, at]) * n
        push_out[:, at] = factor * scaled[:, at] * n
        return 0

    over_chunks(columns, body, 0)


def fill_kernel(keep, give, hot, vectors, sent_out):
    devices, groups, _, _ = sent_out.shape
    half, both = hot.shape[1] // 2, keep.shape[1]
    each = half // devices
    pair = (keep[...] + give[...].astype(F32)).astype(BF16)
    places = quads(each, both)
    for start, stop in blocks(half):
        own = jnp.where(odd_half() == 1, hot[:, half + start : half + stop], hot[:, start:stop])
        slots = dot(own, pair, ((0,), (0,)))
        peers = slice(start // each, stop // each)
        for g, (row, lane) in enumerate(places):
            part = slots[:, lane : lane + LANES].reshape((stop - start) // each, each, LANES)
            sent_out[peers, g] = part[:, row : row + QUAD].astype(BF16)
    for g in range(len(places), groups):
        at = (g - len(places)) * LANES
        sent_out[:, g] = jnp.broadcast_to(vectors[:, at : at + LANES][None], (devices, QUAD, LANES)).astype(BF16)


def slots_of(got, each, both):
    sums = [jnp.sum(got[:, :, g].astype(F32), axis=0) for g in range(len(quads(each, both)))]
    deep = each // QUAD
    lanes = [
        jnp.concatenate([sums[g + i][h] for h in range(2) for i in range(deep)], axis=0) for g in range(0, len(sums), deep)
    ]
    return jnp.concatenate(lanes, axis=1)


def final_kernel(
    got,
    pull,
    push,
    logits,
    inv,
    stu_w,
    xt,
    weight,
    own,
    unit,
    norm,
    out_hbm,
    rows_hbm,
    loss_hbm,
    out,
    rows_out,
    loss_out,
    sems,
):
    rows, columns = pull.shape
    feat = xt.shape[0]
    each = unit.shape[0] // 2
    held = len(quads(each, 2 * feat))
    sums = [jnp.sum(got[:, :, g].astype(F32), axis=(0, 1)) for g in range(held, got.shape[2])]
    partition, total, cross = read_out(jnp.concatenate(sums, axis=1), rows, 3)
    parts = chunks(columns, 256)
    raise_by, lower_by = 1.0 / partition, 1.0 / total
    grow, shrink = spread(raise_by, parts[0].stop), spread(lower_by, parts[0].stop)
    copies = []

    def send(source, target):
        copies.append(pltpu.make_async_copy(source, target, sems.at[len(copies)]))
        copies[-1].start()

    def gradient(at):
        g = grow * pull[:, at] - shrink * push[:, at]
        along = jnp.sum(g * logits[:, at], axis=0, keepdims=True) * (inv[:, at] * STUDENT_TEMP)
        return g.astype(BF16), along

    ready = gradient(parts[0])
    for at, following in zip(parts, parts[1:] + [None]):
        g, along = ready
        direct = dot(xt[...], g, ((1,), (0,)))
        if following is not None:
            ready = gradient(following)
        out[:, at] = direct - stu_w[:, at].astype(F32) * along
        send(out.at[:, at], out_hbm.at[:, at])
    share = weight[...]
    loss = jnp.sum(share * (jnp.log(partition) - cross * lower_by), axis=0, keepdims=True)
    loss_out[...] = loss[:, :1]
    send(loss_out, loss_hbm)
    factors = jnp.concatenate([raise_by, lower_by], axis=1) * spread(share * (rows / STUDENT_TEMP), 2 * LANES)
    scale = dot(own[...], factors, ((1,), (0,)), lax.Precision.HIGHEST)
    sums = slots_of(got, each, 2 * feat)
    full = sums[:, :feat] * scale[:, :1] - sums[:, feat:] * scale[:, LANES : LANES + 1]
    u = unit[...]
    rows_out[...] = (full - u * jnp.sum(u * full, axis=1, keepdims=True)) / norm[:, :1]
    send(rows_out, rows_hbm)
    for copy in copies:
        copy.wait()


def shards(student_feats, teacher_feats, student_weight, teacher_weight, patch_masks):
    devices = lax.axis_size(AXES)
    protos = lax.axis_size("proto")
    images, patches, feat = student_feats.shape
    assert images == 1 and protos % 2 == 0
    columns = student_weight.shape[1]
    own = patches // 2 // protos
    each = own // 2
    half = each * devices
    rows = 2 * half * 5 // 16
    tiles = -(-rows // LANES)
    spare = lambda parts: -(-parts * rows // (QUAD * LANES))
    held = len(quads(each, feat))
    big = rows * columns
    exchange = functools.partial(lax.all_to_all, axis_name=AXES, split_axis=0, concat_axis=0)
    swap = functools.partial(lax.ppermute, axis_name="proto", perm=[(p, p ^ 1) for p in range(protos)])
    matrix = pltpu.VMEM((rows, columns), F32)
    column = pltpu.VMEM((rows, LANES), F32)
    line = pltpu.VMEM((1, columns), F32)

    flags = pltpu.VMEM(patch_masks.shape, patch_masks.dtype)
    feats = pltpu.VMEM(student_feats.shape, BF16)
    early = columns * 3 // 8 // LANES * LANES
    early_w, late_w = pltpu.VMEM((feat, early), BF16), pltpu.VMEM((feat, columns - early), BF16)
    sent, flags, feats, early_w = call(
        teacher_kernel,
        (pltpu.VMEM((devices // 2, own, feat), BF16), flags, feats, early_w),
        far(patch_masks),
        far(student_feats),
        far(teacher_feats),
        far(teacher_weight),
        specs=[HBM] * 4,
        scratch=[feats, pltpu.SemaphoreType.DMA((3,)), pltpu.SemaphoreType.DMA((len(chunks(early)),))],
    )
    mine = exchange(sent.reshape(devices, each, feat)).reshape(half, feat)
    mine, teacher_weight = lax.optimization_barrier((mine, teacher_weight))
    other = near(swap(mine))
    mine = near(mine)
    late_w, tea_inv, unit, norm = call(
        norms_kernel,
        (
            late_w,
            line,
            pltpu.VMEM((own, feat), F32),
            pltpu.VMEM((own, LANES), F32),
        ),
        flags,
        feats,
        early_w,
        far(teacher_weight),
        flops=2 * feat * columns,
        moved=4 * feat * columns,
        specs=[VMEM, VMEM, VMEM, HBM],
        scratch=[pltpu.SemaphoreType.DMA((len(chunks(columns - early)),))],
    )
    kernel, sent, hot = call(
        first_kernel,
        (
            matrix,
            pltpu.VMEM((devices // 2, 2, held + -(-2 * tiles // QUAD), QUAD, LANES), BF16),
            pltpu.VMEM((rows, 2 * half), BF16),
        ),
        mine,
        other,
        early_w,
        late_w,
        tea_inv,
        unit,
        flops=2 * big * feat,
        moved=4 * big,
        exps=big,
    )
    stu_mine = exchange(sent.reshape(devices, *sent.shape[2:]))
    stu_other = near(swap(stu_mine))
    stu_mine = near(stu_mine)
    (sent,) = call(
        functools.partial(sweep_kernel, held=held),
        (pltpu.VMEM((devices, tiles, LANES), F32),),
        stu_mine,
        kernel,
        flops=4 * big,
        moved=4 * big,
    )
    got = near(exchange(sent))
    stu_inv, logits, scaled, xt, sums, keep, give = call(
        student_kernel,
        (
            line,
            matrix,
            matrix,
            pltpu.VMEM((feat, rows), BF16),
            pltpu.VMEM((QUAD, spare(3) * LANES), F32),
            pltpu.VMEM((rows, 2 * feat), F32),
            pltpu.VMEM((rows, 2 * feat), BF16),
        ),
        got,
        kernel,
        stu_mine,
        stu_other,
        hot,
        student_weight,
        flops=6 * big * feat,
        moved=12 * big,
        exps=big,
        scratch=[pltpu.VMEM((2 * rows, columns), BF16)],
        limit=22 + half // 112,
    )
    give = near(swap(give))
    pull, push, own_hot, weight = call(
        functools.partial(prepare_kernel, scale=columns * devices * GRAD_SCALE, protos=protos),
        (matrix, matrix, pltpu.VMEM((own, rows), F32), column),
        scaled,
        logits,
        stu_inv,
        mine,
        other,
        hot,
        flops=4 * big,
        moved=16 * big,
        exps=big,
    )
    keep, pull, push, own_hot, weight = lax.optimization_barrier((keep, pull, push, own_hot, weight))
    payload = pltpu.VMEM((devices, 2 * held + spare(3), QUAD, LANES), BF16)
    (sent,) = call(fill_kernel, (payload,), keep, give, hot, sums)
    got = exchange(sent)
    got = near(got.reshape(devices // 2, 2, *got.shape[1:]))
    grad_weight, grad_rows, loss = call(
        final_kernel,
        (
            jax.ShapeDtypeStruct((feat, columns), F32),
            jax.ShapeDtypeStruct((own, feat), F32),
            jax.ShapeDtypeStruct((1, 1), F32),
        ),
        got,
        pull,
        push,
        logits,
        stu_inv,
        student_weight,
        xt,
        weight,
        own_hot,
        unit,
        norm,
        flops=2 * big * feat,
        moved=8 * feat * columns,
        out_specs=(HBM, HBM, HBM),
        scratch=[
            pltpu.VMEM((feat, columns), F32),
            pltpu.VMEM((own, feat), F32),
            pltpu.VMEM((1, 1), F32),
            pltpu.SemaphoreType.DMA((len(chunks(columns, 256)) + 2,)),
        ],
    )
    return loss.reshape(()), grad_weight, grad_rows


def solution(mesh):
    placed = (
        P("img", None, None),
        P("img", None, None),
        P(None, AXES),
        P(None, AXES),
        P("img", None),
    )
    return jax.shard_map(
        shards,
        mesh=mesh,
        in_specs=placed,
        out_specs=(P(), P(None, AXES), P(AXES, None)),
        check_vma=False,
    )
```

```python
import functools

import jax
import jax.numpy as jnp
from jax import lax
from jax.experimental import pallas as pl
from jax.experimental.pallas import tpu as pltpu
from jax.sharding import PartitionSpec as P

ITERS = 3
TEACHER_TEMP = 0.07
STUDENT_TEMP = 0.1
NORM_EPS = 1e-06
GRAD_SCALE = 1.0 / 128.0
EMPTY = 2.0
LANES = 128
QUAD = 4
F32 = jnp.float32
BF16 = jnp.bfloat16
AXES = ("img", "proto")

VMEM = pl.BlockSpec(memory_space=pltpu.VMEM)
HBM = pl.BlockSpec(memory_space=pltpu.HBM)


def call(body, outs, *args, flops=0, moved=0, exps=0, limit=24, specs=None, out_specs=None, scratch=()):
    return pl.pallas_call(
        body,
        out_shape=outs,
        in_specs=specs or [VMEM] * len(args),
        out_specs=out_specs or tuple(VMEM for _ in outs),
        scratch_shapes=scratch,
        compiler_params=pltpu.CompilerParams(vmem_limit_bytes=limit * 1024 * 1024),
        cost_estimate=pl.CostEstimate(flops=flops, bytes_accessed=moved, transcendentals=exps),
    )(*args)


def near(x):
    return pltpu.with_memory_space_constraint(x, pltpu.VMEM)


def far(x):
    return pltpu.with_memory_space_constraint(x, pltpu.HBM)


def dot(a, b, dims, precision=None):
    return lax.dot_general(a, b, (dims, ((), ())), precision=precision, preferred_element_type=F32)


def iota(shape, dim):
    return lax.broadcasted_iota(jnp.int32, shape, dim)


def add_all(parts):
    return functools.reduce(jnp.add, parts)


def widen(row):
    spare = -row.shape[1] % LANES
    return jnp.concatenate([row, jnp.zeros((1, spare), F32)], axis=1) if spare else row


def tiles_of(row):
    row = widen(row)
    return [row[:, i : i + LANES] for i in range(0, row.shape[1], LANES)]


def to_row(part):
    rows = part.shape[0]
    spare = -rows % LANES
    if spare:
        part = jnp.concatenate([part, jnp.zeros((spare, LANES), F32)], axis=0)
    return jnp.sum(part.T, axis=0, keepdims=True)[:, :rows]


def split(vector):
    high = vector.astype(BF16).astype(F32)
    return [high, vector - high]


def lay_out(vectors, lines, wide):
    tiles = tiles_of(jnp.concatenate(vectors, axis=1))
    tiles += [jnp.zeros((1, LANES), F32)] * (lines * wide // LANES - len(tiles))
    groups = [jnp.concatenate(tiles[g : g + lines], axis=0) for g in range(0, len(tiles), lines)]
    return jnp.concatenate(groups, axis=1)


def read_out(sums, rows, count):
    lines = sums.shape[0]
    turned = [sums[:, g : g + LANES].T for g in range(0, sums.shape[1], LANES)]

    def column(at, stop):
        parts = []
        while at < stop:
            line, lane = divmod(at, LANES)
            until = min(LANES, lane + stop - at)
            parts.append(turned[line // lines][lane:until, line % lines : line % lines + 1])
            at += until - lane
        return jnp.concatenate(parts, axis=0)

    return [jnp.broadcast_to(column(v * rows, (v + 1) * rows), (rows, LANES)) for v in range(count)]


def fold(x):
    return add_all([x[:, i : i + LANES] for i in range(0, x.shape[1], LANES)])


def spread(col, width):
    return jnp.concatenate([col] * (width // LANES), axis=1)


def chunks(columns, step=512):
    step = min(step, columns)
    return [slice(at, at + step) for at in range(0, columns, step)]


def over_chunks(columns, body, start):
    for at in chunks(columns):
        start = body(at, start)
    return start


def start_load(source, target, sems, first=0):
    copies = []
    for i, at in enumerate(chunks(target.shape[1])):
        place = source.at[:, first + at.start : first + at.stop]
        copies.append(pltpu.make_async_copy(place, target.at[:, at], sems.at[i]))
    for copy in copies:
        copy.start()
    return copies


def inverse_norms(w):
    w = w.astype(F32)
    return 1.0 / jnp.sqrt(jnp.sum(w * w, axis=0, keepdims=True) + NORM_EPS)


def odd_half():
    return lax.rem(lax.axis_index("proto"), 2)


def own_slots(mask_ref, feats_ref, own):
    patches = mask_ref.shape[1]
    slot = iota((own, patches), 0) + lax.axis_index("proto") * own
    mask = jnp.broadcast_to(mask_ref[...].astype(F32), (own, patches))
    upto = (iota((patches, patches), 0) <= iota((patches, patches), 1)).astype(BF16)
    rank = dot(mask.astype(BF16), upto, ((1,), (0,)))
    pick = jnp.where((rank == slot.astype(F32) + 1.0) & (mask > 0.5), 1.0, 0.0).astype(BF16)
    valid = slot[:, :1].astype(F32) < rank[:, patches - 1 :]
    rows = dot(pick, feats_ref[0], ((1,), (0,)))
    norm = jnp.sqrt(jnp.sum(rows * rows, axis=1, keepdims=True) + NORM_EPS)
    return (rows / norm).astype(BF16).astype(F32), norm, valid


def teacher_kernel(mask_hbm, stu_hbm, tea_hbm, w_hbm, sent_out, mask_out, stu_out, early_w, tea_ref, sems, w_sems):
    pairs = ((mask_hbm, mask_out), (tea_hbm, tea_ref), (stu_hbm, stu_out))
    copies = [pltpu.make_async_copy(*pair, sems.at[i]) for i, pair in enumerate(pairs)]
    for copy in copies:
        copy.start()
    loads = start_load(w_hbm, early_w, w_sems)
    for copy in copies[:2]:
        copy.wait()
    unit, _, valid = own_slots(mask_out, tea_ref, sent_out.shape[1])
    sent_out[...] = jnp.broadcast_to(jnp.where(valid, unit, EMPTY).astype(BF16)[None], sent_out.shape)
    for copy in copies[2:] + loads:
        copy.wait()


def norms_kernel(mine, mask_ref, stu_ref, early_w, w_hbm, late_w, inv_out, unit_out, norm_out, hot_out, sems):
    early = early_w.shape[1]
    copies = start_load(w_hbm, late_w, sems, early)
    packing([slot_flags(mine[:, :LANES])] * 2, hot_out)
    unit, norm, _ = own_slots(mask_ref, stu_ref, unit_out.shape[0])
    unit_out[...] = unit
    norm_out[...] = jnp.broadcast_to(norm, norm_out.shape)
    for at in chunks(early):
        inv_out[:, at] = inverse_norms(early_w[:, at])
    for copy, at in zip(copies, chunks(late_w.shape[1])):
        copy.wait()
        inv_out[:, early + at.start : early + at.stop] = inverse_norms(late_w[:, at])


def in_order(mine, other, h):
    return jnp.where(odd_half() == h, mine, other)


def slot_flags(data):
    return jnp.where(data[:, :LANES].astype(F32) < 1.5, 1.0, 0.0).astype(BF16)


def packing(flags, hot_out):
    rows = hot_out.shape[0]
    half = flags[0].shape[0]
    step = min(256, half)
    before = jnp.zeros((1, 1), F32)
    upto = (iota((step, step), 0) <= iota((step, step), 1)).astype(BF16)
    same = (iota((step, step), 0) == iota((step, step), 1)).astype(BF16)
    row = iota((rows, step), 0).astype(F32) + 1.0
    for h in range(2):
        for c in range(0, half, step):
            part = flags[h][c : c + step]
            place = before + dot(part, upto, ((0,), (0,)))[:1]
            held = dot(part, same, ((0,), (0,)))[:1]
            hot = jnp.where((row == place) & (held > 0.5), 1.0, 0.0).astype(BF16)
            hot_out[:, h * half + c : h * half + c + step] = hot
            before = place[:, step - 1 :]


def blocks(half):
    step = min(256, half)
    return [(at, at + step) for at in range(0, half, step)]


def pack_rows(hot, read_mine, read_other, half):
    parts = []
    for start, stop in blocks(half):
        mine, other = read_mine(start, stop), read_other(start, stop)
        for h in range(2):
            parts.append(dot(hot[:, h * half + start : h * half + stop], in_order(mine, other, h), ((1,), (0,))))
    return add_all(parts).astype(BF16)


def quads(each, feat):
    return [(row, lane) for lane in range(0, feat, LANES) for row in range(0, each, QUAD)]


def first_kernel(mine, other, early_w, late_w, inv, unit, hot, kernel_out, sent_out):
    rows = kernel_out.shape[0]
    peers, _, groups, _, _ = sent_out.shape
    feat = late_w.shape[0]
    x = pack_rows(hot, lambda a, b: mine[a:b], lambda a, b: other[a:b], mine.shape[0])
    each = unit.shape[0] // 2
    for h in range(2):
        for g, (row, lane) in enumerate(quads(each, feat)):
            part = unit[h * each + row : h * each + row + QUAD, lane : lane + LANES]
            sent_out[:, h, g] = jnp.broadcast_to(part[None], (peers, QUAD, LANES)).astype(BF16)

    acc = jnp.zeros((rows, LANES), F32)
    for w, first in ((early_w, 0), (late_w, early_w.shape[1])):
        for part in chunks(w.shape[1]):
            at = slice(first + part.start, first + part.stop)
            z = dot(x, w[:, part], ((1,), (0,)))
            k = jnp.exp(z * (inv[:, at] * (1.0 / TEACHER_TEMP)))
            kernel_out[:, at] = k
            c = 1.0 / jnp.sum(k, axis=0, keepdims=True)
            acc = acc + fold(k * c)
    held = len(quads(each, feat))
    tiles = lay_out(split(widen(to_row(acc))), QUAD, (groups - held) * LANES)
    for g in range(groups - held):
        tile = tiles[:, g * LANES : (g + 1) * LANES]
        for h in range(2):
            sent_out[:, h, held + g] = jnp.broadcast_to(tile[None], (peers, QUAD, LANES)).astype(BF16)


def row_weights(mine, other, hot, own_out, weight_out, protos):
    devices = lax.axis_size(AXES)
    half = mine.shape[0]
    each = half // devices
    per_image = each * protos
    step = min(256, half)
    count, images = [], []
    block = iota((step, step), 0) // per_image
    same = (block == iota((step, step), 1) // per_image).astype(BF16)
    for c in range(0, half, step):
        flags = [slot_flags(ref[c : c + step, :LANES]).astype(F32) for ref in (mine, other)]
        held = dot(same, (flags[0] + flags[1]).astype(BF16), ((1,), (0,)))
        for h in range(2):
            count.append(dot(hot[:, h * half + c : h * half + c + step], held.astype(BF16), ((1,), (0,))))
        first = (iota(held.shape, 0) % per_image == 0) & (held > 0.5)
        images.append(jnp.sum(first.astype(F32), axis=0, keepdims=True))
    weight_out[...] = 1.0 / (jnp.maximum(add_all(count), 1.0) * add_all(images))

    own = own_out.shape[0]
    me = lax.axis_index("img") * protos + lax.axis_index("proto")
    q = iota((own, 2 * half), 0)
    spot = q // each * half + me * each + q % each
    mark = (iota((own, 2 * half), 1) == spot).astype(BF16)
    own_out[...] = dot(mark, hot[...], ((1,), (1,)))


def sweep_kernel(got, kernel, sent_out, *, held):
    rows, columns = kernel.shape
    sums = [jnp.sum(got[:, g].astype(F32), axis=0) for g in range(held, got.shape[1])]
    width = -(-rows // LANES) * LANES
    high, low = read_out(jnp.concatenate(sums, axis=1), width, 2)
    total = (high + low)[:rows]
    wide = spread(1.0 / total, chunks(columns)[0].stop)

    def body(at, acc):
        k = kernel[:, at]
        c = 1.0 / jnp.sum(k * wide, axis=0, keepdims=True)
        return acc + fold(k * c)

    acc = over_chunks(columns, body, jnp.zeros((rows, LANES), F32))
    tiles = jnp.concatenate(tiles_of(to_row(acc)), axis=0)
    sent_out[...] = jnp.broadcast_to(tiles[None], sent_out.shape)


def student_kernel(
    got,
    kernel,
    mine,
    other,
    hot,
    stu_w,
    inv_out,
    logits_out,
    scaled_out,
    xt_out,
    vectors_out,
    keep_out,
    give_out,
    stack,
):
    rows, columns = logits_out.shape
    feat = stu_w.shape[0]
    half = hot.shape[1] // 2
    each = half // lax.axis_size(AXES)

    def reader(ref):
        def read(start, stop):
            peers = slice(start // each, stop // each)
            parts = [ref[peers, g].astype(F32) for g in range(len(quads(each, feat)))]
            deep = each // QUAD
            lanes = [jnp.concatenate(parts[g : g + deep], axis=1) for g in range(0, len(parts), deep)]
            return jnp.concatenate([part.reshape(stop - start, LANES) for part in lanes], axis=1).astype(BF16)

        return read

    x = pack_rows(hot, reader(mine), reader(other), half)
    xt = x.astype(F32).T
    xt_out[...] = xt.astype(BF16)
    (total,) = read_out(jnp.sum(got[...], axis=0), rows, 1)
    wide = spread(1.0 / total, chunks(columns)[0].stop)

    def student(at, acc):
        w = stu_w[:, at]
        n = inv_out[:, at]
        l = dot(x, w, ((1,), (0,))) * (n * (1.0 / STUDENT_TEMP))
        logits_out[:, at] = l
        p = jnp.exp(l)
        stack[:rows, at] = (p * n).astype(BF16)
        return acc + fold(p)

    def sweep(at, acc):
        k = kernel[:, at]
        kc = k * (1.0 / jnp.sum(k * wide, axis=0, keepdims=True))
        scaled_out[:, at] = kc
        n = inverse_norms(stu_w[:, at])
        inv_out[:, at] = n
        stack[rows:, at] = (kc * n).astype(BF16)
        return acc + fold(kc)

    zero = jnp.zeros((rows, LANES), F32)
    total = over_chunks(columns, sweep, zero)
    part = over_chunks(columns, student, zero)
    sums = dot(stack[...], stu_w[...], ((1,), (1,)))
    for part_of, lanes in ((sums[:rows], slice(0, feat)), (sums[rows:], slice(feat, 2 * feat))):
        keep_out[:, lanes] = part_of
        give_out[:, lanes] = part_of.astype(BF16)
    cross = to_row(fold(sums[rows:] * x.astype(F32))) * (1.0 / STUDENT_TEMP)
    vectors_out[...] = lay_out([to_row(part), to_row(total), cross], *vectors_out.shape)


def prepare_kernel(
    scaled, logits, inv, mine, other, hot, pull_out, push_out, own_out, weight_out, spots_out, *, scale, protos
):
    rows, columns = scaled.shape
    row_weights(mine, other, hot, own_out, weight_out, protos)
    half = spots_out.shape[0]
    for start, stop in blocks(half):
        own = jnp.where(odd_half() == 1, hot[:, half + start : half + stop], hot[:, start:stop])
        spots_out[start:stop] = own.astype(F32).T.astype(BF16)
    factor = spread(weight_out[...] * (rows / STUDENT_TEMP), chunks(columns)[0].stop)

    def body(at, _):
        n = inv[:, at] * scale
        pull_out[:, at] = factor * jnp.exp(logits[:, at]) * n
        push_out[:, at] = factor * scaled[:, at] * n
        return 0

    over_chunks(columns, body, 0)


def fill_kernel(keep, give, hot, vectors, sent_out):
    devices, groups, _, _ = sent_out.shape
    half, both = hot.shape[0], keep.shape[1]
    each = half // devices
    pair = (keep[...] + give[...].astype(F32)).astype(BF16)
    places = quads(each, both)
    for start, stop in blocks(half):
        slots = dot(hot[start:stop], pair, ((1,), (0,)))
        peers = slice(start // each, stop // each)
        for g, (row, lane) in enumerate(places):
            part = slots[:, lane : lane + LANES].reshape((stop - start) // each, each, LANES)
            sent_out[peers, g] = part[:, row : row + QUAD].astype(BF16)
    for g in range(len(places), groups):
        at = (g - len(places)) * LANES
        sent_out[:, g] = jnp.broadcast_to(vectors[:, at : at + LANES][None], (devices, QUAD, LANES)).astype(BF16)


def slots_of(got, each, both):
    sums = [jnp.sum(got[:, :, g].astype(F32), axis=0) for g in range(len(quads(each, both)))]
    deep = each // QUAD
    lanes = [
        jnp.concatenate([sums[g + i][h] for h in range(2) for i in range(deep)], axis=0) for g in range(0, len(sums), deep)
    ]
    return jnp.concatenate(lanes, axis=1)


def final_kernel(
    got,
    pull,
    push,
    logits,
    inv,
    stu_w,
    xt,
    weight,
    own,
    unit,
    norm,
    out_hbm,
    rows_hbm,
    loss_hbm,
    out,
    rows_out,
    loss_out,
    sems,
):
    rows, columns = pull.shape
    feat = xt.shape[0]
    each = unit.shape[0] // 2
    held = len(quads(each, 2 * feat))
    sums = [jnp.sum(got[:, :, g].astype(F32), axis=(0, 1)) for g in range(held, got.shape[2])]
    partition, total, cross = read_out(jnp.concatenate(sums, axis=1), rows, 3)
    parts = chunks(columns, 256)
    raise_by, lower_by = 1.0 / partition, 1.0 / total
    grow, shrink = spread(raise_by, parts[0].stop), spread(lower_by, parts[0].stop)
    copies = []

    def send(source, target):
        copies.append(pltpu.make_async_copy(source, target, sems.at[len(copies)]))
        copies[-1].start()

    def gradient(at):
        g = grow * pull[:, at] - shrink * push[:, at]
        along = jnp.sum(g * logits[:, at], axis=0, keepdims=True) * (inv[:, at] * STUDENT_TEMP)
        return g.astype(BF16), along

    ready = gradient(parts[0])
    for at, following in zip(parts, parts[1:] + [None]):
        g, along = ready
        direct = dot(xt[...], g, ((1,), (0,)))
        if following is not None:
            ready = gradient(following)
        out[:, at] = direct - stu_w[:, at].astype(F32) * along
        send(out.at[:, at], out_hbm.at[:, at])
    share = weight[...]
    loss = jnp.sum(share * (jnp.log(partition) - cross * lower_by), axis=0, keepdims=True)
    loss_out[...] = loss[:, :1]
    send(loss_out, loss_hbm)
    factors = jnp.concatenate([raise_by, lower_by], axis=1) * spread(share * (rows / STUDENT_TEMP), 2 * LANES)
    scale = dot(own[...], factors, ((1,), (0,)), lax.Precision.HIGHEST)
    sums = slots_of(got, each, 2 * feat)
    full = sums[:, :feat] * scale[:, :1] - sums[:, feat:] * scale[:, LANES : LANES + 1]
    u = unit[...]
    rows_out[...] = (full - u * jnp.sum(u * full, axis=1, keepdims=True)) / norm[:, :1]
    send(rows_out, rows_hbm)
    for copy in copies:
        copy.wait()


def shards(student_feats, teacher_feats, student_weight, teacher_weight, patch_masks):
    devices = lax.axis_size(AXES)
    protos = lax.axis_size("proto")
    images, patches, feat = student_feats.shape
    assert images == 1 and protos % 2 == 0
    columns = student_weight.shape[1]
    own = patches // 2 // protos
    assert patches // 8 % own == 0
    each = own // 2
    half = each * devices
    rows = 2 * half * 5 // 16
    tiles = -(-rows // LANES)
    spare = lambda parts: -(-parts * rows // (QUAD * LANES))
    held = len(quads(each, feat))
    big = rows * columns
    exchange = functools.partial(lax.all_to_all, axis_name=AXES, split_axis=0, concat_axis=0)
    swap = functools.partial(lax.ppermute, axis_name="proto", perm=[(p, p ^ 1) for p in range(protos)])
    matrix = pltpu.VMEM((rows, columns), F32)
    column = pltpu.VMEM((rows, LANES), F32)
    line = pltpu.VMEM((1, columns), F32)

    flags = pltpu.VMEM(patch_masks.shape, patch_masks.dtype)
    feats = pltpu.VMEM(student_feats.shape, BF16)
    early = columns * 3 // 8 // LANES * LANES
    early_w, late_w = pltpu.VMEM((feat, early), BF16), pltpu.VMEM((feat, columns - early), BF16)
    sent, flags, feats, early_w = call(
        teacher_kernel,
        (pltpu.VMEM((devices // 2, own, feat), BF16), flags, feats, early_w),
        far(patch_masks),
        far(student_feats),
        far(teacher_feats),
        far(teacher_weight),
        specs=[HBM] * 4,
        scratch=[feats, pltpu.SemaphoreType.DMA((3,)), pltpu.SemaphoreType.DMA((len(chunks(early)),))],
    )
    mine = exchange(sent.reshape(devices, each, feat)).reshape(half, feat)
    mine, teacher_weight = lax.optimization_barrier((mine, teacher_weight))
    other = near(swap(mine))
    mine = near(mine)
    late_w, tea_inv, unit, norm, hot = call(
        norms_kernel,
        (
            late_w,
            line,
            pltpu.VMEM((own, feat), F32),
            pltpu.VMEM((own, LANES), F32),
            pltpu.VMEM((rows, 2 * half), BF16),
        ),
        mine,
        flags,
        feats,
        early_w,
        far(teacher_weight),
        flops=2 * feat * columns,
        moved=4 * feat * columns,
        specs=[VMEM, VMEM, VMEM, VMEM, HBM],
        scratch=[pltpu.SemaphoreType.DMA((len(chunks(columns - early)),))],
    )
    kernel, sent = call(
        first_kernel,
        (
            matrix,
            pltpu.VMEM((devices // 2, 2, held + -(-2 * tiles // QUAD), QUAD, LANES), BF16),
        ),
        mine,
        other,
        early_w,
        late_w,
        tea_inv,
        unit,
        hot,
        flops=2 * big * feat,
        moved=4 * big,
        exps=big,
    )
    stu_mine = exchange(sent.reshape(devices, *sent.shape[2:]))
    stu_other = near(swap(stu_mine))
    stu_mine = near(stu_mine)
    (sent,) = call(
        functools.partial(sweep_kernel, held=held),
        (pltpu.VMEM((devices, tiles, LANES), F32),),
        stu_mine,
        kernel,
        flops=4 * big,
        moved=4 * big,
    )
    got = near(exchange(sent))
    stu_inv, logits, scaled, xt, sums, keep, give = call(
        student_kernel,
        (
            line,
            matrix,
            matrix,
            pltpu.VMEM((feat, rows), BF16),
            pltpu.VMEM((QUAD, spare(3) * LANES), F32),
            pltpu.VMEM((rows, 2 * feat), F32),
            pltpu.VMEM((rows, 2 * feat), BF16),
        ),
        got,
        kernel,
        stu_mine,
        stu_other,
        hot,
        student_weight,
        flops=6 * big * feat,
        moved=12 * big,
        exps=big,
        scratch=[pltpu.VMEM((2 * rows, columns), BF16)],
        limit=22 + half // 112,
    )
    give = near(swap(give))
    pull, push, own_hot, weight, spots = call(
        functools.partial(prepare_kernel, scale=columns * devices * GRAD_SCALE, protos=protos),
        (matrix, matrix, pltpu.VMEM((own, rows), F32), column, pltpu.VMEM((half, rows), BF16)),
        scaled,
        logits,
        stu_inv,
        mine,
        other,
        hot,
        flops=4 * big,
        moved=16 * big,
        exps=big,
    )
    keep, pull, push, own_hot, weight = lax.optimization_barrier((keep, pull, push, own_hot, weight))
    payload = pltpu.VMEM((devices, 2 * held + spare(3), QUAD, LANES), BF16)
    (sent,) = call(fill_kernel, (payload,), keep, give, spots, sums)
    got = exchange(sent)
    got = near(got.reshape(devices // 2, 2, *got.shape[1:]))
    grad_weight, grad_rows, loss = call(
        final_kernel,
        (
            jax.ShapeDtypeStruct((feat, columns), F32),
            jax.ShapeDtypeStruct((own, feat), F32),
            jax.ShapeDtypeStruct((1, 1), F32),
        ),
        got,
        pull,
        push,
        logits,
        stu_inv,
        student_weight,
        xt,
        weight,
        own_hot,
        unit,
        norm,
        flops=2 * big * feat,
        moved=8 * feat * columns,
        out_specs=(HBM, HBM, HBM),
        scratch=[
            pltpu.VMEM((feat, columns), F32),
            pltpu.VMEM((own, feat), F32),
            pltpu.VMEM((1, 1), F32),
            pltpu.SemaphoreType.DMA((len(chunks(columns, 256)) + 2,)),
        ],
    )
    return loss.reshape(()), grad_weight, grad_rows


def solution(mesh):
    placed = (
        P("img", None, None),
        P("img", None, None),
        P(None, AXES),
        P(None, AXES),
        P("img", None),
    )
    return jax.shard_map(
        shards,
        mesh=mesh,
        in_specs=placed,
        out_specs=(P(), P(None, AXES), P(AXES, None)),
        check_vma=False,
    )
```

```python
import functools

import jax
import jax.numpy as jnp
from jax import lax
from jax.experimental import pallas as pl
from jax.experimental.pallas import tpu as pltpu
from jax.sharding import PartitionSpec as P

ITERS = 3
TEACHER_TEMP = 0.07
STUDENT_TEMP = 0.1
NORM_EPS = 1e-06
GRAD_SCALE = 1.0 / 128.0
EMPTY = 2.0
LANES = 128
QUAD = 4
F32 = jnp.float32
BF16 = jnp.bfloat16
AXES = ("img", "proto")

VMEM = pl.BlockSpec(memory_space=pltpu.VMEM)
HBM = pl.BlockSpec(memory_space=pltpu.HBM)


def call(body, outs, *args, flops=0, moved=0, exps=0, limit=24, specs=None, out_specs=None, scratch=()):
    return pl.pallas_call(
        body,
        out_shape=outs,
        in_specs=specs or [VMEM] * len(args),
        out_specs=out_specs or tuple(VMEM for _ in outs),
        scratch_shapes=scratch,
        compiler_params=pltpu.CompilerParams(vmem_limit_bytes=limit * 1024 * 1024),
        cost_estimate=pl.CostEstimate(flops=flops, bytes_accessed=moved, transcendentals=exps),
    )(*args)


def near(x):
    return pltpu.with_memory_space_constraint(x, pltpu.VMEM)


def far(x):
    return pltpu.with_memory_space_constraint(x, pltpu.HBM)


def dot(a, b, dims, precision=None):
    return lax.dot_general(a, b, (dims, ((), ())), precision=precision, preferred_element_type=F32)


def iota(shape, dim):
    return lax.broadcasted_iota(jnp.int32, shape, dim)


def add_all(parts):
    return functools.reduce(jnp.add, parts)


def widen(row):
    spare = -row.shape[1] % LANES
    return jnp.concatenate([row, jnp.zeros((1, spare), F32)], axis=1) if spare else row


def tiles_of(row):
    row = widen(row)
    return [row[:, i : i + LANES] for i in range(0, row.shape[1], LANES)]


def to_row(part):
    rows = part.shape[0]
    spare = -rows % LANES
    if spare:
        part = jnp.concatenate([part, jnp.zeros((spare, LANES), F32)], axis=0)
    return jnp.sum(part.T, axis=0, keepdims=True)[:, :rows]


def split(vector):
    high = vector.astype(BF16).astype(F32)
    return [high, vector - high]


def lay_out(vectors, lines, wide):
    tiles = tiles_of(jnp.concatenate(vectors, axis=1))
    tiles += [jnp.zeros((1, LANES), F32)] * (lines * wide // LANES - len(tiles))
    groups = [jnp.concatenate(tiles[g : g + lines], axis=0) for g in range(0, len(tiles), lines)]
    return jnp.concatenate(groups, axis=1)


def read_out(sums, rows, count):
    lines = sums.shape[0]
    turned = [sums[:, g : g + LANES].T for g in range(0, sums.shape[1], LANES)]

    def column(at, stop):
        parts = []
        while at < stop:
            line, lane = divmod(at, LANES)
            until = min(LANES, lane + stop - at)
            parts.append(turned[line // lines][lane:until, line % lines : line % lines + 1])
            at += until - lane
        return jnp.concatenate(parts, axis=0)

    return [jnp.broadcast_to(column(v * rows, (v + 1) * rows), (rows, LANES)) for v in range(count)]


def fold(x):
    return add_all([x[:, i : i + LANES] for i in range(0, x.shape[1], LANES)])


def spread(col, width):
    return jnp.concatenate([col] * (width // LANES), axis=1)


def chunks(columns, step=512):
    step = min(step, columns)
    return [slice(at, at + step) for at in range(0, columns, step)]


def over_chunks(columns, body, start):
    for at in chunks(columns):
        start = body(at, start)
    return start


def start_load(source, target, sems, first=0):
    copies = []
    for i, at in enumerate(chunks(target.shape[1])):
        place = source.at[:, first + at.start : first + at.stop]
        copies.append(pltpu.make_async_copy(place, target.at[:, at], sems.at[i]))
    for copy in copies:
        copy.start()
    return copies


def inverse_norms(w):
    w = w.astype(F32)
    return 1.0 / jnp.sqrt(jnp.sum(w * w, axis=0, keepdims=True) + NORM_EPS)


def odd_half():
    return lax.rem(lax.axis_index("proto"), 2)


def own_slots(mask_ref, feats_ref, own):
    patches = mask_ref.shape[1]
    slot = iota((own, patches), 0) + lax.axis_index("proto") * own
    mask = jnp.broadcast_to(mask_ref[...].astype(F32), (own, patches))
    upto = (iota((patches, patches), 0) <= iota((patches, patches), 1)).astype(BF16)
    rank = dot(mask.astype(BF16), upto, ((1,), (0,)))
    pick = jnp.where((rank == slot.astype(F32) + 1.0) & (mask > 0.5), 1.0, 0.0).astype(BF16)
    valid = slot[:, :1].astype(F32) < rank[:, patches - 1 :]
    rows = dot(pick, feats_ref[0], ((1,), (0,)))
    norm = jnp.sqrt(jnp.sum(rows * rows, axis=1, keepdims=True) + NORM_EPS)
    return (rows / norm).astype(BF16).astype(F32), norm, valid


def teacher_kernel(mask_hbm, stu_hbm, tea_hbm, w_hbm, sent_out, mask_out, stu_out, early_w, tea_ref, sems, w_sems):
    pairs = ((mask_hbm, mask_out), (tea_hbm, tea_ref), (stu_hbm, stu_out))
    copies = [pltpu.make_async_copy(*pair, sems.at[i]) for i, pair in enumerate(pairs)]
    for copy in copies:
        copy.start()
    loads = start_load(w_hbm, early_w, w_sems)
    for copy in copies[:2]:
        copy.wait()
    unit, _, valid = own_slots(mask_out, tea_ref, sent_out.shape[1])
    sent_out[...] = jnp.broadcast_to(jnp.where(valid, unit, EMPTY).astype(BF16)[None], sent_out.shape)
    for copy in copies[2:] + loads:
        copy.wait()


def norms_kernel(mine, mask_ref, stu_ref, early_w, w_hbm, late_w, inv_out, unit_out, norm_out, hot_out, sems):
    early = early_w.shape[1]
    copies = start_load(w_hbm, late_w, sems, early)
    packing([slot_flags(mine[:, :LANES])] * 2, hot_out)
    unit, norm, _ = own_slots(mask_ref, stu_ref, unit_out.shape[0])
    unit_out[...] = unit
    norm_out[...] = jnp.broadcast_to(norm, norm_out.shape)
    for at in chunks(early):
        inv_out[:, at] = inverse_norms(early_w[:, at])
    for copy, at in zip(copies, chunks(late_w.shape[1])):
        copy.wait()
        inv_out[:, early + at.start : early + at.stop] = inverse_norms(late_w[:, at])


def in_order(mine, other, h):
    return jnp.where(odd_half() == h, mine, other)


def slot_flags(data):
    return jnp.where(data[:, :LANES].astype(F32) < 1.5, 1.0, 0.0).astype(BF16)


def packing(flags, hot_out):
    rows = hot_out.shape[0]
    half = flags[0].shape[0]
    step = min(256, half)
    before = jnp.zeros((1, 1), F32)
    upto = (iota((step, step), 0) <= iota((step, step), 1)).astype(BF16)
    same = (iota((step, step), 0) == iota((step, step), 1)).astype(BF16)
    row = iota((rows, step), 0).astype(F32) + 1.0
    for h in range(2):
        for c in range(0, half, step):
            part = flags[h][c : c + step]
            place = before + dot(part, upto, ((0,), (0,)))[:1]
            held = dot(part, same, ((0,), (0,)))[:1]
            hot = jnp.where((row == place) & (held > 0.5), 1.0, 0.0).astype(BF16)
            hot_out[:, h * half + c : h * half + c + step] = hot
            before = place[:, step - 1 :]


def blocks(half):
    step = min(256, half)
    return [(at, at + step) for at in range(0, half, step)]


def pack_rows(hot, read_mine, read_other, half):
    parts = []
    for start, stop in blocks(half):
        mine, other = read_mine(start, stop), read_other(start, stop)
        for h in range(2):
            parts.append(dot(hot[:, h * half + start : h * half + stop], in_order(mine, other, h), ((1,), (0,))))
    return add_all(parts).astype(BF16)


def quads(each, feat):
    return [(row, lane) for lane in range(0, feat, LANES) for row in range(0, each, QUAD)]


def first_kernel(mine, other, early_w, late_w, inv, unit, hot, kernel_out, sent_out):
    rows = kernel_out.shape[0]
    peers, _, groups, _, _ = sent_out.shape
    feat = late_w.shape[0]
    x = pack_rows(hot, lambda a, b: mine[a:b], lambda a, b: other[a:b], mine.shape[0])
    each = unit.shape[0] // 2
    for h in range(2):
        for g, (row, lane) in enumerate(quads(each, feat)):
            part = unit[h * each + row : h * each + row + QUAD, lane : lane + LANES]
            sent_out[:, h, g] = jnp.broadcast_to(part[None], (peers, QUAD, LANES)).astype(BF16)

    acc = jnp.zeros((rows, LANES), F32)
    for w, first in ((early_w, 0), (late_w, early_w.shape[1])):
        for part in chunks(w.shape[1]):
            at = slice(first + part.start, first + part.stop)
            z = dot(x, w[:, part], ((1,), (0,)))
            k = jnp.exp(z * (inv[:, at] * (1.0 / TEACHER_TEMP)))
            kernel_out[:, at] = k
            c = 1.0 / jnp.sum(k, axis=0, keepdims=True)
            acc = acc + fold(k * c)
    held = len(quads(each, feat))
    tiles = lay_out(split(widen(to_row(acc))), QUAD, (groups - held) * LANES)
    for g in range(groups - held):
        tile = tiles[:, g * LANES : (g + 1) * LANES]
        for h in range(2):
            sent_out[:, h, held + g] = jnp.broadcast_to(tile[None], (peers, QUAD, LANES)).astype(BF16)


def row_weights(mine, other, hot, own_out, weight_out, protos):
    devices = lax.axis_size(AXES)
    half = mine.shape[0]
    each = half // devices
    per_image = each * protos
    step = min(256, half)
    count, images = [], []
    block = iota((step, step), 0) // per_image
    same = (block == iota((step, step), 1) // per_image).astype(BF16)
    for c in range(0, half, step):
        flags = [slot_flags(ref[c : c + step, :LANES]).astype(F32) for ref in (mine, other)]
        held = dot(same, (flags[0] + flags[1]).astype(BF16), ((1,), (0,)))
        for h in range(2):
            count.append(dot(hot[:, h * half + c : h * half + c + step], held.astype(BF16), ((1,), (0,))))
        first = (iota(held.shape, 0) % per_image == 0) & (held > 0.5)
        images.append(jnp.sum(first.astype(F32), axis=0, keepdims=True))
    weight_out[...] = 1.0 / (jnp.maximum(add_all(count), 1.0) * add_all(images))

    own = own_out.shape[0]
    me = lax.axis_index("img") * protos + lax.axis_index("proto")
    q = iota((own, 2 * half), 0)
    spot = q // each * half + me * each + q % each
    mark = (iota((own, 2 * half), 1) == spot).astype(BF16)
    own_out[...] = dot(mark, hot[...], ((1,), (1,)))


def sweep_kernel(got, kernel, sent_out, *, held):
    rows, columns = kernel.shape
    sums = [jnp.sum(got[:, g].astype(F32), axis=0) for g in range(held, got.shape[1])]
    width = -(-rows // LANES) * LANES
    high, low = read_out(jnp.concatenate(sums, axis=1), width, 2)
    total = (high + low)[:rows]
    wide = spread(1.0 / total, chunks(columns)[0].stop)

    def body(at, acc):
        k = kernel[:, at]
        c = 1.0 / jnp.sum(k * wide, axis=0, keepdims=True)
        return acc + fold(k * c)

    acc = over_chunks(columns, body, jnp.zeros((rows, LANES), F32))
    tiles = jnp.concatenate(tiles_of(to_row(acc)), axis=0)
    sent_out[...] = jnp.broadcast_to(tiles[None], sent_out.shape).astype(BF16)


def student_kernel(
    got,
    kernel,
    mine,
    other,
    hot,
    stu_w,
    inv_out,
    logits_out,
    scaled_out,
    xt_out,
    vectors_out,
    keep_out,
    give_out,
    stack,
):
    rows, columns = logits_out.shape
    feat = stu_w.shape[0]
    half = hot.shape[1] // 2
    each = half // lax.axis_size(AXES)

    def reader(ref):
        def read(start, stop):
            peers = slice(start // each, stop // each)
            parts = [ref[peers, g].astype(F32) for g in range(len(quads(each, feat)))]
            deep = each // QUAD
            lanes = [jnp.concatenate(parts[g : g + deep], axis=1) for g in range(0, len(parts), deep)]
            return jnp.concatenate([part.reshape(stop - start, LANES) for part in lanes], axis=1).astype(BF16)

        return read

    x = pack_rows(hot, reader(mine), reader(other), half)
    xt = x.astype(F32).T
    xt_out[...] = xt.astype(BF16)
    (total,) = read_out(jnp.sum(got[...].astype(F32), axis=0), rows, 1)
    wide = spread(1.0 / total, chunks(columns)[0].stop)

    def student(at, acc):
        w = stu_w[:, at]
        n = inv_out[:, at]
        l = dot(x, w, ((1,), (0,))) * (n * (1.0 / STUDENT_TEMP))
        logits_out[:, at] = l
        p = jnp.exp(l)
        stack[:rows, at] = (p * n).astype(BF16)
        return acc + fold(p)

    def sweep(at, acc):
        k = kernel[:, at]
        kc = k * (1.0 / jnp.sum(k * wide, axis=0, keepdims=True))
        scaled_out[:, at] = kc
        n = inverse_norms(stu_w[:, at])
        inv_out[:, at] = n
        stack[rows:, at] = (kc * n).astype(BF16)
        return acc + fold(kc)

    zero = jnp.zeros((rows, LANES), F32)
    total = over_chunks(columns, sweep, zero)
    part = over_chunks(columns, student, zero)
    sums = dot(stack[...], stu_w[...], ((1,), (1,)))
    for part_of, lanes in ((sums[:rows], slice(0, feat)), (sums[rows:], slice(feat, 2 * feat))):
        keep_out[:, lanes] = part_of
        give_out[:, lanes] = part_of.astype(BF16)
    cross = to_row(fold(sums[rows:] * x.astype(F32))) * (1.0 / STUDENT_TEMP)
    vectors_out[...] = lay_out([to_row(part), to_row(total), cross], *vectors_out.shape)


def prepare_kernel(
    scaled, logits, inv, mine, other, hot, pull_out, push_out, own_out, weight_out, spots_out, *, scale, protos
):
    rows, columns = scaled.shape
    row_weights(mine, other, hot, own_out, weight_out, protos)
    half = spots_out.shape[0]
    for start, stop in blocks(half):
        own = jnp.where(odd_half() == 1, hot[:, half + start : half + stop], hot[:, start:stop])
        spots_out[start:stop] = own.astype(F32).T.astype(BF16)
    factor = spread(weight_out[...] * (rows / STUDENT_TEMP), chunks(columns)[0].stop)

    def body(at, _):
        n = inv[:, at] * scale
        pull_out[:, at] = factor * jnp.exp(logits[:, at]) * n
        push_out[:, at] = factor * scaled[:, at] * n
        return 0

    over_chunks(columns, body, 0)


def fill_kernel(keep, give, hot, vectors, sent_out):
    devices, groups, _, _ = sent_out.shape
    half, both = hot.shape[0], keep.shape[1]
    each = half // devices
    pair = (keep[...] + give[...].astype(F32)).astype(BF16)
    places = quads(each, both)
    for start, stop in blocks(half):
        slots = dot(hot[start:stop], pair, ((1,), (0,)))
        peers = slice(start // each, stop // each)
        for g, (row, lane) in enumerate(places):
            part = slots[:, lane : lane + LANES].reshape((stop - start) // each, each, LANES)
            sent_out[peers, g] = part[:, row : row + QUAD].astype(BF16)
    for g in range(len(places), groups):
        at = (g - len(places)) * LANES
        sent_out[:, g] = jnp.broadcast_to(vectors[:, at : at + LANES][None], (devices, QUAD, LANES)).astype(BF16)


def slots_of(got, each, both):
    sums = [jnp.sum(got[:, :, g].astype(F32), axis=0) for g in range(len(quads(each, both)))]
    deep = each // QUAD
    lanes = [
        jnp.concatenate([sums[g + i][h] for h in range(2) for i in range(deep)], axis=0) for g in range(0, len(sums), deep)
    ]
    return jnp.concatenate(lanes, axis=1)


def final_kernel(
    got,
    pull,
    push,
    logits,
    inv,
    stu_w,
    xt,
    weight,
    own,
    unit,
    norm,
    out_hbm,
    rows_hbm,
    loss_hbm,
    out,
    rows_out,
    loss_out,
    sems,
):
    rows, columns = pull.shape
    feat = xt.shape[0]
    each = unit.shape[0] // 2
    held = len(quads(each, 2 * feat))
    sums = [jnp.sum(got[:, :, g].astype(F32), axis=(0, 1)) for g in range(held, got.shape[2])]
    partition, total, cross = read_out(jnp.concatenate(sums, axis=1), rows, 3)
    parts = chunks(columns, 256)
    raise_by, lower_by = 1.0 / partition, 1.0 / total
    grow, shrink = spread(raise_by, parts[0].stop), spread(lower_by, parts[0].stop)
    copies = []

    def send(source, target):
        copies.append(pltpu.make_async_copy(source, target, sems.at[len(copies)]))
        copies[-1].start()

    def gradient(at):
        g = grow * pull[:, at] - shrink * push[:, at]
        along = jnp.sum(g * logits[:, at], axis=0, keepdims=True) * (inv[:, at] * STUDENT_TEMP)
        return g.astype(BF16), along

    ready = gradient(parts[0])
    for at, following in zip(parts, parts[1:] + [None]):
        g, along = ready
        direct = dot(xt[...], g, ((1,), (0,)))
        if following is not None:
            ready = gradient(following)
        out[:, at] = direct - stu_w[:, at].astype(F32) * along
        send(out.at[:, at], out_hbm.at[:, at])
    share = weight[...]
    loss = jnp.sum(share * (jnp.log(partition) - cross * lower_by), axis=0, keepdims=True)
    loss_out[...] = loss[:, :1]
    send(loss_out, loss_hbm)
    factors = jnp.concatenate([raise_by, lower_by], axis=1) * spread(share * (rows / STUDENT_TEMP), 2 * LANES)
    scale = dot(own[...], factors, ((1,), (0,)), lax.Precision.HIGHEST)
    sums = slots_of(got, each, 2 * feat)
    full = sums[:, :feat] * scale[:, :1] - sums[:, feat:] * scale[:, LANES : LANES + 1]
    u = unit[...]
    rows_out[...] = (full - u * jnp.sum(u * full, axis=1, keepdims=True)) / norm[:, :1]
    send(rows_out, rows_hbm)
    for copy in copies:
        copy.wait()


def shards(student_feats, teacher_feats, student_weight, teacher_weight, patch_masks):
    devices = lax.axis_size(AXES)
    protos = lax.axis_size("proto")
    images, patches, feat = student_feats.shape
    assert images == 1 and protos % 2 == 0
    columns = student_weight.shape[1]
    own = patches // 2 // protos
    assert patches // 8 % own == 0
    each = own // 2
    half = each * devices
    rows = 2 * half * 5 // 16
    tiles = -(-rows // LANES)
    spare = lambda parts: -(-parts * rows // (QUAD * LANES))
    held = len(quads(each, feat))
    big = rows * columns
    exchange = functools.partial(lax.all_to_all, axis_name=AXES, split_axis=0, concat_axis=0)
    swap = functools.partial(lax.ppermute, axis_name="proto", perm=[(p, p ^ 1) for p in range(protos)])
    matrix = pltpu.VMEM((rows, columns), F32)
    column = pltpu.VMEM((rows, LANES), F32)
    line = pltpu.VMEM((1, columns), F32)

    flags = pltpu.VMEM(patch_masks.shape, patch_masks.dtype)
    feats = pltpu.VMEM(student_feats.shape, BF16)
    early = columns * 3 // 8 // LANES * LANES
    early_w, late_w = pltpu.VMEM((feat, early), BF16), pltpu.VMEM((feat, columns - early), BF16)
    sent, flags, feats, early_w = call(
        teacher_kernel,
        (pltpu.VMEM((devices // 2, own, feat), BF16), flags, feats, early_w),
        far(patch_masks),
        far(student_feats),
        far(teacher_feats),
        far(teacher_weight),
        specs=[HBM] * 4,
        scratch=[feats, pltpu.SemaphoreType.DMA((3,)), pltpu.SemaphoreType.DMA((len(chunks(early)),))],
    )
    mine = exchange(sent.reshape(devices, each, feat)).reshape(half, feat)
    mine, teacher_weight = lax.optimization_barrier((mine, teacher_weight))
    other = near(swap(mine))
    mine = near(mine)
    late_w, tea_inv, unit, norm, hot = call(
        norms_kernel,
        (
            late_w,
            line,
            pltpu.VMEM((own, feat), F32),
            pltpu.VMEM((own, LANES), F32),
            pltpu.VMEM((rows, 2 * half), BF16),
        ),
        mine,
        flags,
        feats,
        early_w,
        far(teacher_weight),
        flops=2 * feat * columns,
        moved=4 * feat * columns,
        specs=[VMEM, VMEM, VMEM, VMEM, HBM],
        scratch=[pltpu.SemaphoreType.DMA((len(chunks(columns - early)),))],
    )
    kernel, sent = call(
        first_kernel,
        (
            matrix,
            pltpu.VMEM((devices // 2, 2, held + -(-2 * tiles // QUAD), QUAD, LANES), BF16),
        ),
        mine,
        other,
        early_w,
        late_w,
        tea_inv,
        unit,
        hot,
        flops=2 * big * feat,
        moved=4 * big,
        exps=big,
    )
    stu_mine = exchange(sent.reshape(devices, *sent.shape[2:]))
    stu_other = near(swap(stu_mine))
    stu_mine = near(stu_mine)
    (sent,) = call(
        functools.partial(sweep_kernel, held=held),
        (pltpu.VMEM((devices, tiles, LANES), BF16),),
        stu_mine,
        kernel,
        flops=4 * big,
        moved=4 * big,
    )
    got = near(exchange(sent))
    stu_inv, logits, scaled, xt, sums, keep, give = call(
        student_kernel,
        (
            line,
            matrix,
            matrix,
            pltpu.VMEM((feat, rows), BF16),
            pltpu.VMEM((QUAD, spare(3) * LANES), F32),
            pltpu.VMEM((rows, 2 * feat), F32),
            pltpu.VMEM((rows, 2 * feat), BF16),
        ),
        got,
        kernel,
        stu_mine,
        stu_other,
        hot,
        student_weight,
        flops=6 * big * feat,
        moved=12 * big,
        exps=big,
        scratch=[pltpu.VMEM((2 * rows, columns), BF16)],
        limit=22 + half // 112,
    )
    give = near(swap(give))
    pull, push, own_hot, weight, spots = call(
        functools.partial(prepare_kernel, scale=columns * devices * GRAD_SCALE, protos=protos),
        (matrix, matrix, pltpu.VMEM((own, rows), F32), column, pltpu.VMEM((half, rows), BF16)),
        scaled,
        logits,
        stu_inv,
        mine,
        other,
        hot,
        flops=4 * big,
        moved=16 * big,
        exps=big,
    )
    keep, pull, push, own_hot, weight = lax.optimization_barrier((keep, pull, push, own_hot, weight))
    payload = pltpu.VMEM((devices, 2 * held + spare(3), QUAD, LANES), BF16)
    (sent,) = call(fill_kernel, (payload,), keep, give, spots, sums)
    got = exchange(sent)
    got = near(got.reshape(devices // 2, 2, *got.shape[1:]))
    grad_weight, grad_rows, loss = call(
        final_kernel,
        (
            jax.ShapeDtypeStruct((feat, columns), F32),
            jax.ShapeDtypeStruct((own, feat), F32),
            jax.ShapeDtypeStruct((1, 1), F32),
        ),
        got,
        pull,
        push,
        logits,
        stu_inv,
        student_weight,
        xt,
        weight,
        own_hot,
        unit,
        norm,
        flops=2 * big * feat,
        moved=8 * feat * columns,
        out_specs=(HBM, HBM, HBM),
        scratch=[
            pltpu.VMEM((feat, columns), F32),
            pltpu.VMEM((own, feat), F32),
            pltpu.VMEM((1, 1), F32),
            pltpu.SemaphoreType.DMA((len(chunks(columns, 256)) + 2,)),
        ],
    )
    return loss.reshape(()), grad_weight, grad_rows


def solution(mesh):
    placed = (
        P("img", None, None),
        P("img", None, None),
        P(None, AXES),
        P(None, AXES),
        P("img", None),
    )
    return jax.shard_map(
        shards,
        mesh=mesh,
        in_specs=placed,
        out_specs=(P(), P(None, AXES), P(AXES, None)),
        check_vma=False,
    )
```

```python
import functools

import jax
import jax.numpy as jnp
from jax import lax
from jax.experimental import pallas as pl
from jax.experimental.pallas import tpu as pltpu
from jax.sharding import PartitionSpec as P

ITERS = 3
TEACHER_TEMP = 0.07
STUDENT_TEMP = 0.1
NORM_EPS = 1e-06
GRAD_SCALE = 1.0 / 128.0
EMPTY = 2.0
LANES = 128
QUAD = 4
F32 = jnp.float32
BF16 = jnp.bfloat16
AXES = ("img", "proto")

VMEM = pl.BlockSpec(memory_space=pltpu.VMEM)
HBM = pl.BlockSpec(memory_space=pltpu.HBM)


def call(body, outs, *args, flops=0, moved=0, exps=0, limit=24, specs=None, out_specs=None, scratch=()):
    return pl.pallas_call(
        body,
        out_shape=outs,
        in_specs=specs or [VMEM] * len(args),
        out_specs=out_specs or tuple(VMEM for _ in outs),
        scratch_shapes=scratch,
        compiler_params=pltpu.CompilerParams(vmem_limit_bytes=limit * 1024 * 1024),
        cost_estimate=pl.CostEstimate(flops=flops, bytes_accessed=moved, transcendentals=exps),
    )(*args)


def near(x):
    return pltpu.with_memory_space_constraint(x, pltpu.VMEM)


def far(x):
    return pltpu.with_memory_space_constraint(x, pltpu.HBM)


def dot(a, b, dims, precision=None):
    return lax.dot_general(a, b, (dims, ((), ())), precision=precision, preferred_element_type=F32)


def iota(shape, dim):
    return lax.broadcasted_iota(jnp.int32, shape, dim)


def add_all(parts):
    return functools.reduce(jnp.add, parts)


def widen(row):
    spare = -row.shape[1] % LANES
    return jnp.concatenate([row, jnp.zeros((1, spare), F32)], axis=1) if spare else row


def tiles_of(row):
    row = widen(row)
    return [row[:, i : i + LANES] for i in range(0, row.shape[1], LANES)]


def to_row(part):
    rows = part.shape[0]
    spare = -rows % LANES
    if spare:
        part = jnp.concatenate([part, jnp.zeros((spare, LANES), F32)], axis=0)
    return jnp.sum(part.T, axis=0, keepdims=True)[:, :rows]


def split(vector):
    high = vector.astype(BF16).astype(F32)
    return [high, vector - high]


def lay_out(vectors, lines, wide):
    tiles = tiles_of(jnp.concatenate(vectors, axis=1))
    tiles += [jnp.zeros((1, LANES), F32)] * (lines * wide // LANES - len(tiles))
    groups = [jnp.concatenate(tiles[g : g + lines], axis=0) for g in range(0, len(tiles), lines)]
    return jnp.concatenate(groups, axis=1)


def read_out(sums, rows, count):
    lines = sums.shape[0]
    turned = [sums[:, g : g + LANES].T for g in range(0, sums.shape[1], LANES)]

    def column(at, stop):
        parts = []
        while at < stop:
            line, lane = divmod(at, LANES)
            until = min(LANES, lane + stop - at)
            parts.append(turned[line // lines][lane:until, line % lines : line % lines + 1])
            at += until - lane
        return jnp.concatenate(parts, axis=0)

    return [jnp.broadcast_to(column(v * rows, (v + 1) * rows), (rows, LANES)) for v in range(count)]


def fold(x):
    return add_all([x[:, i : i + LANES] for i in range(0, x.shape[1], LANES)])


def spread(col, width):
    return jnp.concatenate([col] * (width // LANES), axis=1)


def chunks(columns, step=512):
    step = min(step, columns)
    return [slice(at, at + step) for at in range(0, columns, step)]


def over_chunks(columns, body, start):
    for at in chunks(columns):
        start = body(at, start)
    return start


def start_load(source, target, sems, first=0):
    copies = []
    for i, at in enumerate(chunks(target.shape[1])):
        place = source.at[:, first + at.start : first + at.stop]
        copies.append(pltpu.make_async_copy(place, target.at[:, at], sems.at[i]))
    for copy in copies:
        copy.start()
    return copies


def inverse_norms(w):
    w = w.astype(F32)
    return 1.0 / jnp.sqrt(jnp.sum(w * w, axis=0, keepdims=True) + NORM_EPS)


def odd_half():
    return lax.rem(lax.axis_index("proto"), 2)


def own_slots(mask_ref, feats_ref, own):
    patches = mask_ref.shape[1]
    slot = iota((own, patches), 0) + lax.axis_index("proto") * own
    mask = jnp.broadcast_to(mask_ref[...].astype(F32), (own, patches))
    upto = (iota((patches, patches), 0) <= iota((patches, patches), 1)).astype(BF16)
    rank = dot(mask.astype(BF16), upto, ((1,), (0,)))
    pick = jnp.where((rank == slot.astype(F32) + 1.0) & (mask > 0.5), 1.0, 0.0).astype(BF16)
    valid = slot[:, :1].astype(F32) < rank[:, patches - 1 :]
    rows = dot(pick, feats_ref[0], ((1,), (0,)))
    norm = jnp.sqrt(jnp.sum(rows * rows, axis=1, keepdims=True) + NORM_EPS)
    return (rows / norm).astype(BF16).astype(F32), norm, valid


def teacher_kernel(mask_hbm, stu_hbm, tea_hbm, w_hbm, sent_out, mask_out, stu_out, early_w, tea_ref, sems, w_sems):
    pairs = ((mask_hbm, mask_out), (tea_hbm, tea_ref), (stu_hbm, stu_out))
    copies = [pltpu.make_async_copy(*pair, sems.at[i]) for i, pair in enumerate(pairs)]
    for copy in copies:
        copy.start()
    loads = start_load(w_hbm, early_w, w_sems)
    for copy in copies[:2]:
        copy.wait()
    unit, _, valid = own_slots(mask_out, tea_ref, sent_out.shape[1])
    sent_out[...] = jnp.broadcast_to(jnp.where(valid, unit, EMPTY).astype(BF16)[None], sent_out.shape)
    for copy in copies[2:] + loads:
        copy.wait()


def norms_kernel(mine, mask_ref, stu_ref, early_w, w_hbm, late_w, inv_out, unit_out, norm_out, hot_out, sems):
    early = early_w.shape[1]
    copies = start_load(w_hbm, late_w, sems, early)
    packing([slot_flags(mine[:, :LANES])] * 2, hot_out)
    unit, norm, _ = own_slots(mask_ref, stu_ref, unit_out.shape[0])
    unit_out[...] = unit
    norm_out[...] = jnp.broadcast_to(norm, norm_out.shape)
    for at in chunks(early):
        inv_out[:, at] = inverse_norms(early_w[:, at])
    for copy, at in zip(copies, chunks(late_w.shape[1])):
        copy.wait()
        inv_out[:, early + at.start : early + at.stop] = inverse_norms(late_w[:, at])


def in_order(mine, other, h):
    return jnp.where(odd_half() == h, mine, other)


def slot_flags(data):
    return jnp.where(data[:, :LANES].astype(F32) < 1.5, 1.0, 0.0).astype(BF16)


def packing(flags, hot_out):
    rows = hot_out.shape[0]
    half = flags[0].shape[0]
    step = min(256, half)
    before = jnp.zeros((1, 1), F32)
    upto = (iota((step, step), 0) <= iota((step, step), 1)).astype(BF16)
    same = (iota((step, step), 0) == iota((step, step), 1)).astype(BF16)
    row = iota((rows, step), 0).astype(F32) + 1.0
    for h in range(2):
        for c in range(0, half, step):
            part = flags[h][c : c + step]
            place = before + dot(part, upto, ((0,), (0,)))[:1]
            held = dot(part, same, ((0,), (0,)))[:1]
            hot = jnp.where((row == place) & (held > 0.5), 1.0, 0.0).astype(BF16)
            hot_out[:, h * half + c : h * half + c + step] = hot
            before = place[:, step - 1 :]


def blocks(half):
    step = min(256, half)
    return [(at, at + step) for at in range(0, half, step)]


def pack_rows(hot, read_mine, read_other, half):
    parts = []
    for start, stop in blocks(half):
        mine, other = read_mine(start, stop), read_other(start, stop)
        for h in range(2):
            parts.append(dot(hot[:, h * half + start : h * half + stop], in_order(mine, other, h), ((1,), (0,))))
    return add_all(parts).astype(BF16)


def quads(each, feat):
    return [(row, lane) for lane in range(0, feat, LANES) for row in range(0, each, QUAD)]


def first_kernel(mine, other, early_w, late_w, inv, unit, hot, kernel_out, sent_out):
    rows = kernel_out.shape[0]
    peers, _, groups, _, _ = sent_out.shape
    feat = late_w.shape[0]
    x = pack_rows(hot, lambda a, b: mine[a:b], lambda a, b: other[a:b], mine.shape[0])
    each = unit.shape[0] // 2
    for h in range(2):
        for g, (row, lane) in enumerate(quads(each, feat)):
            part = unit[h * each + row : h * each + row + QUAD, lane : lane + LANES]
            sent_out[:, h, g] = jnp.broadcast_to(part[None], (peers, QUAD, LANES)).astype(BF16)

    acc = jnp.zeros((rows, LANES), F32)
    for w, first in ((early_w, 0), (late_w, early_w.shape[1])):
        for part in chunks(w.shape[1]):
            at = slice(first + part.start, first + part.stop)
            z = dot(x, w[:, part], ((1,), (0,)))
            k = jnp.exp(z * (inv[:, at] * (1.0 / TEACHER_TEMP)))
            kernel_out[:, at] = k
            c = 1.0 / jnp.sum(k, axis=0, keepdims=True)
            acc = acc + fold(k * c)
    held = len(quads(each, feat))
    tiles = lay_out(split(widen(to_row(acc))), QUAD, (groups - held) * LANES)
    for g in range(groups - held):
        tile = tiles[:, g * LANES : (g + 1) * LANES]
        for h in range(2):
            sent_out[:, h, held + g] = jnp.broadcast_to(tile[None], (peers, QUAD, LANES)).astype(BF16)


def row_weights(mine, other, hot, own_out, weight_out, protos):
    devices = lax.axis_size(AXES)
    half = mine.shape[0]
    each = half // devices
    per_image = each * protos
    step = min(256, half)
    count, images = [], []
    block = iota((step, step), 0) // per_image
    same = (block == iota((step, step), 1) // per_image).astype(BF16)
    for c in range(0, half, step):
        flags = [slot_flags(ref[c : c + step, :LANES]).astype(F32) for ref in (mine, other)]
        held = dot(same, (flags[0] + flags[1]).astype(BF16), ((1,), (0,)))
        for h in range(2):
            count.append(dot(hot[:, h * half + c : h * half + c + step], held.astype(BF16), ((1,), (0,))))
        first = (iota(held.shape, 0) % per_image == 0) & (held > 0.5)
        images.append(jnp.sum(first.astype(F32), axis=0, keepdims=True))
    weight_out[...] = 1.0 / (jnp.maximum(add_all(count), 1.0) * add_all(images))

    own = own_out.shape[0]
    me = lax.axis_index("img") * protos + lax.axis_index("proto")
    q = iota((own, 2 * half), 0)
    spot = q // each * half + me * each + q % each
    mark = (iota((own, 2 * half), 1) == spot).astype(BF16)
    own_out[...] = dot(mark, hot[...], ((1,), (1,)))


def sweep_kernel(got, kernel, sent_out, *, held):
    rows, columns = kernel.shape
    sums = [jnp.sum(got[:, g].astype(F32), axis=0) for g in range(held, got.shape[1])]
    width = -(-rows // LANES) * LANES
    high, low = read_out(jnp.concatenate(sums, axis=1), width, 2)
    total = (high + low)[:rows]
    wide = spread(1.0 / total, chunks(columns)[0].stop)

    def body(at, acc):
        k = kernel[:, at]
        c = 1.0 / jnp.sum(k * wide, axis=0, keepdims=True)
        return acc + fold(k * c)

    acc = over_chunks(columns, body, jnp.zeros((rows, LANES), F32))
    tiles = jnp.concatenate(tiles_of(to_row(acc)), axis=0)
    sent_out[...] = jnp.broadcast_to(tiles[None], sent_out.shape)


def student_kernel(
    got,
    kernel,
    mine,
    other,
    hot,
    stu_w,
    inv_out,
    logits_out,
    scaled_out,
    xt_out,
    vectors_out,
    keep_out,
    give_out,
    stack,
):
    rows, columns = logits_out.shape
    feat = stu_w.shape[0]
    half = hot.shape[1] // 2
    each = half // lax.axis_size(AXES)

    def reader(ref):
        def read(start, stop):
            peers = slice(start // each, stop // each)
            parts = [ref[peers, g].astype(F32) for g in range(len(quads(each, feat)))]
            deep = each // QUAD
            lanes = [jnp.concatenate(parts[g : g + deep], axis=1) for g in range(0, len(parts), deep)]
            return jnp.concatenate([part.reshape(stop - start, LANES) for part in lanes], axis=1).astype(BF16)

        return read

    x = pack_rows(hot, reader(mine), reader(other), half)
    xt = x.astype(F32).T
    xt_out[...] = xt.astype(BF16)
    (total,) = read_out(jnp.sum(got[...], axis=0), rows, 1)
    wide = spread(1.0 / total, chunks(columns)[0].stop)

    def student(at, acc):
        w = stu_w[:, at]
        n = inv_out[:, at]
        l = dot(x, w, ((1,), (0,))) * (n * (1.0 / STUDENT_TEMP))
        logits_out[:, at] = l
        p = jnp.exp(l)
        stack[:rows, at] = (p * n).astype(BF16)
        return acc + fold(p)

    def sweep(at, acc):
        k = kernel[:, at]
        kc = k * (1.0 / jnp.sum(k * wide, axis=0, keepdims=True))
        scaled_out[:, at] = kc
        n = inverse_norms(stu_w[:, at])
        inv_out[:, at] = n
        stack[rows:, at] = (kc * n).astype(BF16)
        return acc + fold(kc)

    zero = jnp.zeros((rows, LANES), F32)
    both = lambda at, accs: (sweep(at, accs[0]), student(at, accs[1]))
    total, part = over_chunks(columns, both, (zero, zero))
    sums = dot(stack[...], stu_w[...], ((1,), (1,)))
    for part_of, lanes in ((sums[:rows], slice(0, feat)), (sums[rows:], slice(feat, 2 * feat))):
        keep_out[:, lanes] = part_of
        give_out[:, lanes] = part_of.astype(BF16)
    cross = to_row(fold(sums[rows:] * x.astype(F32))) * (1.0 / STUDENT_TEMP)
    vectors_out[...] = lay_out([to_row(part), to_row(total), cross], *vectors_out.shape)


def prepare_kernel(
    scaled, logits, inv, mine, other, hot, pull_out, push_out, own_out, weight_out, spots_out, *, scale, protos
):
    rows, columns = scaled.shape
    row_weights(mine, other, hot, own_out, weight_out, protos)
    half = spots_out.shape[0]
    for start, stop in blocks(half):
        own = jnp.where(odd_half() == 1, hot[:, half + start : half + stop], hot[:, start:stop])
        spots_out[start:stop] = own.astype(F32).T.astype(BF16)
    factor = spread(weight_out[...] * (rows / STUDENT_TEMP), chunks(columns)[0].stop)

    def body(at, _):
        n = inv[:, at] * scale
        pull_out[:, at] = factor * jnp.exp(logits[:, at]) * n
        push_out[:, at] = factor * scaled[:, at] * n
        return 0

    over_chunks(columns, body, 0)


def fill_kernel(keep, give, hot, vectors, sent_out):
    devices, groups, _, _ = sent_out.shape
    half, both = hot.shape[0], keep.shape[1]
    each = half // devices
    pair = (keep[...] + give[...].astype(F32)).astype(BF16)
    places = quads(each, both)
    for start, stop in blocks(half):
        slots = dot(hot[start:stop], pair, ((1,), (0,)))
        peers = slice(start // each, stop // each)
        for g, (row, lane) in enumerate(places):
            part = slots[:, lane : lane + LANES].reshape((stop - start) // each, each, LANES)
            sent_out[peers, g] = part[:, row : row + QUAD].astype(BF16)
    for g in range(len(places), groups):
        at = (g - len(places)) * LANES
        sent_out[:, g] = jnp.broadcast_to(vectors[:, at : at + LANES][None], (devices, QUAD, LANES)).astype(BF16)


def slots_of(got, each, both):
    sums = [jnp.sum(got[:, :, g].astype(F32), axis=0) for g in range(len(quads(each, both)))]
    deep = each // QUAD
    lanes = [
        jnp.concatenate([sums[g + i][h] for h in range(2) for i in range(deep)], axis=0) for g in range(0, len(sums), deep)
    ]
    return jnp.concatenate(lanes, axis=1)


def final_kernel(
    got,
    pull,
    push,
    logits,
    inv,
    stu_w,
    xt,
    weight,
    own,
    unit,
    norm,
    out_hbm,
    rows_hbm,
    loss_hbm,
    out,
    rows_out,
    loss_out,
    sems,
):
    rows, columns = pull.shape
    feat = xt.shape[0]
    each = unit.shape[0] // 2
    held = len(quads(each, 2 * feat))
    sums = [jnp.sum(got[:, :, g].astype(F32), axis=(0, 1)) for g in range(held, got.shape[2])]
    partition, total, cross = read_out(jnp.concatenate(sums, axis=1), rows, 3)
    parts = chunks(columns, 256)
    raise_by, lower_by = 1.0 / partition, 1.0 / total
    grow, shrink = spread(raise_by, parts[0].stop), spread(lower_by, parts[0].stop)
    copies = []

    def send(source, target):
        copies.append(pltpu.make_async_copy(source, target, sems.at[len(copies)]))
        copies[-1].start()

    def gradient(at):
        g = grow * pull[:, at] - shrink * push[:, at]
        along = jnp.sum(g * logits[:, at], axis=0, keepdims=True) * (inv[:, at] * STUDENT_TEMP)
        return g.astype(BF16), along

    ready = gradient(parts[0])
    for at, following in zip(parts, parts[1:] + [None]):
        g, along = ready
        direct = dot(xt[...], g, ((1,), (0,)))
        if following is not None:
            ready = gradient(following)
        out[:, at] = direct - stu_w[:, at].astype(F32) * along
        send(out.at[:, at], out_hbm.at[:, at])
    share = weight[...]
    loss = jnp.sum(share * (jnp.log(partition) - cross * lower_by), axis=0, keepdims=True)
    loss_out[...] = loss[:, :1]
    send(loss_out, loss_hbm)
    factors = jnp.concatenate([raise_by, lower_by], axis=1) * spread(share * (rows / STUDENT_TEMP), 2 * LANES)
    scale = dot(own[...], factors, ((1,), (0,)), lax.Precision.HIGHEST)
    sums = slots_of(got, each, 2 * feat)
    full = sums[:, :feat] * scale[:, :1] - sums[:, feat:] * scale[:, LANES : LANES + 1]
    u = unit[...]
    rows_out[...] = (full - u * jnp.sum(u * full, axis=1, keepdims=True)) / norm[:, :1]
    send(rows_out, rows_hbm)
    for copy in copies:
        copy.wait()


def shards(student_feats, teacher_feats, student_weight, teacher_weight, patch_masks):
    devices = lax.axis_size(AXES)
    protos = lax.axis_size("proto")
    images, patches, feat = student_feats.shape
    assert images == 1 and protos % 2 == 0
    columns = student_weight.shape[1]
    own = patches // 2 // protos
    assert patches // 8 % own == 0
    each = own // 2
    half = each * devices
    rows = 2 * half * 5 // 16
    tiles = -(-rows // LANES)
    spare = lambda parts: -(-parts * rows // (QUAD * LANES))
    held = len(quads(each, feat))
    big = rows * columns
    exchange = functools.partial(lax.all_to_all, axis_name=AXES, split_axis=0, concat_axis=0)
    swap = functools.partial(lax.ppermute, axis_name="proto", perm=[(p, p ^ 1) for p in range(protos)])
    matrix = pltpu.VMEM((rows, columns), F32)
    column = pltpu.VMEM((rows, LANES), F32)
    line = pltpu.VMEM((1, columns), F32)

    flags = pltpu.VMEM(patch_masks.shape, patch_masks.dtype)
    feats = pltpu.VMEM(student_feats.shape, BF16)
    early = columns * 3 // 8 // LANES * LANES
    early_w, late_w = pltpu.VMEM((feat, early), BF16), pltpu.VMEM((feat, columns - early), BF16)
    sent, flags, feats, early_w = call(
        teacher_kernel,
        (pltpu.VMEM((devices // 2, own, feat), BF16), flags, feats, early_w),
        far(patch_masks),
        far(student_feats),
        far(teacher_feats),
        far(teacher_weight),
        specs=[HBM] * 4,
        scratch=[feats, pltpu.SemaphoreType.DMA((3,)), pltpu.SemaphoreType.DMA((len(chunks(early)),))],
    )
    mine = exchange(sent.reshape(devices, each, feat)).reshape(half, feat)
    mine, teacher_weight = lax.optimization_barrier((mine, teacher_weight))
    other = near(swap(mine))
    mine = near(mine)
    late_w, tea_inv, unit, norm, hot = call(
        norms_kernel,
        (
            late_w,
            line,
            pltpu.VMEM((own, feat), F32),
            pltpu.VMEM((own, LANES), F32),
            pltpu.VMEM((rows, 2 * half), BF16),
        ),
        mine,
        flags,
        feats,
        early_w,
        far(teacher_weight),
        flops=2 * feat * columns,
        moved=4 * feat * columns,
        specs=[VMEM, VMEM, VMEM, VMEM, HBM],
        scratch=[pltpu.SemaphoreType.DMA((len(chunks(columns - early)),))],
    )
    kernel, sent = call(
        first_kernel,
        (
            matrix,
            pltpu.VMEM((devices // 2, 2, held + -(-2 * tiles // QUAD), QUAD, LANES), BF16),
        ),
        mine,
        other,
        early_w,
        late_w,
        tea_inv,
        unit,
        hot,
        flops=2 * big * feat,
        moved=4 * big,
        exps=big,
    )
    stu_mine = exchange(sent.reshape(devices, *sent.shape[2:]))
    stu_other = near(swap(stu_mine))
    stu_mine = near(stu_mine)
    (sent,) = call(
        functools.partial(sweep_kernel, held=held),
        (pltpu.VMEM((devices, tiles, LANES), F32),),
        stu_mine,
        kernel,
        flops=4 * big,
        moved=4 * big,
    )
    got = near(exchange(sent))
    stu_inv, logits, scaled, xt, sums, keep, give = call(
        student_kernel,
        (
            line,
            matrix,
            matrix,
            pltpu.VMEM((feat, rows), BF16),
            pltpu.VMEM((QUAD, spare(3) * LANES), F32),
            pltpu.VMEM((rows, 2 * feat), F32),
            pltpu.VMEM((rows, 2 * feat), BF16),
        ),
        got,
        kernel,
        stu_mine,
        stu_other,
        hot,
        student_weight,
        flops=6 * big * feat,
        moved=12 * big,
        exps=big,
        scratch=[pltpu.VMEM((2 * rows, columns), BF16)],
        limit=22 + half // 112,
    )
    give = near(swap(give))
    pull, push, own_hot, weight, spots = call(
        functools.partial(prepare_kernel, scale=columns * devices * GRAD_SCALE, protos=protos),
        (matrix, matrix, pltpu.VMEM((own, rows), F32), column, pltpu.VMEM((half, rows), BF16)),
        scaled,
        logits,
        stu_inv,
        mine,
        other,
        hot,
        flops=4 * big,
        moved=16 * big,
        exps=big,
    )
    keep, pull, push, own_hot, weight = lax.optimization_barrier((keep, pull, push, own_hot, weight))
    payload = pltpu.VMEM((devices, 2 * held + spare(3), QUAD, LANES), BF16)
    (sent,) = call(fill_kernel, (payload,), keep, give, spots, sums)
    got = exchange(sent)
    got = near(got.reshape(devices // 2, 2, *got.shape[1:]))
    grad_weight, grad_rows, loss = call(
        final_kernel,
        (
            jax.ShapeDtypeStruct((feat, columns), F32),
            jax.ShapeDtypeStruct((own, feat), F32),
            jax.ShapeDtypeStruct((1, 1), F32),
        ),
        got,
        pull,
        push,
        logits,
        stu_inv,
        student_weight,
        xt,
        weight,
        own_hot,
        unit,
        norm,
        flops=2 * big * feat,
        moved=8 * feat * columns,
        out_specs=(HBM, HBM, HBM),
        scratch=[
            pltpu.VMEM((feat, columns), F32),
            pltpu.VMEM((own, feat), F32),
            pltpu.VMEM((1, 1), F32),
            pltpu.SemaphoreType.DMA((len(chunks(columns, 256)) + 2,)),
        ],
    )
    return loss.reshape(()), grad_weight, grad_rows


def solution(mesh):
    placed = (
        P("img", None, None),
        P("img", None, None),
        P(None, AXES),
        P(None, AXES),
        P("img", None),
    )
    return jax.shard_map(
        shards,
        mesh=mesh,
        in_specs=placed,
        out_specs=(P(), P(None, AXES), P(AXES, None)),
        check_vma=False,
    )
```
